256 devices in a mesh: dp: 4 (over x_lo, core), tile: 64 (over y, x_hi, z).
Axes of the slice: x: 4 (x_hi: 2, x_lo: 2; x = x_hi * 2 + x_lo), y: 4, z: 8, core: 2. Of those that a mesh axis runs over, the one named last changes fastest.
Arguments:
- activations: bfloat16 [4, 512, 8192], P('dp', None, 'tile'), may hold values from -6 to 6
- gradients: bfloat16 [4, 512, 8192], P('dp', None, 'tile'), may hold values from -6 to 6
- basis_in: float32 [8192, 8192], P(None, 'tile'), may hold values from -0.0625 to 0.0625
- basis_out: float32 [8192, 8192], P(None, 'tile'), may hold values from -0.0625 to 0.0625
Outputs:
- eigenvalues: float32 [8192, 8192], P('tile', 'dp')
The draws below stay inside these ranges and needn't reach their ends.
All inputs are finite; a program needn't handle non-finite values.
Results may differ from the reference program's by a relative error of at most 0.0035.
Values may be sent and summed in bfloat16 or wider, within the bound.
No kernel may reach another device: no remote copies, remote signals or barrier semaphores. Data moves between devices by JAX's collectives and lax.ppermute only.
A program may use at most 64 MiB of HBM per device.

```python
import jax
import jax.numpy as jnp
from jax import lax

D = 8192
TOK = 512
SEQS = 4


def shard_levels(stream_key, dims, shards, least, largest):
    factor_of, own = 1.0, jax.random.fold_in(stream_key, 6)
    for position, shards_of in shards:
        draws = jnp.exp(jax.random.uniform(jax.random.fold_in(own, position), (shards_of,), jnp.float32, least / len(shards), largest / len(shards)))
        factor_of = factor_of * jnp.repeat(draws, dims[position] // shards_of).reshape([-1 if axis == position else 1 for axis in range(len(dims))])
    return factor_of


def gaussian(rng, shape, deviation, reach, cuts=(), kind=jnp.bfloat16):
    drawn = deviation * jax.random.normal(rng, shape, jnp.float32)
    if cuts:
        drawn = drawn * shard_levels(rng, shape, cuts, -0.22, 0.18)
    return jnp.clip(drawn, -reach, reach).astype(kind)


def setup_inputs(seed: int = 0) -> dict:
    key_of = jax.random.split(jax.random.key(seed), 5)
    return {
        "activations": gaussian(key_of[0], (SEQS, TOK, D), 1.0, 6.0, ((0, 4), (2, 64))),
        "gradients": gaussian(key_of[1], (SEQS, TOK, D), 1.0, 6.0, ((0, 4), (2, 64))),
        "basis_in": gaussian(key_of[2], (D, D), D ** -0.5, 0.0625, ((1, 64),), jnp.float32),
        "basis_out": gaussian(key_of[3], (D, D), D ** -0.5, 0.0625, ((1, 64),), jnp.float32),
    }


def rotate_rows(rows, basis):
    return jnp.einsum("stf,fk->stk", rows.astype(jnp.float32), basis, precision=lax.Precision.HIGHEST).astype(jnp.bfloat16)


def reference(activations, gradients, basis_in, basis_out):
    rot_acts = rotate_rows(activations, basis_in).astype(jnp.float32)
    rot_grads = rotate_rows(gradients, basis_out).astype(jnp.float32)
    block_rows = min(512, D)
    count = D // block_rows

    def one_block(index):
        first = (index * block_rows).astype(jnp.int32)
        grad_block = lax.dynamic_slice_in_dim(rot_grads, first, block_rows, 2)
        products = jnp.einsum("sti,stj->sij", grad_block, rot_acts)
        return jnp.sum(products * products, axis=0)

    blocks = lax.map(one_block, jnp.arange(count, dtype=jnp.int32))
    scale = jnp.float32(1.0 / (TOK * SEQS))
    return blocks.reshape(D, D) * scale
```

```python
import functools

import jax
import jax.numpy as jnp
from jax import lax
from jax.experimental import pallas as pl
from jax.experimental.pallas import tpu as pltpu
from jax.sharding import Mesh, PartitionSpec as P

AXES = ("xl", "c", "y", "xh", "z")
SIZES = (2, 2, 4, 2, 8)
DP = ("xl", "c")
TILE = ("y", "xh", "z")
TOK = 512
COLS = 128
F32 = jnp.float32
BF16 = jnp.bfloat16
VMEM_LIMIT = 48 * 1024 * 1024
OFFSETS = (0, -1, 1, -2, 2, -3, 3, -4)


def shift(x, axis, by):
    n = lax.axis_size(axis)
    return lax.ppermute(x, axis, [(i, (i + by) % n) for i in range(n)])


def gather_z(x):
    blocks = [x]
    up = down = x
    for step in range(1, 4):
        up = shift(up, "z", 1)
        down = shift(down, "z", -1)
        blocks += [up, down]
    blocks.append(shift(up, "z", 1))
    return blocks


def whole(shape):
    return pl.BlockSpec(shape, lambda *_: (0,) * len(shape))


def rotate_kernel(z_ref, *refs):
    blocks, (own_ref, other_ref, out_ref, lhs, rhs) = refs[:8], refs[8:]

    @pl.when(pl.program_id(0) == 0)
    def _():
        for k, block in enumerate(blocks):
            lhs[:, k * 256 : (k + 1) * 256] = block[...]

    for k, offset in enumerate(OFFSETS):
        at = lax.rem(z_ref[0] + 8 + offset, 8) * COLS
        for half, ref in enumerate((own_ref, other_ref)):
            exact = ref[0, pl.ds(pl.multiple_of(at, COLS), COLS), :]
            high = exact.astype(BF16)
            low = (exact - high.astype(F32)).astype(BF16)
            row = k * 256 + half * COLS
            rhs[row : row + COLS, :COLS] = high
            rhs[row : row + COLS, COLS:] = low
    both = jnp.dot(lhs[...], rhs[...], preferred_element_type=F32)
    out_ref[0] = (both[:, :COLS] + both[:, COLS:]).T


def rotate(z, blocks, own, other):
    slab = pl.BlockSpec((1, 1024, COLS), lambda g: (g, 0, 0))
    return pl.pallas_call(
        rotate_kernel,
        grid=(4,),
        out_shape=jax.ShapeDtypeStruct((4, COLS, TOK), F32),
        in_specs=[pl.BlockSpec(memory_space=pltpu.SMEM)]
        + [whole((TOK, 256))] * 8
        + [slab, slab],
        out_specs=pl.BlockSpec((1, COLS, TOK), lambda g: (g, 0, 0)),
        scratch_shapes=[pltpu.VMEM((TOK, 2048), BF16), pltpu.VMEM((2048, 256), BF16)],
        compiler_params=pltpu.CompilerParams(vmem_limit_bytes=VMEM_LIMIT),
        cost_estimate=pl.CostEstimate(
            flops=4 * TOK * 2048 * 512, bytes_accessed=7 << 20, transcendentals=0
        ),
    )(z, *blocks, own, other)


def product_kernel(scale, at_ref, *refs):
    acts, grads, out_ref, right = refs[:8], refs[8:16], refs[16], refs[17]
    z, xh, y, xl, c = (at_ref[i] for i in range(5))
    for k, offset in enumerate(OFFSETS):
        for half in range(2):
            place = (xh if half == 0 else 1 - xh) * 8 + lax.rem(z + 8 + offset, 8)
            for s in range(4):
                right[s, pl.ds(pl.multiple_of(place * 32, 32), 32), :] = acts[k][half, s]
    for step in range(4):
        total = None
        for core in range(2):
            for side in range(2):
                s = (xl if side == 0 else 1 - xl) * 2 + (c if core == 0 else 1 - c)
                part = lax.dot_general(
                    grads[core * 4 + step][side],
                    right[s],
                    (((1,), (1,)), ((), ())),
                    preferred_element_type=F32,
                )
                total = part * part if total is None else total + part * part
        out_ref[lax.rem(y + step, 4)] = total * scale


def products(at, acts, grads, scale):
    return pl.pallas_call(
        functools.partial(product_kernel, scale),
        out_shape=jax.ShapeDtypeStruct((4, COLS, 512), F32),
        in_specs=[pl.BlockSpec(memory_space=pltpu.SMEM)]
        + [pl.BlockSpec(memory_space=pltpu.VMEM)] * 16,
        out_specs=pl.BlockSpec(memory_space=pltpu.VMEM),
        scratch_shapes=[pltpu.VMEM((4, 512, TOK), BF16)],
        compiler_params=pltpu.CompilerParams(vmem_limit_bytes=VMEM_LIMIT),
        cost_estimate=pl.CostEstimate(
            flops=2 * 4 * 512 * 512 * TOK, bytes_accessed=5 << 20, transcendentals=0
        ),
    )(at, *acts, *grads)


def weave_kernel(in_ref, out_ref):
    for tile in range(4):
        lanes = slice(tile * 32, tile * 32 + 32)
        out_ref[:, tile * COLS : (tile + 1) * COLS] = jnp.concatenate(
            [in_ref[q, :, lanes] for q in range(4)], axis=1
        )


def weave(parts):
    return pl.pallas_call(
        weave_kernel,
        grid=(4,),
        out_shape=jax.ShapeDtypeStruct((COLS, 2048), F32),
        in_specs=[pl.BlockSpec((4, COLS, 128), lambda g: (0, 0, g))],
        out_specs=pl.BlockSpec((COLS, 512), lambda g: (0, g)),
        compiler_params=pltpu.CompilerParams(vmem_limit_bytes=VMEM_LIMIT),
    )(parts)


def spread_basis(basis):
    halves = basis.reshape(4, 2, 1024, COLS)
    mine = lax.dynamic_index_in_dim(halves, lax.axis_index("c"), 1, keepdims=False)
    own = lax.all_to_all(mine, "y", 0, 0)
    return own, shift(own, "c", 1)


def gather_rows(x):
    x = x[0]
    other = shift(x, "xh", 1)
    same = lax.axis_index("xh") == lax.axis_index("c")
    pair = jnp.concatenate(
        [jnp.where(same, x, other), jnp.where(same, other, x)], axis=1
    )
    return gather_z(pair)


def body(activations, gradients, basis_in, basis_out):
    z, xh, y, xl, c = (lax.axis_index(a) for a in ("z", "xh", "y", "xl", "c"))
    at = jnp.stack([z, xh, y, xl, c]).astype(jnp.int32)

    act_blocks = gather_rows(activations)
    own_in, other_in = spread_basis(basis_in)
    acts_part = rotate(at, act_blocks, own_in, other_in)
    acts_in = lax.all_to_all(acts_part.reshape(16, 32, TOK), ("xl", "c", "y"), 0, 0)
    acts = jnp.sum(acts_in.reshape(4, 4, 32, TOK), axis=1).astype(BF16)
    acts_pair = jnp.stack([acts, shift(acts, "xh", 1)])
    rot_acts = gather_z(acts_pair)

    grad_blocks = gather_rows(gradients)
    own_out, other_out = spread_basis(basis_out)
    grads_part = rotate(at, grad_blocks, own_out, other_out)
    grads_in = lax.all_to_all(grads_part, "y", 0, 0)
    grads = jnp.sum(grads_in, axis=0).astype(BF16)
    sides = jnp.stack([grads, shift(grads, "xl", 1)])
    along = [sides] + [shift(sides, "y", -step) for step in range(1, 4)]
    rot_grads = along + [shift(block, "c", 1) for block in along]

    scale = 1.0 / (TOK * 4)
    part = products(at, rot_acts, rot_grads, scale)
    return weave(lax.all_to_all(part, "y", 0, 0))


def solution(mesh):
    fine = Mesh(mesh.devices.reshape(SIZES), AXES)
    return jax.shard_map(
        body,
        mesh=fine,
        in_specs=(P(DP, None, TILE), P(DP, None, TILE), P(None, TILE), P(None, TILE)),
        out_specs=P(TILE, DP),
        check_vma=False,
    )
```

```python
import functools

import jax
import jax.numpy as jnp
from jax import lax
from jax.experimental import pallas as pl
from jax.experimental.pallas import tpu as pltpu
from jax.sharding import Mesh, PartitionSpec as P

AXES = ("xl", "c", "y", "xh", "z")
SIZES = (2, 2, 4, 2, 8)
DP = ("xl", "c")
TILE = ("y", "xh", "z")
TOK = 512
COLS = 128
F32 = jnp.float32
BF16 = jnp.bfloat16
VMEM_LIMIT = 48 * 1024 * 1024
PARAMS = pltpu.CompilerParams(vmem_limit_bytes=VMEM_LIMIT)


def shift(x, axis, by):
    n = lax.axis_size(axis)
    return lax.ppermute(x, axis, [(i, (i + by) % n) for i in range(n)])


def after(x, *others):
    return lax.optimization_barrier((x, *others))[0]


def whole(shape):
    return pl.BlockSpec(shape, lambda *_: (0,) * len(shape))


def split_kernel(core_ref, in_ref, out_ref):
    exact = in_ref[...]
    high = exact.astype(BF16)
    out_ref[0, :, :COLS] = high
    out_ref[0, :, COLS:] = (exact - high.astype(F32)).astype(BF16)


def split_basis(core, basis):
    return pl.pallas_call(
        split_kernel,
        grid_spec=pltpu.PrefetchScalarGridSpec(
            num_scalar_prefetch=1,
            grid=(4,),
            in_specs=[pl.BlockSpec((1024, COLS), lambda g, core: (g * 2 + core[0], 0))],
            out_specs=pl.BlockSpec((1, 1024, 256), lambda g, core: (g, 0, 0)),
        ),
        out_shape=jax.ShapeDtypeStruct((4, 1024, 256), BF16),
        compiler_params=PARAMS,
        cost_estimate=pl.CostEstimate(
            flops=1 << 20, bytes_accessed=4 << 20, transcendentals=0
        ),
    )(core, basis)


def rotate_kernel(places, at_ref, *refs):
    blocks, (own_ref, other_ref, out_ref, lhs) = refs[: len(places)], refs[len(places) :]

    @pl.when(pl.program_id(0) == 0)
    def _():
        z, xh, c = at_ref[0], at_ref[1], at_ref[4]
        turned = lax.rem(xh + c, 2)
        for block, parts in zip(blocks, places):
            for i, (offset, side) in enumerate(parts):
                half = turned if side == 0 else 1 - turned
                at = (half * 8 + lax.rem(z + 8 + offset, 8)) * COLS
                lhs[:, pl.ds(pl.multiple_of(at, COLS), COLS)] = block[i]

    both = jnp.dot(lhs[:, :1024], own_ref[0], preferred_element_type=F32)
    both += jnp.dot(lhs[:, 1024:], other_ref[0], preferred_element_type=F32)
    out_ref[0] = (both[:, :COLS] + both[:, COLS:]).T


def rotate(at, blocks, places, own, other):
    slab = pl.BlockSpec((1, 1024, 256), lambda g: (g, 0, 0))
    return pl.pallas_call(
        functools.partial(rotate_kernel, places),
        grid=(4,),
        out_shape=jax.ShapeDtypeStruct((4, COLS, TOK), F32),
        in_specs=[pl.BlockSpec(memory_space=pltpu.SMEM)]
        + [whole(b.shape) for b in blocks]
        + [slab, slab],
        out_specs=pl.BlockSpec((1, COLS, TOK), lambda g: (g, 0, 0)),
        scratch_shapes=[pltpu.VMEM((TOK, 2048), BF16)],
        compiler_params=PARAMS,
        cost_estimate=pl.CostEstimate(
            flops=4 * TOK * 2048 * 512, bytes_accessed=7 << 20, transcendentals=0
        ),
    )(at, *blocks, own, other)


def product_kernel(scale, places, at_ref, *refs):
    n = len(places)
    acts, grads, out_ref, right = refs[:n], refs[n : n + 2], refs[n + 2], refs[n + 3]
    z, xh, y, xl, c = (at_ref[i] for i in range(5))
    for block, parts in zip(acts, places):
        for i, (offset, side) in enumerate(parts):
            place = (xh if side == 0 else 1 - xh) * 8 + lax.rem(z + 8 + offset, 8)
            for s in range(4):
                right[s, pl.ds(pl.multiple_of(place * 32, 32), 32), :] = block[i, s]
    for row in range(4):
        total = None
        for core in range(2):
            for side in range(2):
                s = side * 2 + (c if core == 0 else 1 - c)
                part = lax.dot_general(
                    grads[core][side, row],
                    right[s],
                    (((1,), (1,)), ((), ())),
                    preferred_element_type=F32,
                )
                total = part * part if total is None else total + part * part
        out_ref[row] = total * scale


def products(at, acts, places, grads, scale):
    return pl.pallas_call(
        functools.partial(product_kernel, scale, places),
        out_shape=jax.ShapeDtypeStruct((4, COLS, 512), F32),
        in_specs=[pl.BlockSpec(memory_space=pltpu.SMEM)]
        + [pl.BlockSpec(memory_space=pltpu.VMEM)] * (len(acts) + 2),
        out_specs=pl.BlockSpec(memory_space=pltpu.VMEM),
        scratch_shapes=[pltpu.VMEM((4, 512, TOK), BF16)],
        compiler_params=PARAMS,
        cost_estimate=pl.CostEstimate(
            flops=2 * 4 * 512 * 512 * TOK, bytes_accessed=5 << 20, transcendentals=0
        ),
    )(at, *acts, *grads)


def weave_kernel(in_ref, out_ref):
    for tile in range(4):
        lanes = slice(tile * 32, tile * 32 + 32)
        out_ref[:, tile * COLS : (tile + 1) * COLS] = jnp.concatenate(
            [in_ref[q, :, lanes] for q in range(4)], axis=1
        )


def weave(parts):
    return pl.pallas_call(
        weave_kernel,
        grid=(4,),
        out_shape=jax.ShapeDtypeStruct((COLS, 2048), F32),
        in_specs=[pl.BlockSpec((4, COLS, 128), lambda g: (0, 0, g))],
        out_specs=pl.BlockSpec((COLS, 512), lambda g: (0, g)),
        compiler_params=PARAMS,
    )(parts)


def sync(*arrays):
    return lax.optimization_barrier(arrays)


def ring_step(up, down):
    return shift(up, "z", 1), shift(down, "z", -1)


PAIR = ((0, 0), (0, 1))


def both_sides(offset):
    return ((offset, 0), (offset, 1))


def body(activations, gradients, basis_in, basis_out):
    z, xh, y, xl, c = (lax.axis_index(a) for a in ("z", "xh", "y", "xl", "c"))
    at = jnp.stack([z, xh, y, xl, c]).astype(jnp.int32)
    core = c.astype(jnp.int32).reshape(1)

    own_in = lax.all_to_all(split_basis(core, basis_in), "y", 0, 0)
    acts_other = shift(activations, "xh", 1)
    g_up1, g_down1 = ring_step(gradients, gradients)
    acts_other, g_up1, g_down1, basis_out = sync(acts_other, g_up1, g_down1, basis_out)

    a0 = jnp.concatenate([activations, acts_other])
    g_near = jnp.concatenate([gradients, g_up1, g_down1])
    a_up1, a_down1 = ring_step(a0, a0)
    g_near_other = shift(g_near, "xh", 1)
    g_up2, g_down2 = ring_step(g_up1, g_down1)
    mine_out = split_basis(core, basis_out)
    a_up1, a_down1, g_near_other, g_up2, g_down2, mine_out = sync(
        a_up1, a_down1, g_near_other, g_up2, g_down2, mine_out
    )

    a_up2, a_down2 = ring_step(a_up1, a_down1)
    g_two = jnp.concatenate([g_up2, g_down2])
    g_two_other = shift(g_two, "xh", 1)
    g_up3, g_down3 = ring_step(g_up2, g_down2)
    a_up2, a_down2, g_two_other, g_up3, g_down3, mine_out, own_in = sync(
        a_up2, a_down2, g_two_other, g_up3, g_down3, mine_out, own_in
    )

    own_out = lax.all_to_all(mine_out, "y", 0, 0)
    a_up3, a_down3 = ring_step(a_up2, a_down2)
    g_three = jnp.concatenate([g_up3, g_down3])
    g_three_other = shift(g_three, "xh", 1)
    g_up4 = shift(g_up3, "z", 1)
    other_in = shift(own_in, "c", 1)
    a_up3, a_down3, g_three_other, g_up4, other_in = sync(
        a_up3, a_down3, g_three_other, g_up4, other_in
    )

    a_up4, a_down4 = ring_step(a_up3[:1], a_down3[1:])
    g_four_other = shift(g_up4, "xh", 1)
    act_blocks = [a0, a_up1, a_down1, a_up2, a_down2, a_up3, a_down3, a_up4, a_down4]
    act_places = [both_sides(o) for o in (0, -1, 1, -2, 2, -3, 3)] + [((-4, 0),), ((4, 1),)]
    acts_part = rotate(at, act_blocks, act_places, own_in, other_in)
    acts_in = lax.all_to_all(acts_part.reshape(16, 32, TOK), ("xl", "c", "y"), 0, 0)

    grad_blocks = [g_near, g_near_other, g_two, g_two_other, g_three, g_three_other, g_up4, g_four_other]
    grad_places = []
    for offsets in ((0, -1, 1), (-2, 2), (-3, 3), (-4,)):
        grad_places += [tuple((o, 0) for o in offsets), tuple((o, 1) for o in offsets)]
    other_out = shift(after(own_out, acts_part), "c", 1)
    grads_part = rotate(at, grad_blocks, grad_places, own_out, other_out)
    grads_in = lax.all_to_all(grads_part, "y", 0, 0)

    acts = jnp.sum(acts_in.reshape(4, 4, 32, TOK), axis=1).astype(BF16)[None]
    r0 = jnp.concatenate([acts, shift(acts, "xh", 1)])
    r_up1, r_down1 = sync(*ring_step(r0, r0))
    r_up2, r_down2, grads_in = sync(*ring_step(r_up1, r_down1), grads_in)
    grads = jnp.sum(grads_in, axis=0).astype(BF16)
    copies = jnp.broadcast_to(grads, (8, COLS, TOK))
    rot_own = lax.all_to_all(copies, ("xl", "y"), 0, 0).reshape(2, 4, COLS, TOK)
    r_up3, r_down3, rot_own = sync(*ring_step(r_up2, r_down2), rot_own)
    r_up4, r_down4 = ring_step(r_up3[:1], r_down3[1:])
    rot_grads = [rot_own, shift(rot_own, "c", 1)]
    rot_acts = [r0, r_up1, r_down1, r_up2, r_down2, r_up3, r_down3, r_up4, r_down4]

    scale = 1.0 / (TOK * 4)
    part = products(at, rot_acts, act_places, rot_grads, scale)
    return weave(lax.all_to_all(part, "y", 0, 0))


def solution(mesh):
    fine = Mesh(mesh.devices.reshape(SIZES), AXES)
    return jax.shard_map(
        body,
        mesh=fine,
        in_specs=(P(DP, None, TILE), P(DP, None, TILE), P(None, TILE), P(None, TILE)),
        out_specs=P(TILE, DP),
        check_vma=False,
    )
```

```python
import functools

import jax
import jax.numpy as jnp
from jax import lax
from jax.experimental import pallas as pl
from jax.experimental.pallas import tpu as pltpu
from jax.sharding import Mesh, PartitionSpec as P

AXES = ("xl", "c", "y", "xh", "z")
SIZES = (2, 2, 4, 2, 8)
DP = ("xl", "c")
TILE = ("y", "xh", "z")
TOK = 512
COLS = 128
F32 = jnp.float32
BF16 = jnp.bfloat16
VMEM_LIMIT = 48 * 1024 * 1024
PARAMS = pltpu.CompilerParams(vmem_limit_bytes=VMEM_LIMIT)


def shift(x, axis, by):
    n = lax.axis_size(axis)
    return lax.ppermute(x, axis, [(i, (i + by) % n) for i in range(n)])


def after(x, *others):
    return lax.optimization_barrier((x, *others))[0]


def whole(shape):
    return pl.BlockSpec(shape, lambda *_: (0,) * len(shape))


def split_kernel(rows_ref, in_ref, own_ref, near_ref, far_ref):
    def put(out_ref):
        exact = in_ref[...]
        high = exact.astype(BF16)
        out_ref[:, :COLS] = high
        out_ref[:, COLS:] = (exact - high.astype(F32)).astype(BF16)

    step = pl.program_id(0)
    pl.when(step < 2)(lambda: put(own_ref))
    pl.when((step >= 2) & (step < 4))(lambda: put(near_ref))
    pl.when(step == 4)(lambda: put(far_ref))


def split_basis(rows, basis):
    return pl.pallas_call(
        split_kernel,
        grid_spec=pltpu.PrefetchScalarGridSpec(
            num_scalar_prefetch=1,
            grid=(5,),
            in_specs=[pl.BlockSpec((1024, COLS), lambda g, rows: (rows[g], 0))],
            out_specs=[
                pl.BlockSpec((1024, 256), lambda g, rows: (jnp.minimum(g, 1), 0)),
                pl.BlockSpec((1024, 256), lambda g, rows: (jnp.clip(g - 2, 0, 1), 0)),
                pl.BlockSpec((1024, 256), lambda g, rows: (0, 0)),
            ],
        ),
        out_shape=[jax.ShapeDtypeStruct((n, 256), BF16) for n in (2048, 2048, 1024)],
        compiler_params=PARAMS,
        cost_estimate=pl.CostEstimate(
            flops=1 << 20, bytes_accessed=5 << 20, transcendentals=0
        ),
    )(rows, basis)


def rotate_kernel(places, at_ref, *refs):
    blocks, refs = refs[: len(places)], refs[len(places) :]
    own_ref, near_ref, near_swapped, far_ref, far_swapped, out_ref, lhs = refs
    z, xh, y, c = at_ref[0], at_ref[1], at_ref[2], at_ref[4]
    for block, parts in zip(blocks, places):
        for i, (offset, side, token) in enumerate(parts):
            half = xh if side == 0 else 1 - xh
            at = (half * 8 + lax.rem(z + 8 + offset, 8)) * COLS
            rows = pl.ds(token, block.shape[1])
            lhs[rows, pl.ds(pl.multiple_of(at, COLS), COLS)] = block[i]

    def put(place, both):
        out_ref[lax.rem(place, 4)] = (both[:, :COLS] + both[:, COLS:]).T

    for offset, ref in ((4, own_ref), (3 + 2 * c, near_ref), (5 - 2 * c, near_swapped)):
        put(y + offset, jnp.dot(lhs[...], ref[...], preferred_element_type=F32))
    mine = lhs[:, pl.ds(pl.multiple_of(c * 1024, 1024), 1024)]
    rest = lhs[:, pl.ds(pl.multiple_of((1 - c) * 1024, 1024), 1024)]
    both = jnp.dot(mine, far_ref[...], preferred_element_type=F32)
    put(y + 2, both + jnp.dot(rest, far_swapped[...], preferred_element_type=F32))


def rotate(at, entries, slabs):
    blocks = [
        pl.BlockSpec((len(parts), *array.shape[1:]), lambda g, index=index: (index, 0, 0))
        for array, index, parts in entries
    ]
    return pl.pallas_call(
        functools.partial(rotate_kernel, [parts for _, _, parts in entries]),
        grid=(1,),
        out_shape=jax.ShapeDtypeStruct((4, COLS, TOK), F32),
        in_specs=[pl.BlockSpec(memory_space=pltpu.SMEM)]
        + blocks
        + [whole(slab.shape) for slab in slabs],
        out_specs=whole((4, COLS, TOK)),
        scratch_shapes=[pltpu.VMEM((TOK, 2048), BF16)],
        compiler_params=PARAMS,
        cost_estimate=pl.CostEstimate(
            flops=4 * TOK * 2048 * 512, bytes_accessed=7 << 20, transcendentals=0
        ),
    )(at, *[array for array, _, _ in entries], *slabs)


def product_kernel(scale, places, at_ref, *refs):
    n = len(places)
    acts, grads, out_ref, right = refs[:n], refs[n : n + 2], refs[n + 2], refs[n + 3]
    z, xh, y, xl, c = (at_ref[i] for i in range(5))
    for block, parts in zip(acts, places):
        for i, (offset, side) in enumerate(parts):
            place = (xh if side == 0 else 1 - xh) * 8 + lax.rem(z + 8 + offset, 8)
            for s in range(4):
                right[s, pl.ds(pl.multiple_of(place * 32, 32), 32), :] = block[i, s]
    for row in range(4):
        total = None
        for core in range(2):
            for side in range(2):
                s = side * 2 + (c if core == 0 else 1 - c)
                part = lax.dot_general(
                    grads[core][side, row],
                    right[s],
                    (((1,), (1,)), ((), ())),
                    preferred_element_type=F32,
                )
                total = part * part if total is None else total + part * part
        out_ref[row] = total * scale


def products(at, acts, places, grads, scale):
    return pl.pallas_call(
        functools.partial(product_kernel, scale, places),
        out_shape=jax.ShapeDtypeStruct((4, COLS, 512), F32),
        in_specs=[pl.BlockSpec(memory_space=pltpu.SMEM)]
        + [pl.BlockSpec(memory_space=pltpu.VMEM)] * (len(acts) + 2),
        out_specs=pl.BlockSpec(memory_space=pltpu.VMEM),
        scratch_shapes=[pltpu.VMEM((4, 512, TOK), BF16)],
        compiler_params=PARAMS,
        cost_estimate=pl.CostEstimate(
            flops=2 * 4 * 512 * 512 * TOK, bytes_accessed=5 << 20, transcendentals=0
        ),
    )(at, *acts, *grads)


def weave_kernel(in_ref, out_ref):
    for tile in range(4):
        lanes = slice(tile * 32, tile * 32 + 32)
        out_ref[:, tile * COLS : (tile + 1) * COLS] = jnp.concatenate(
            [in_ref[q, :, lanes] for q in range(4)], axis=1
        )


def weave(parts):
    return pl.pallas_call(
        weave_kernel,
        grid=(4,),
        out_shape=jax.ShapeDtypeStruct((COLS, 2048), F32),
        in_specs=[pl.BlockSpec((4, COLS, 128), lambda g: (0, 0, g))],
        out_specs=pl.BlockSpec((COLS, 512), lambda g: (0, g)),
        compiler_params=PARAMS,
    )(parts)


def sync(*arrays):
    return lax.optimization_barrier(arrays)


def ring_step(up, down):
    return shift(up, "z", 1), shift(down, "z", -1)


def shift_near(x):
    pairs = [(i, (i + 1) % 4) for i in range(4)] + [(4 + i, 4 + (i + 3) % 4) for i in range(4)]
    return lax.ppermute(x, ("c", "y"), pairs)


def body(activations, gradients, basis_in, basis_out):
    z, xh, y, xl, c = (lax.axis_index(a) for a in ("z", "xh", "y", "xl", "c"))
    at = jnp.stack([z, xh, y, xl, c]).astype(jnp.int32)
    near_y, far_y = (y + 1 + 2 * c) % 4, (y + 2) % 4
    rows = jnp.stack(
        [y * 2, y * 2 + 1, near_y * 2, near_y * 2 + 1, far_y * 2 + c]
    ).astype(jnp.int32)

    own_in, near_in, far_in = split_basis(rows, basis_in)
    acts_other, own_in, near_in, far_in, basis_out = sync(
        shift(activations, "xh", 1), own_in, near_in, far_in, basis_out
    )
    base = jnp.concatenate([activations, acts_other, gradients])
    own_out, near_out, far_out = split_basis(rows, basis_out)
    up1, down1, near_in, far_in, own_out, near_out, far_out = sync(
        *ring_step(base, base), shift_near(near_in), far_in, own_out, near_out, far_out
    )
    up2, down2, far_in, near_in2, near_out, far_out = sync(
        *ring_step(up1, down1), shift(far_in, "y", 2), shift(near_in, "c", 1), near_out, far_out
    )
    near = jnp.concatenate([a[2:] for a in (base, up1, down1, up2, down2)])
    up3, down3, near_out, far_in2, near_other, far_out = sync(
        *ring_step(up2, down2), shift_near(near_out), shift(far_in, "c", 1), shift(near, "xh", 1), far_out
    )
    up_end = jnp.concatenate([up3[0].reshape(2, 256, COLS), up3[2:, :256]])
    down_end = jnp.concatenate([down3[1].reshape(2, 256, COLS), down3[2:, 256:]])
    far_out = shift(far_out, "y", 2)
    up4, down4, near_out2 = sync(*ring_step(up_end, down_end), shift(near_out, "c", 1))
    ring = [(base, 0), (up1, -1), (down1, 1), (up2, -2), (down2, 2), (up3, -3), (down3, 3)]

    acts_entries = [(a, 0, ((o, 0, 0), (o, 1, 0))) for a, o in ring]
    acts_entries += [(up4, 0, ((-4, 0, 0), (-4, 0, 256))), (down4, 0, ((4, 1, 0), (4, 1, 256)))]
    acts_part = rotate(at, acts_entries, (own_in, near_in, near_in2, far_in, far_in2))
    acts_in = lax.all_to_all(acts_part.reshape(16, 32, TOK), ("xl", "c", "y"), 0, 0)

    end = jnp.concatenate([up4[2], down4[2]])[None]
    far_other = shift(jnp.concatenate([up3[2:], down3[2:], end]), "xh", 1)
    far_out2 = shift(after(far_out, acts_part), "c", 1)
    grads_entries = [(a, 2, ((o, 0, 0),)) for a, o in ring]
    grads_entries += [(up4, 2, ((-4, 0, 0),)), (down4, 2, ((4, 0, 256),))]
    grads_entries += [(near_other, 0, tuple((o, 1, 0) for o in (0, -1, 1, -2, 2)))]
    grads_entries += [(far_other, 0, tuple((o, 1, 0) for o in (-3, 3, 4)))]
    grads_part = rotate(at, grads_entries, (own_out, near_out, near_out2, far_out, far_out2))
    grads_in = lax.all_to_all(grads_part, "y", 0, 0)

    acts = jnp.sum(acts_in.reshape(4, 4, 32, TOK), axis=1).astype(BF16)[None]
    r0 = jnp.concatenate([acts, shift(acts, "xh", 1)])
    r_up1, r_down1 = sync(*ring_step(r0, r0))
    r_up2, r_down2, grads_in = sync(*ring_step(r_up1, r_down1), grads_in)
    grads = jnp.sum(grads_in, axis=0).astype(BF16)
    copies = jnp.broadcast_to(grads, (8, COLS, TOK))
    rot_own = lax.all_to_all(copies, ("xl", "y"), 0, 0).reshape(2, 4, COLS, TOK)
    r_up3, r_down3, rot_own = sync(*ring_step(r_up2, r_down2), rot_own)
    r_up4, r_down4 = ring_step(r_up3[:1], r_down3[1:])
    rot_grads = [rot_own, shift(rot_own, "c", 1)]
    rot_acts = [r0, r_up1, r_down1, r_up2, r_down2, r_up3, r_down3, r_up4, r_down4]
    rot_places = [((o, 0), (o, 1)) for _, o in ring] + [((-4, 0),), ((4, 1),)]

    scale = 1.0 / (TOK * 4)
    part = products(at, rot_acts, rot_places, rot_grads, scale)
    return weave(lax.all_to_all(part, "y", 0, 0))


def solution(mesh):
    fine = Mesh(mesh.devices.reshape(SIZES), AXES)
    return jax.shard_map(
        body,
        mesh=fine,
        in_specs=(P(DP, None, TILE), P(DP, None, TILE), P(None, TILE), P(None, TILE)),
        out_specs=P(TILE, DP),
        check_vma=False,
    )
```

```python
import functools

import jax
import jax.numpy as jnp
from jax import lax
from jax.experimental import pallas as pl
from jax.experimental.pallas import tpu as pltpu
from jax.sharding import Mesh, PartitionSpec as P

AXES = ("xl", "c", "y", "xh", "z")
SIZES = (2, 2, 4, 2, 8)
DP = ("xl", "c")
TILE = ("y", "xh", "z")
TOK = 512
COLS = 128
F32 = jnp.float32
BF16 = jnp.bfloat16
VMEM_LIMIT = 48 * 1024 * 1024
PARAMS = pltpu.CompilerParams(vmem_limit_bytes=VMEM_LIMIT)


def shift(x, axis, by):
    n = lax.axis_size(axis)
    return lax.ppermute(x, axis, [(i, (i + by) % n) for i in range(n)])


def after(x, *others):
    return lax.optimization_barrier((x, *others))[0]


def whole(shape):
    return pl.BlockSpec(shape, lambda *_: (0,) * len(shape))


def split_kernel(core_ref, in_ref, out_ref):
    exact = in_ref[...]
    high = exact.astype(BF16)
    out_ref[0, :, :COLS] = high
    out_ref[0, :, COLS:] = (exact - high.astype(F32)).astype(BF16)


def split_basis(core, basis):
    return pl.pallas_call(
        split_kernel,
        grid_spec=pltpu.PrefetchScalarGridSpec(
            num_scalar_prefetch=1,
            grid=(4,),
            in_specs=[pl.BlockSpec((1024, COLS), lambda g, core: (g * 2 + core[0], 0))],
            out_specs=pl.BlockSpec((1, 1024, 256), lambda g, core: (g, 0, 0)),
        ),
        out_shape=jax.ShapeDtypeStruct((4, 1024, 256), BF16),
        compiler_params=PARAMS,
        cost_estimate=pl.CostEstimate(
            flops=1 << 20, bytes_accessed=4 << 20, transcendentals=0
        ),
    )(core, basis)


def rotate_kernel(places, at_ref, *refs):
    blocks, (own_ref, other_ref, out_ref, lhs) = refs[: len(places)], refs[len(places) :]

    @pl.when(pl.program_id(0) == 0)
    def _():
        z, xh, c = at_ref[0], at_ref[1], at_ref[4]
        turned = lax.rem(xh + c, 2)
        for block, parts in zip(blocks, places):
            for i, (offset, side) in enumerate(parts):
                half = turned if side == 0 else 1 - turned
                at = (half * 8 + lax.rem(z + 8 + offset, 8)) * COLS
                lhs[:, pl.ds(pl.multiple_of(at, COLS), COLS)] = block[i]

    both = jnp.dot(lhs[:, :1024], own_ref[0], preferred_element_type=F32)
    both += jnp.dot(lhs[:, 1024:], other_ref[0], preferred_element_type=F32)
    out_ref[0] = (both[:, :COLS] + both[:, COLS:]).T


def rotate(at, entries, own, other):
    slab = pl.BlockSpec((1, 1024, 256), lambda g: (g, 0, 0))
    blocks = [
        pl.BlockSpec((len(parts), *array.shape[1:]), lambda g, index=index: (index, 0, 0))
        for array, index, parts in entries
    ]
    return pl.pallas_call(
        functools.partial(rotate_kernel, [parts for _, _, parts in entries]),
        grid=(4,),
        out_shape=jax.ShapeDtypeStruct((4, COLS, TOK), F32),
        in_specs=[pl.BlockSpec(memory_space=pltpu.SMEM)] + blocks + [slab, slab],
        out_specs=pl.BlockSpec((1, COLS, TOK), lambda g: (g, 0, 0)),
        scratch_shapes=[pltpu.VMEM((TOK, 2048), BF16)],
        compiler_params=PARAMS,
        cost_estimate=pl.CostEstimate(
            flops=4 * TOK * 2048 * 512, bytes_accessed=7 << 20, transcendentals=0
        ),
    )(at, *[array for array, _, _ in entries], own, other)


def product_kernel(scale, places, at_ref, *refs):
    n = len(places)
    acts, grads, out_ref, right = refs[:n], refs[n : n + 2], refs[n + 2], refs[n + 3]
    z, xh, y, xl, c = (at_ref[i] for i in range(5))
    for block, parts in zip(acts, places):
        for i, (offset, side) in enumerate(parts):
            place = (xh if side == 0 else 1 - xh) * 8 + lax.rem(z + 8 + offset, 8)
            for s in range(4):
                right[s, pl.ds(pl.multiple_of(place * 32, 32), 32), :] = block[i, s]
    for row in range(4):
        total = None
        for core in range(2):
            for side in range(2):
                s = side * 2 + (c if core == 0 else 1 - c)
                part = lax.dot_general(
                    grads[core][side, row],
                    right[s],
                    (((1,), (1,)), ((), ())),
                    preferred_element_type=F32,
                )
                total = part * part if total is None else total + part * part
        out_ref[row] = total * scale


def products(at, acts, places, grads, scale):
    return pl.pallas_call(
        functools.partial(product_kernel, scale, places),
        out_shape=jax.ShapeDtypeStruct((4, COLS, 512), F32),
        in_specs=[pl.BlockSpec(memory_space=pltpu.SMEM)]
        + [pl.BlockSpec(memory_space=pltpu.VMEM)] * (len(acts) + 2),
        out_specs=pl.BlockSpec(memory_space=pltpu.VMEM),
        scratch_shapes=[pltpu.VMEM((4, 512, TOK), BF16)],
        compiler_params=PARAMS,
        cost_estimate=pl.CostEstimate(
            flops=2 * 4 * 512 * 512 * TOK, bytes_accessed=5 << 20, transcendentals=0
        ),
    )(at, *acts, *grads)


def weave_kernel(in_ref, out_ref):
    for tile in range(4):
        lanes = slice(tile * 32, tile * 32 + 32)
        out_ref[:, tile * COLS : (tile + 1) * COLS] = jnp.concatenate(
            [in_ref[q, :, lanes] for q in range(4)], axis=1
        )


def weave(parts):
    return pl.pallas_call(
        weave_kernel,
        grid=(4,),
        out_shape=jax.ShapeDtypeStruct((COLS, 2048), F32),
        in_specs=[pl.BlockSpec((4, COLS, 128), lambda g: (0, 0, g))],
        out_specs=pl.BlockSpec((COLS, 512), lambda g: (0, g)),
        compiler_params=PARAMS,
    )(parts)


def sync(*arrays):
    return lax.optimization_barrier(arrays)


def ring_step(up, down):
    return shift(up, "z", 1), shift(down, "z", -1)


def body(activations, gradients, basis_in, basis_out):
    z, xh, y, xl, c = (lax.axis_index(a) for a in ("z", "xh", "y", "xl", "c"))
    at = jnp.stack([z, xh, y, xl, c]).astype(jnp.int32)
    core = c.astype(jnp.int32).reshape(1)

    acts_other, mine_in, basis_out = sync(
        shift(activations, "xh", 1), split_basis(core, basis_in), basis_out
    )
    own_in = lax.all_to_all(mine_in, "y", 0, 0)
    base = jnp.concatenate([activations, acts_other, gradients])
    up1, down1, mine_out = sync(*ring_step(base, base), split_basis(core, basis_out))
    up2, down2, mine_out, own_in = sync(*ring_step(up1, down1), mine_out, own_in)
    own_out = lax.all_to_all(mine_out, "y", 0, 0)
    near = jnp.concatenate([a[2:] for a in (base, up1, down1, up2, down2)])
    up3, down3, other_in, near_other = sync(
        *ring_step(up2, down2), shift(own_in, "c", 1), shift(near, "xh", 1)
    )
    three = jnp.concatenate([up3[2:], down3[2:]])
    up4, three_other = sync(shift(up3, "z", 1), shift(three, "xh", 1))
    ring = [(base, 0), (up1, -1), (down1, 1), (up2, -2), (down2, 2), (up3, -3), (down3, 3), (up4, -4)]

    acts_entries = [(a, 0, ((o, 0), (o, 1))) for a, o in ring]
    acts_part = rotate(at, acts_entries, own_in, other_in)
    acts_in = lax.all_to_all(acts_part.reshape(16, 32, TOK), ("xl", "c", "y"), 0, 0)

    four_other = shift(up4[2:], "xh", 1)
    other_out = shift(after(own_out, acts_part), "c", 1)
    grads_entries = [(a, 2, ((o, 0),)) for a, o in ring]
    grads_entries += [(near_other, 0, tuple((o, 1) for o in (0, -1, 1, -2, 2)))]
    grads_entries += [(three_other, 0, ((-3, 1), (3, 1))), (four_other, 0, ((4, 1),))]
    grads_part = rotate(at, grads_entries, own_out, other_out)
    grads_in = lax.all_to_all(grads_part, "y", 0, 0)

    acts = jnp.sum(acts_in.reshape(4, 4, 32, TOK), axis=1).astype(BF16)[None]
    r0 = jnp.concatenate([acts, shift(acts, "xh", 1)])
    r_up1, r_down1 = sync(*ring_step(r0, r0))
    r_up2, r_down2, grads_in = sync(*ring_step(r_up1, r_down1), grads_in)
    grads = jnp.sum(grads_in, axis=0).astype(BF16)
    copies = jnp.broadcast_to(grads, (8, COLS, TOK))
    rot_own = lax.all_to_all(copies, ("xl", "y"), 0, 0).reshape(2, 4, COLS, TOK)
    r_up3, r_down3, rot_own = sync(*ring_step(r_up2, r_down2), rot_own)
    r_up4 = shift(r_up3, "z", 1)
    rot_grads = [rot_own, shift(rot_own, "c", 1)]
    rot_acts = [r0, r_up1, r_down1, r_up2, r_down2, r_up3, r_down3, r_up4]
    rot_places = [((o, 0), (o, 1)) for _, o in ring]

    scale = 1.0 / (TOK * 4)
    part = products(at, rot_acts, rot_places, rot_grads, scale)
    return weave(lax.all_to_all(part, "y", 0, 0))


def solution(mesh):
    fine = Mesh(mesh.devices.reshape(SIZES), AXES)
    return jax.shard_map(
        body,
        mesh=fine,
        in_specs=(P(DP, None, TILE), P(DP, None, TILE), P(None, TILE), P(None, TILE)),
        out_specs=P(TILE, DP),
        check_vma=False,
    )
```

```python
import functools

import jax
import jax.numpy as jnp
from jax import lax
from jax.experimental import pallas as pl
from jax.experimental.pallas import tpu as pltpu
from jax.sharding import Mesh, PartitionSpec as P

AXES = ("xl", "c", "y", "xh", "z")
SIZES = (2, 2, 4, 2, 8)
DP = ("xl", "c")
TILE = ("y", "xh", "z")
TOK = 512
COLS = 128
F32 = jnp.float32
BF16 = jnp.bfloat16
VMEM_LIMIT = 48 * 1024 * 1024
PARAMS = pltpu.CompilerParams(vmem_limit_bytes=VMEM_LIMIT)


def shift(x, axis, by):
    n = lax.axis_size(axis)
    return lax.ppermute(x, axis, [(i, (i + by) % n) for i in range(n)])


def after(x, *others):
    return lax.optimization_barrier((x, *others))[0]


def whole(shape):
    return pl.BlockSpec(shape, lambda *_: (0,) * len(shape))


def split_kernel(core_ref, in_ref, out_ref):
    exact = in_ref[...]
    high = exact.astype(BF16)
    out_ref[0, :, :COLS] = high
    out_ref[0, :, COLS:] = (exact - high.astype(F32)).astype(BF16)


def split_basis(core, basis):
    return pl.pallas_call(
        split_kernel,
        grid_spec=pltpu.PrefetchScalarGridSpec(
            num_scalar_prefetch=1,
            grid=(4,),
            in_specs=[pl.BlockSpec((1024, COLS), lambda g, core: (g * 2 + core[0], 0))],
            out_specs=pl.BlockSpec((1, 1024, 256), lambda g, core: (g, 0, 0)),
        ),
        out_shape=jax.ShapeDtypeStruct((4, 1024, 256), BF16),
        compiler_params=PARAMS,
        cost_estimate=pl.CostEstimate(
            flops=1 << 20, bytes_accessed=4 << 20, transcendentals=0
        ),
    )(core, basis)


def rotate_kernel(at_ref, block_ref, own_ref, other_ref, out_ref, lhs):
    @pl.when(pl.program_id(0) == 0)
    def _():
        turned = lax.rem(at_ref[1] + at_ref[4], 2)
        for z in range(8):
            for side in range(2):
                half = turned if side == 0 else 1 - turned
                at = pl.multiple_of((half * 8 + z) * COLS, COLS)
                lhs[:, pl.ds(at, COLS)] = block_ref[z, side]

    both = jnp.dot(lhs[:, :1024], own_ref[0], preferred_element_type=F32)
    both += jnp.dot(lhs[:, 1024:], other_ref[0], preferred_element_type=F32)
    out_ref[0] = (both[:, :COLS] + both[:, COLS:]).T


def rotate(at, blocks, own, other):
    slab = pl.BlockSpec((1, 1024, 256), lambda g: (g, 0, 0))
    return pl.pallas_call(
        rotate_kernel,
        grid=(4,),
        out_shape=jax.ShapeDtypeStruct((4, COLS, TOK), F32),
        in_specs=[pl.BlockSpec(memory_space=pltpu.SMEM), whole(blocks.shape), slab, slab],
        out_specs=pl.BlockSpec((1, COLS, TOK), lambda g: (g, 0, 0)),
        scratch_shapes=[pltpu.VMEM((TOK, 2048), BF16)],
        compiler_params=PARAMS,
        cost_estimate=pl.CostEstimate(
            flops=4 * TOK * 2048 * 512, bytes_accessed=7 << 20, transcendentals=0
        ),
    )(at, blocks, own, other)


def reach_kernel(rows_ref, in_ref, own_ref, near_ref, far_ref):
    def put(out_ref):
        exact = in_ref[...]
        high = exact.astype(BF16)
        out_ref[:, :COLS] = high
        out_ref[:, COLS:] = (exact - high.astype(F32)).astype(BF16)

    step = pl.program_id(0)
    pl.when(step < 2)(lambda: put(own_ref))
    pl.when((step >= 2) & (step < 4))(lambda: put(near_ref))
    pl.when(step == 4)(lambda: put(far_ref))


def reach_basis(rows, basis):
    return pl.pallas_call(
        reach_kernel,
        grid_spec=pltpu.PrefetchScalarGridSpec(
            num_scalar_prefetch=1,
            grid=(5,),
            in_specs=[pl.BlockSpec((1024, COLS), lambda g, rows: (rows[g], 0))],
            out_specs=[
                pl.BlockSpec((1024, 256), lambda g, rows: (jnp.minimum(g, 1), 0)),
                pl.BlockSpec((1024, 256), lambda g, rows: (jnp.clip(g - 2, 0, 1), 0)),
                pl.BlockSpec((1024, 256), lambda g, rows: (0, 0)),
            ],
        ),
        out_shape=[jax.ShapeDtypeStruct((n, 256), BF16) for n in (2048, 2048, 1024)],
        compiler_params=PARAMS,
        cost_estimate=pl.CostEstimate(
            flops=1 << 20, bytes_accessed=5 << 20, transcendentals=0
        ),
    )(rows, basis)


def rotate_ring_kernel(places, at_ref, *refs):
    blocks, refs = refs[: len(places)], refs[len(places) :]
    own_ref, near_ref, near_swapped, far_ref, far_swapped, out_ref, lhs = refs
    z, xh, y, c = at_ref[0], at_ref[1], at_ref[2], at_ref[4]
    for block, parts in zip(blocks, places):
        for i, (offset, side) in enumerate(parts):
            half = xh if side == 0 else 1 - xh
            at = (half * 8 + lax.rem(z + 8 + offset, 8)) * COLS
            lhs[:, pl.ds(pl.multiple_of(at, COLS), COLS)] = block[i]

    def put(place, both):
        out_ref[lax.rem(place, 4)] = (both[:, :COLS] + both[:, COLS:]).T

    for offset, ref in ((4, own_ref), (3 + 2 * c, near_ref), (5 - 2 * c, near_swapped)):
        put(y + offset, jnp.dot(lhs[...], ref[...], preferred_element_type=F32))
    mine = lhs[:, pl.ds(pl.multiple_of(c * 1024, 1024), 1024)]
    rest = lhs[:, pl.ds(pl.multiple_of((1 - c) * 1024, 1024), 1024)]
    both = jnp.dot(mine, far_ref[...], preferred_element_type=F32)
    put(y + 2, both + jnp.dot(rest, far_swapped[...], preferred_element_type=F32))


def rotate_ring(at, entries, slabs):
    blocks = [
        pl.BlockSpec((len(parts), *array.shape[1:]), lambda g, index=index: (index, 0, 0))
        for array, index, parts in entries
    ]
    return pl.pallas_call(
        functools.partial(rotate_ring_kernel, [parts for _, _, parts in entries]),
        grid=(1,),
        out_shape=jax.ShapeDtypeStruct((4, COLS, TOK), F32),
        in_specs=[pl.BlockSpec(memory_space=pltpu.SMEM)]
        + blocks
        + [whole(slab.shape) for slab in slabs],
        out_specs=whole((4, COLS, TOK)),
        scratch_shapes=[pltpu.VMEM((TOK, 2048), BF16)],
        compiler_params=PARAMS,
        cost_estimate=pl.CostEstimate(
            flops=4 * TOK * 2048 * 512, bytes_accessed=7 << 20, transcendentals=0
        ),
    )(at, *[array for array, _, _ in entries], *slabs)


def product_kernel(scale, at_ref, acts_ref, own_ref, other_ref, out_ref, right):
    xh, c = at_ref[1], at_ref[4]
    for z in range(8):
        for side in range(2):
            place = (xh if side == 0 else 1 - xh) * 8 + z
            for s in range(4):
                right[s, pl.ds(pl.multiple_of(place * 32, 32), 32), :] = acts_ref[z, side, s]
    for row in range(4):
        total = None
        for grads_ref, core in ((own_ref, c), (other_ref, 1 - c)):
            for side in range(2):
                part = lax.dot_general(
                    grads_ref[side, row],
                    right[side * 2 + core],
                    (((1,), (1,)), ((), ())),
                    preferred_element_type=F32,
                )
                total = part * part if total is None else total + part * part
        out_ref[row] = total * scale


def products(at, acts, own, other, scale):
    return pl.pallas_call(
        functools.partial(product_kernel, scale),
        out_shape=jax.ShapeDtypeStruct((4, COLS, 512), F32),
        in_specs=[pl.BlockSpec(memory_space=pltpu.SMEM)]
        + [pl.BlockSpec(memory_space=pltpu.VMEM)] * 3,
        out_specs=pl.BlockSpec(memory_space=pltpu.VMEM),
        scratch_shapes=[pltpu.VMEM((4, 512, TOK), BF16)],
        compiler_params=PARAMS,
        cost_estimate=pl.CostEstimate(
            flops=2 * 4 * 512 * 512 * TOK, bytes_accessed=5 << 20, transcendentals=0
        ),
    )(at, acts, own, other)


def weave_kernel(in_ref, out_ref):
    for tile in range(4):
        lanes = slice(tile * 32, tile * 32 + 32)
        out_ref[:, tile * COLS : (tile + 1) * COLS] = jnp.concatenate(
            [in_ref[q, :, lanes] for q in range(4)], axis=1
        )


def weave(parts):
    return pl.pallas_call(
        weave_kernel,
        grid=(4,),
        out_shape=jax.ShapeDtypeStruct((COLS, 2048), F32),
        in_specs=[pl.BlockSpec((4, COLS, 128), lambda g: (0, 0, g))],
        out_specs=pl.BlockSpec((COLS, 512), lambda g: (0, g)),
        compiler_params=PARAMS,
    )(parts)


def sync(*arrays):
    return lax.optimization_barrier(arrays)


def pair(x):
    return jnp.concatenate([x, shift(x, "xh", 1)])


def ring_step(up, down):
    return shift(up, "z", 1), shift(down, "z", -1)


def shift_near(x):
    pairs = [(i, (i + 1) % 4) for i in range(4)] + [(4 + i, 4 + (i + 3) % 4) for i in range(4)]
    return lax.ppermute(x, ("c", "y"), pairs)


def body(activations, gradients, basis_in, basis_out):
    z, xh, y, xl, c = (lax.axis_index(a) for a in ("z", "xh", "y", "xl", "c"))
    at = jnp.stack([z, xh, y, xl, c]).astype(jnp.int32)
    core = c.astype(jnp.int32).reshape(1)
    near_y, far_y = (y + 1 + 2 * c) % 4, (y + 2) % 4
    rows = jnp.stack(
        [y * 2, y * 2 + 1, near_y * 2, near_y * 2 + 1, far_y * 2 + c]
    ).astype(jnp.int32)

    acts_pair, g0, mine_in, basis_out = sync(
        pair(activations), pair(gradients), split_basis(core, basis_in), basis_out
    )
    own_in = lax.all_to_all(mine_in, "y", 0, 0)
    act_blocks = lax.all_gather(acts_pair, "z")
    own_out, near_out, far_out = reach_basis(rows, basis_out)
    up1, down1, near_out, far_out = sync(*ring_step(g0, g0), near_out, far_out)
    up2, down2, own_in, near_out, far_out = sync(*ring_step(up1, down1), own_in, near_out, far_out)
    up3, down3, other_in, near_out, far_out = sync(
        *ring_step(up2, down2), shift(own_in, "c", 1), shift_near(near_out), far_out
    )
    up4 = shift(up3, "z", 1)
    far_out = shift(far_out, "y", 2)
    near_out2 = shift(near_out, "c", 1)
    acts_part = rotate(at, act_blocks, own_in, other_in)
    acts_part, up4, far_out, near_out2 = sync(acts_part, up4, far_out, near_out2)
    acts_in = lax.all_to_all(acts_part.reshape(16, 32, TOK), ("xl", "c", "y"), 0, 0)

    ring = [(g0, 0), (up1, -1), (down1, 1), (up2, -2), (down2, 2), (up3, -3), (down3, 3), (up4, -4)]
    far_out2 = shift(far_out, "c", 1)
    grads_part = rotate_ring(
        at,
        [(a, 0, ((o, 0), (o, 1))) for a, o in ring],
        (own_out, near_out, near_out2, far_out, far_out2),
    )
    acts_in, grads_part = sync(acts_in, grads_part)
    grads_in = lax.all_to_all(grads_part, "y", 0, 0)

    acts = jnp.sum(acts_in.reshape(4, 4, 32, TOK), axis=1).astype(BF16)[None]
    rot_acts = lax.all_gather(pair(acts), "z")

    grads = jnp.sum(grads_in, axis=0).astype(BF16)
    copies = jnp.broadcast_to(grads, (8, COLS, TOK))
    rot_own = lax.all_to_all(copies, ("xl", "y"), 0, 0).reshape(2, 4, COLS, TOK)
    rot_other = shift(rot_own, "c", 1)

    part = products(at, rot_acts, rot_own, rot_other, 1.0 / (TOK * 4))
    return weave(lax.all_to_all(part, "y", 0, 0))


def solution(mesh):
    fine = Mesh(mesh.devices.reshape(SIZES), AXES)
    return jax.shard_map(
        body,
        mesh=fine,
        in_specs=(P(DP, None, TILE), P(DP, None, TILE), P(None, TILE), P(None, TILE)),
        out_specs=P(TILE, DP),
        check_vma=False,
    )
```

```python
import functools

import jax
import jax.numpy as jnp
from jax import lax
from jax.experimental import pallas as pl
from jax.experimental.pallas import tpu as pltpu
from jax.sharding import Mesh, PartitionSpec as P

AXES = ("xl", "c", "y", "xh", "z")
SIZES = (2, 2, 4, 2, 8)
DP = ("xl", "c")
TILE = ("y", "xh", "z")
TOK = 512
COLS = 128
F32 = jnp.float32
BF16 = jnp.bfloat16
VMEM_LIMIT = 48 * 1024 * 1024
PARAMS = pltpu.CompilerParams(vmem_limit_bytes=VMEM_LIMIT)


def shift(x, axis, by):
    n = lax.axis_size(axis)
    return lax.ppermute(x, axis, [(i, (i + by) % n) for i in range(n)])


def after(x, *others):
    return lax.optimization_barrier((x, *others))[0]


def whole(shape):
    return pl.BlockSpec(shape, lambda *_: (0,) * len(shape))


def split_kernel(core_ref, in_ref, out_ref, split_ref):
    def put(ref):
        exact = ref[...]
        high = exact.astype(BF16)
        split_ref[0, :, :COLS] = high
        split_ref[0, :, COLS:] = (exact - high.astype(F32)).astype(BF16)

    of_out = lax.rem(pl.program_id(0), 2)
    pl.when(of_out == 0)(lambda: put(in_ref))
    pl.when(of_out == 1)(lambda: put(out_ref))


def split_bases(core, basis_in, basis_out):
    rows = pl.BlockSpec((1024, COLS), lambda g, core: (g // 2 * 2 + core[0], 0))
    return pl.pallas_call(
        split_kernel,
        grid_spec=pltpu.PrefetchScalarGridSpec(
            num_scalar_prefetch=1,
            grid=(8,),
            in_specs=[rows, rows],
            out_specs=pl.BlockSpec((1, 1024, 256), lambda g, core: (g // 2, g % 2, 0)),
        ),
        out_shape=jax.ShapeDtypeStruct((4, 2048, 256), BF16),
        compiler_params=PARAMS,
        cost_estimate=pl.CostEstimate(
            flops=1 << 20, bytes_accessed=8 << 20, transcendentals=0
        ),
    )(core, basis_in, basis_out)


def rotate_kernel(places, at_ref, *refs):
    blocks, (own_ref, other_ref, out_ref, lhs) = refs[: len(places)], refs[len(places) :]

    @pl.when(pl.program_id(0) == 0)
    def _():
        z, xh, c = at_ref[0], at_ref[1], at_ref[4]
        turned = lax.rem(xh + c, 2)
        for block, parts in zip(blocks, places):
            for i, (offset, side) in enumerate(parts):
                half = turned if side == 0 else 1 - turned
                at = (half * 8 + lax.rem(z + 8 + offset, 8)) * COLS
                lhs[:, pl.ds(pl.multiple_of(at, COLS), COLS)] = block[i]

    both = jnp.dot(lhs[:, :1024], own_ref[0], preferred_element_type=F32)
    both += jnp.dot(lhs[:, 1024:], other_ref[0], preferred_element_type=F32)
    out_ref[0] = (both[:, :COLS] + both[:, COLS:]).T


def rotate(at, entries, own, other, which):
    slab = pl.BlockSpec((1, 1024, 256), lambda g: (g, which, 0))
    blocks = [
        pl.BlockSpec((len(parts), *array.shape[1:]), lambda g, index=index: (index, 0, 0))
        for array, index, parts in entries
    ]
    return pl.pallas_call(
        functools.partial(rotate_kernel, [parts for _, _, parts in entries]),
        grid=(4,),
        out_shape=jax.ShapeDtypeStruct((4, COLS, TOK), F32),
        in_specs=[pl.BlockSpec(memory_space=pltpu.SMEM)] + blocks + [slab, slab],
        out_specs=pl.BlockSpec((1, COLS, TOK), lambda g: (g, 0, 0)),
        scratch_shapes=[pltpu.VMEM((TOK, 2048), BF16)],
        compiler_params=PARAMS,
        cost_estimate=pl.CostEstimate(
            flops=4 * TOK * 2048 * 512, bytes_accessed=7 << 20, transcendentals=0
        ),
    )(at, *[array for array, _, _ in entries], own, other)


def product_kernel(scale, places, at_ref, *refs):
    n = len(places)
    acts, grads, out_ref, right = refs[:n], refs[n : n + 2], refs[n + 2], refs[n + 3]
    z, xh, y, xl, c = (at_ref[i] for i in range(5))
    for block, parts in zip(acts, places):
        for i, (offset, side) in enumerate(parts):
            place = (xh if side == 0 else 1 - xh) * 8 + lax.rem(z + 8 + offset, 8)
            for s in range(4):
                right[s, pl.ds(pl.multiple_of(place * 32, 32), 32), :] = block[i, s]
    for row in range(4):
        total = None
        for core in range(2):
            for side in range(2):
                s = side * 2 + (c if core == 0 else 1 - c)
                part = lax.dot_general(
                    grads[core][side, row],
                    right[s],
                    (((1,), (1,)), ((), ())),
                    preferred_element_type=F32,
                )
                total = part * part if total is None else total + part * part
        out_ref[row] = total * scale


def products(at, acts, places, grads, scale):
    return pl.pallas_call(
        functools.partial(product_kernel, scale, places),
        out_shape=jax.ShapeDtypeStruct((4, COLS, 512), F32),
        in_specs=[pl.BlockSpec(memory_space=pltpu.SMEM)]
        + [pl.BlockSpec(memory_space=pltpu.VMEM)] * (len(acts) + 2),
        out_specs=pl.BlockSpec(memory_space=pltpu.VMEM),
        scratch_shapes=[pltpu.VMEM((4, 512, TOK), BF16)],
        compiler_params=PARAMS,
        cost_estimate=pl.CostEstimate(
            flops=2 * 4 * 512 * 512 * TOK, bytes_accessed=5 << 20, transcendentals=0
        ),
    )(at, *acts, *grads)


def weave_kernel(in_ref, out_ref):
    for tile in range(4):
        lanes = slice(tile * 32, tile * 32 + 32)
        out_ref[:, tile * COLS : (tile + 1) * COLS] = jnp.concatenate(
            [in_ref[q, :, lanes] for q in range(4)], axis=1
        )


def weave(parts):
    return pl.pallas_call(
        weave_kernel,
        grid=(4,),
        out_shape=jax.ShapeDtypeStruct((COLS, 2048), F32),
        in_specs=[pl.BlockSpec((4, COLS, 128), lambda g: (0, 0, g))],
        out_specs=pl.BlockSpec((COLS, 512), lambda g: (0, g)),
        compiler_params=PARAMS,
    )(parts)


def sync(*arrays):
    return lax.optimization_barrier(arrays)


def ring_step(up, down):
    return shift(up, "z", 1), shift(down, "z", -1)


def pair(x):
    return jnp.concatenate([x, shift(x, "xh", 1)])


def body(activations, gradients, basis_in, basis_out):
    z, xh, y, xl, c = (lax.axis_index(a) for a in ("z", "xh", "y", "xl", "c"))
    at = jnp.stack([z, xh, y, xl, c]).astype(jnp.int32)
    core = c.astype(jnp.int32).reshape(1)

    acts_other, grads_other, mine = sync(
        shift(activations, "xh", 1),
        shift(gradients, "xh", 1),
        split_bases(core, basis_in, basis_out),
    )
    own = lax.all_to_all(mine, "y", 0, 0)
    base = jnp.concatenate([activations, acts_other, gradients, grads_other])
    up1, down1 = sync(*ring_step(base, base))
    up2, down2 = sync(*ring_step(up1, down1))
    up3, down3, own = sync(*ring_step(up2, down2), own)
    acts4, grads4, other = sync(shift(up3[:2], "z", 1), shift(down3[2:], "z", -1), shift(own, "c", 1))
    ring = [(base, 0), (up1, -1), (down1, 1), (up2, -2), (down2, 2), (up3, -3), (down3, 3)]

    acts_entries = [(a, 0, ((o, 0), (o, 1))) for a, o in ring + [(acts4, -4)]]
    acts_part = rotate(at, acts_entries, own, other, 0)
    acts_in = lax.all_to_all(acts_part.reshape(16, 32, TOK), ("xl", "c", "y"), 0, 0)
    grads_entries = [(a, 1, ((o, 0), (o, 1))) for a, o in ring] + [(grads4, 0, ((4, 0), (4, 1)))]
    grads_part = rotate(after(at, acts_part), grads_entries, own, other, 1)
    acts_in, grads_part = sync(acts_in, grads_part)
    grads_in = lax.all_to_all(grads_part, "y", 0, 0)

    acts = jnp.sum(acts_in.reshape(4, 4, 32, TOK), axis=1).astype(BF16)[None]
    r0 = pair(acts)
    r_up1, r_down1 = sync(*ring_step(r0, r0))
    r_up2, r_down2, grads_in = sync(*ring_step(r_up1, r_down1), grads_in)
    grads = jnp.sum(grads_in, axis=0).astype(BF16)
    copies = jnp.broadcast_to(grads, (8, COLS, TOK))
    rot_own = lax.all_to_all(copies, ("xl", "y"), 0, 0).reshape(2, 4, COLS, TOK)
    r_up3, r_down3, rot_own = sync(*ring_step(r_up2, r_down2), rot_own)
    r_up4 = shift(r_up3, "z", 1)
    rot_grads = [rot_own, shift(rot_own, "c", 1)]
    rot_acts = [r0, r_up1, r_down1, r_up2, r_down2, r_up3, r_down3, r_up4]
    rot_places = [((o, 0), (o, 1)) for _, o in ring] + [((-4, 0), (-4, 1))]

    part = products(at, rot_acts, rot_places, rot_grads, 1.0 / (TOK * 4))
    return weave(lax.all_to_all(part, "y", 0, 0))


def solution(mesh):
    fine = Mesh(mesh.devices.reshape(SIZES), AXES)
    return jax.shard_map(
        body,
        mesh=fine,
        in_specs=(P(DP, None, TILE), P(DP, None, TILE), P(None, TILE), P(None, TILE)),
        out_specs=P(TILE, DP),
        check_vma=False,
    )
```

```python
import functools

import jax
import jax.numpy as jnp
from jax import lax
from jax.experimental import pallas as pl
from jax.experimental.pallas import tpu as pltpu
from jax.sharding import Mesh, PartitionSpec as P

AXES = ("xl", "c", "y", "xh", "z")
SIZES = (2, 2, 4, 2, 8)
DP = ("xl", "c")
TILE = ("y", "xh", "z")
TOK = 512
COLS = 128
F32 = jnp.float32
BF16 = jnp.bfloat16
VMEM_LIMIT = 48 * 1024 * 1024
PARAMS = pltpu.CompilerParams(vmem_limit_bytes=VMEM_LIMIT)


def shift(x, axis, by):
    n = lax.axis_size(axis)
    return lax.ppermute(x, axis, [(i, (i + by) % n) for i in range(n)])


def after(x, *others):
    return lax.optimization_barrier((x, *others))[0]


def whole(shape):
    return pl.BlockSpec(shape, lambda *_: (0,) * len(shape))


def split_kernel(core_ref, in_ref, out_ref):
    exact = in_ref[...]
    high = exact.astype(BF16)
    out_ref[0, :, :COLS] = high
    out_ref[0, :, COLS:] = (exact - high.astype(F32)).astype(BF16)


def split_basis(core, basis):
    return pl.pallas_call(
        split_kernel,
        grid_spec=pltpu.PrefetchScalarGridSpec(
            num_scalar_prefetch=1,
            grid=(4,),
            in_specs=[pl.BlockSpec((1024, COLS), lambda g, core: (g * 2 + core[0], 0))],
            out_specs=pl.BlockSpec((1, 1024, 256), lambda g, core: (g, 0, 0)),
        ),
        out_shape=jax.ShapeDtypeStruct((4, 1024, 256), BF16),
        compiler_params=PARAMS,
        cost_estimate=pl.CostEstimate(
            flops=1 << 20, bytes_accessed=4 << 20, transcendentals=0
        ),
    )(core, basis)


def rotate_kernel(at_ref, block_ref, own_ref, other_ref, out_ref, lhs):
    @pl.when(pl.program_id(0) == 0)
    def _():
        turned = lax.rem(at_ref[1] + at_ref[4], 2)
        for z in range(8):
            for side in range(2):
                half = turned if side == 0 else 1 - turned
                at = pl.multiple_of((half * 8 + z) * COLS, COLS)
                lhs[:, pl.ds(at, COLS)] = block_ref[z, side]

    both = jnp.dot(lhs[:, :1024], own_ref[0], preferred_element_type=F32)
    both += jnp.dot(lhs[:, 1024:], other_ref[0], preferred_element_type=F32)
    out_ref[0] = (both[:, :COLS] + both[:, COLS:]).T


def rotate(at, blocks, own, other):
    slab = pl.BlockSpec((1, 1024, 256), lambda g: (g, 0, 0))
    return pl.pallas_call(
        rotate_kernel,
        grid=(4,),
        out_shape=jax.ShapeDtypeStruct((4, COLS, TOK), F32),
        in_specs=[pl.BlockSpec(memory_space=pltpu.SMEM), whole(blocks.shape), slab, slab],
        out_specs=pl.BlockSpec((1, COLS, TOK), lambda g: (g, 0, 0)),
        scratch_shapes=[pltpu.VMEM((TOK, 2048), BF16)],
        compiler_params=PARAMS,
        cost_estimate=pl.CostEstimate(
            flops=4 * TOK * 2048 * 512, bytes_accessed=7 << 20, transcendentals=0
        ),
    )(at, blocks, own, other)


def rotate_head_kernel(offsets, at_ref, *refs):
    blocks, (own_ref, other_ref, out_ref, lhs) = refs[: len(offsets)], refs[len(offsets) :]

    @pl.when(pl.program_id(0) == 0)
    def _():
        turned = lax.rem(at_ref[1] + at_ref[4], 2)
        for side in range(2):
            half = turned if side == 0 else 1 - turned
            for block, offset in zip(blocks, offsets):
                at = (half * 8 + lax.rem(at_ref[0] + 8 + offset, 8)) * COLS
                lhs[:, pl.ds(pl.multiple_of(at, COLS), COLS)] = block[side]
            at = (half * 8 + lax.rem(at_ref[0] + 4, 8)) * COLS
            lhs[:, pl.ds(pl.multiple_of(at, COLS), COLS)] = jnp.zeros((TOK, COLS), BF16)

    both = jnp.dot(lhs[:, :1024], own_ref[0], preferred_element_type=F32)
    both += jnp.dot(lhs[:, 1024:], other_ref[0], preferred_element_type=F32)
    out_ref[0] = (both[:, :COLS] + both[:, COLS:]).T


def rotate_head(at, ring, own, other):
    slab = pl.BlockSpec((1, 1024, 256), lambda g: (g, 0, 0))
    return pl.pallas_call(
        functools.partial(rotate_head_kernel, [offset for _, offset in ring]),
        grid=(4,),
        out_shape=jax.ShapeDtypeStruct((4, COLS, TOK), F32),
        in_specs=[pl.BlockSpec(memory_space=pltpu.SMEM)]
        + [whole((2, TOK, COLS))] * len(ring)
        + [slab, slab],
        out_specs=pl.BlockSpec((1, COLS, TOK), lambda g: (g, 0, 0)),
        scratch_shapes=[pltpu.VMEM((TOK, 2048), BF16)],
        compiler_params=PARAMS,
        cost_estimate=pl.CostEstimate(
            flops=4 * TOK * 2048 * 512, bytes_accessed=7 << 20, transcendentals=0
        ),
    )(at, *[block for block, _ in ring], own, other)


def rotate_tail_kernel(at_ref, head_ref, block_ref, own_ref, other_ref, out_ref, lhs):
    @pl.when(pl.program_id(0) == 0)
    def _():
        turned = lax.rem(at_ref[1] + at_ref[4], 2)
        for side in range(2):
            half = turned if side == 0 else 1 - turned
            lhs[:, pl.ds(pl.multiple_of(half * COLS, COLS), COLS)] = block_ref[side]

    both = jnp.dot(lhs[:, :COLS], own_ref[0], preferred_element_type=F32)
    both += jnp.dot(lhs[:, COLS:], other_ref[0], preferred_element_type=F32)
    out_ref[0] = head_ref[0] + (both[:, :COLS] + both[:, COLS:]).T


def rotate_tail(at, head, block, own, other):
    slab = pl.BlockSpec((1, COLS, 256), lambda g, at: (g, (at[0] + 4) % 8, 0))
    part = pl.BlockSpec((1, COLS, TOK), lambda g, at: (g, 0, 0))
    return pl.pallas_call(
        rotate_tail_kernel,
        grid_spec=pltpu.PrefetchScalarGridSpec(
            num_scalar_prefetch=1,
            grid=(4,),
            in_specs=[part, whole((2, TOK, COLS)), slab, slab],
            out_specs=part,
            scratch_shapes=[pltpu.VMEM((TOK, 256), BF16)],
        ),
        out_shape=jax.ShapeDtypeStruct((4, COLS, TOK), F32),
        compiler_params=PARAMS,
        cost_estimate=pl.CostEstimate(
            flops=4 * TOK * 256 * 512, bytes_accessed=3 << 20, transcendentals=0
        ),
    )(at, head, block, own, other)


def product_kernel(scale, at_ref, acts_ref, own_ref, other_ref, out_ref, right):
    xh, c = at_ref[1], at_ref[4]
    for z in range(8):
        for side in range(2):
            place = (xh if side == 0 else 1 - xh) * 8 + z
            for s in range(4):
                right[s, pl.ds(pl.multiple_of(place * 32, 32), 32), :] = acts_ref[z, side, s]
    for row in range(4):
        total = None
        for grads_ref, core in ((own_ref, c), (other_ref, 1 - c)):
            for side in range(2):
                part = lax.dot_general(
                    grads_ref[side, row],
                    right[side * 2 + core],
                    (((1,), (1,)), ((), ())),
                    preferred_element_type=F32,
                )
                total = part * part if total is None else total + part * part
        out_ref[row] = total * scale


def products(at, acts, own, other, scale):
    return pl.pallas_call(
        functools.partial(product_kernel, scale),
        out_shape=jax.ShapeDtypeStruct((4, COLS, 512), F32),
        in_specs=[pl.BlockSpec(memory_space=pltpu.SMEM)]
        + [pl.BlockSpec(memory_space=pltpu.VMEM)] * 3,
        out_specs=pl.BlockSpec(memory_space=pltpu.VMEM),
        scratch_shapes=[pltpu.VMEM((4, 512, TOK), BF16)],
        compiler_params=PARAMS,
        cost_estimate=pl.CostEstimate(
            flops=2 * 4 * 512 * 512 * TOK, bytes_accessed=5 << 20, transcendentals=0
        ),
    )(at, acts, own, other)


def weave_kernel(in_ref, out_ref):
    for tile in range(4):
        lanes = slice(tile * 32, tile * 32 + 32)
        out_ref[:, tile * COLS : (tile + 1) * COLS] = jnp.concatenate(
            [in_ref[q, :, lanes] for q in range(4)], axis=1
        )


def weave(parts):
    return pl.pallas_call(
        weave_kernel,
        grid=(4,),
        out_shape=jax.ShapeDtypeStruct((COLS, 2048), F32),
        in_specs=[pl.BlockSpec((4, COLS, 128), lambda g: (0, 0, g))],
        out_specs=pl.BlockSpec((COLS, 512), lambda g: (0, g)),
        compiler_params=PARAMS,
    )(parts)


def sync(*arrays):
    return lax.optimization_barrier(arrays)


def pair(x):
    return jnp.concatenate([x, shift(x, "xh", 1)])


def ring_step(up, down):
    return shift(up, "z", 1), shift(down, "z", -1)


def body(activations, gradients, basis_in, basis_out):
    z, xh, y, xl, c = (lax.axis_index(a) for a in ("z", "xh", "y", "xl", "c"))
    at = jnp.stack([z, xh, y, xl, c]).astype(jnp.int32)
    core = c.astype(jnp.int32).reshape(1)

    a0, grads_pair, mine_in, basis_out = sync(
        pair(activations), pair(gradients), split_basis(core, basis_in), basis_out
    )
    own_in = lax.all_to_all(mine_in, "y", 0, 0)
    grad_blocks = lax.all_gather(grads_pair, "z")
    up1, down1, mine_out = sync(*ring_step(a0, a0), split_basis(core, basis_out))
    up2, down2, own_in, mine_out = sync(*ring_step(up1, down1), own_in, mine_out)
    own_out = lax.all_to_all(mine_out, "y", 0, 0)
    up3, down3, other_in = sync(*ring_step(up2, down2), shift(own_in, "c", 1))
    ring = [(a0, 0), (up1, -1), (down1, 1), (up2, -2), (down2, 2), (up3, -3), (down3, 3)]
    up4, head, grad_blocks = sync(
        shift(up3, "z", 1), rotate_head(at, ring, own_in, other_in), grad_blocks
    )
    acts_part = rotate_tail(at, head, up4, own_in, other_in)
    acts_in = lax.all_to_all(acts_part.reshape(16, 32, TOK), ("xl", "c", "y"), 0, 0)

    other_out = shift(after(own_out, acts_part), "c", 1)
    grads_part = rotate(at, grad_blocks, own_out, other_out)
    acts_in, grads_part = sync(acts_in, grads_part)
    grads_in = lax.all_to_all(grads_part, "y", 0, 0)

    acts = jnp.sum(acts_in.reshape(4, 4, 32, TOK), axis=1).astype(BF16)[None]
    rot_acts = lax.all_gather(pair(acts), "z")

    grads = jnp.sum(grads_in, axis=0).astype(BF16)
    copies = jnp.broadcast_to(grads, (8, COLS, TOK))
    rot_own = lax.all_to_all(copies, ("xl", "y"), 0, 0).reshape(2, 4, COLS, TOK)
    rot_other = shift(rot_own, "c", 1)

    part = products(at, rot_acts, rot_own, rot_other, 1.0 / (TOK * 4))
    return weave(lax.all_to_all(part, "y", 0, 0))


def solution(mesh):
    fine = Mesh(mesh.devices.reshape(SIZES), AXES)
    return jax.shard_map(
        body,
        mesh=fine,
        in_specs=(P(DP, None, TILE), P(DP, None, TILE), P(None, TILE), P(None, TILE)),
        out_specs=P(TILE, DP),
        check_vma=False,
    )
```

```python
import functools

import jax
import jax.numpy as jnp
from jax import lax
from jax.experimental import pallas as pl
from jax.experimental.pallas import tpu as pltpu
from jax.sharding import Mesh, PartitionSpec as P

AXES = ("xl", "c", "y", "xh", "z")
SIZES = (2, 2, 4, 2, 8)
DP = ("xl", "c")
TILE = ("y", "xh", "z")
TOK = 512
COLS = 128
F32 = jnp.float32
BF16 = jnp.bfloat16
VMEM_LIMIT = 58 * 1024 * 1024
PARAMS = pltpu.CompilerParams(vmem_limit_bytes=VMEM_LIMIT)


def shift(x, axis, by):
    n = lax.axis_size(axis)
    return lax.ppermute(x, axis, [(i, (i + by) % n) for i in range(n)])


def after(x, *others):
    return lax.optimization_barrier((x, *others))[0]


def whole(shape):
    return pl.BlockSpec(shape, lambda *_: (0,) * len(shape))


def split_kernel(core_ref, in_ref, out_ref):
    exact = in_ref[...]
    high = exact.astype(BF16)
    out_ref[0, :, :COLS] = high
    out_ref[0, :, COLS:] = (exact - high.astype(F32)).astype(BF16)


def split_basis(share, count, basis):
    rows = 2048 // count
    return pl.pallas_call(
        split_kernel,
        grid_spec=pltpu.PrefetchScalarGridSpec(
            num_scalar_prefetch=1,
            grid=(4,),
            in_specs=[pl.BlockSpec((rows, COLS), lambda g, share: (g * count + share[0], 0))],
            out_specs=pl.BlockSpec((1, rows, 256), lambda g, share: (g, 0, 0)),
        ),
        out_shape=jax.ShapeDtypeStruct((4, rows, 256), BF16),
        compiler_params=PARAMS,
        cost_estimate=pl.CostEstimate(
            flops=1 << 20, bytes_accessed=4 << 20, transcendentals=0
        ),
    )(share, basis)


def rotate_ring_kernel(offsets, at_ref, *refs):
    blocks, (own_ref, other_ref, out_ref, lhs, sems) = refs[: len(offsets)], refs[len(offsets) :]

    @pl.when(pl.program_id(0) == 0)
    def _():
        turned = lax.rem(at_ref[1] + at_ref[4], 2)
        copies = []
        for i, (block, offset) in enumerate(zip(blocks, offsets)):
            for side in range(2):
                half = turned if side == 0 else 1 - turned
                at = (half * 8 + lax.rem(at_ref[0] + 8 + offset, 8)) * COLS
                lanes = pl.ds(pl.multiple_of(at, COLS), COLS)
                copies.append(
                    pltpu.make_async_copy(block.at[side], lhs.at[:, lanes], sems.at[i * 2 + side])
                )
        for copy in copies:
            copy.start()
        for copy in copies:
            copy.wait()

    both = jnp.dot(lhs[:, :1024], own_ref[0], preferred_element_type=F32)
    both += jnp.dot(lhs[:, 1024:], other_ref[0], preferred_element_type=F32)
    out_ref[0] = (both[:, :COLS] + both[:, COLS:]).T


def rotate_ring(at, ring, own, other):
    slab = pl.BlockSpec((1, 1024, 256), lambda g: (g, 0, 0))
    return pl.pallas_call(
        functools.partial(rotate_ring_kernel, [offset for _, offset in ring]),
        grid=(4,),
        out_shape=jax.ShapeDtypeStruct((4, COLS, TOK), F32),
        in_specs=[pl.BlockSpec(memory_space=pltpu.SMEM)]
        + [pl.BlockSpec(memory_space=pltpu.HBM)] * len(ring)
        + [slab, slab],
        out_specs=pl.BlockSpec((1, COLS, TOK), lambda g: (g, 0, 0)),
        scratch_shapes=[pltpu.VMEM((TOK, 2048), BF16), pltpu.SemaphoreType.DMA((16,))],
        compiler_params=PARAMS,
        cost_estimate=pl.CostEstimate(
            flops=4 * TOK * 2048 * 512, bytes_accessed=7 << 20, transcendentals=0
        ),
    )(at, *[block for block, _ in ring], own, other)


def rotate_kernel(at_ref, block_ref, *refs):
    slabs, (out_ref, lhs, sems) = refs[:4], refs[4:]
    xh, xl, c = at_ref[1], at_ref[3], at_ref[4]

    @pl.when(pl.program_id(0) == 0)
    def _():
        copies = []
        for z in range(8):
            for side in range(2):
                at = ((xh if side == 0 else 1 - xh) * 8 + z) * COLS
                lanes = pl.ds(pl.multiple_of(at, COLS), COLS)
                copies.append(
                    pltpu.make_async_copy(block_ref.at[z, side], lhs.at[:, lanes], sems.at[z * 2 + side])
                )
        for copy in copies:
            copy.start()
        for copy in copies:
            copy.wait()

    both = None
    for i, slab_ref in enumerate(slabs):
        quarter = (c if i < 2 else 1 - c) * 2 + (xl if i % 2 == 0 else 1 - xl)
        lanes = pl.ds(pl.multiple_of(quarter * 512, 512), 512)
        part = jnp.dot(lhs[:, lanes], slab_ref[0], preferred_element_type=F32)
        both = part if both is None else both + part
    out_ref[0] = (both[:, :COLS] + both[:, COLS:]).T


def rotate(at, blocks, slabs):
    slab = pl.BlockSpec((1, 512, 256), lambda g: (g, 0, 0))
    return pl.pallas_call(
        rotate_kernel,
        grid=(4,),
        out_shape=jax.ShapeDtypeStruct((4, COLS, TOK), F32),
        in_specs=[pl.BlockSpec(memory_space=pltpu.SMEM), pl.BlockSpec(memory_space=pltpu.HBM)]
        + [slab] * 4,
        out_specs=pl.BlockSpec((1, COLS, TOK), lambda g: (g, 0, 0)),
        scratch_shapes=[pltpu.VMEM((TOK, 2048), BF16), pltpu.SemaphoreType.DMA((16,))],
        compiler_params=PARAMS,
        cost_estimate=pl.CostEstimate(
            flops=4 * TOK * 2048 * 512, bytes_accessed=7 << 20, transcendentals=0
        ),
    )(at, blocks, *slabs)


def product_kernel(scale, at_ref, acts_ref, own_ref, other_ref, out_ref, right, sems):
    xh, c = at_ref[1], at_ref[4]
    copies = []
    for z in range(8):
        for side in range(2):
            place = (xh if side == 0 else 1 - xh) * 8 + z
            rows = pl.ds(pl.multiple_of(place * 32, 32), 32)
            copies.append(
                pltpu.make_async_copy(acts_ref.at[z, side], right.at[:, rows], sems.at[z * 2 + side])
            )
    for copy in copies:
        copy.start()
    for copy in copies:
        copy.wait()
    for row in range(4):
        total = None
        for grads_ref, core in ((own_ref, c), (other_ref, 1 - c)):
            for side in range(2):
                part = lax.dot_general(
                    grads_ref[side, row],
                    right[side * 2 + core],
                    (((1,), (1,)), ((), ())),
                    preferred_element_type=F32,
                )
                total = part * part if total is None else total + part * part
        out_ref[row] = total * scale


def products(at, acts, own, other, scale):
    return pl.pallas_call(
        functools.partial(product_kernel, scale),
        out_shape=jax.ShapeDtypeStruct((4, COLS, 512), F32),
        in_specs=[pl.BlockSpec(memory_space=pltpu.SMEM), pl.BlockSpec(memory_space=pltpu.HBM)]
        + [pl.BlockSpec(memory_space=pltpu.VMEM)] * 2,
        out_specs=pl.BlockSpec(memory_space=pltpu.VMEM),
        scratch_shapes=[pltpu.VMEM((4, 512, TOK), BF16), pltpu.SemaphoreType.DMA((16,))],
        compiler_params=PARAMS,
        cost_estimate=pl.CostEstimate(
            flops=2 * 4 * 512 * 512 * TOK, bytes_accessed=5 << 20, transcendentals=0
        ),
    )(at, acts, own, other)


def weave_kernel(in_ref, out_ref):
    for tile in range(4):
        lanes = slice(tile * 32, tile * 32 + 32)
        out_ref[:, tile * COLS : (tile + 1) * COLS] = jnp.concatenate(
            [in_ref[q, :, lanes] for q in range(4)], axis=1
        )


def weave(parts):
    return pl.pallas_call(
        weave_kernel,
        grid=(4,),
        out_shape=jax.ShapeDtypeStruct((COLS, 2048), F32),
        in_specs=[pl.BlockSpec((4, COLS, 128), lambda g: (0, 0, g))],
        out_specs=pl.BlockSpec((COLS, 512), lambda g: (0, g)),
        compiler_params=PARAMS,
    )(parts)


def sync(*arrays):
    return lax.optimization_barrier(arrays)


def pair(x):
    return jnp.concatenate([x, shift(x, "xh", 1)])


def ring_step(up, down):
    return shift(up, "z", 1), shift(down, "z", -1)


def body(activations, gradients, basis_in, basis_out):
    z, xh, y, xl, c = (lax.axis_index(a) for a in ("z", "xh", "y", "xl", "c"))
    at = jnp.stack([z, xh, y, xl, c]).astype(jnp.int32)
    half = c.astype(jnp.int32).reshape(1)
    quarter = (c * 2 + xl).astype(jnp.int32).reshape(1)

    a0, grads_pair, mine_in, basis_out = sync(
        pair(activations), pair(gradients), split_basis(half, 2, basis_in), basis_out
    )
    own_in = lax.all_to_all(mine_in, "y", 0, 0)
    up1, down1, mine_out = sync(*ring_step(a0, a0), split_basis(quarter, 4, basis_out))
    up2, down2, mine_out = sync(*ring_step(up1, down1), mine_out)
    up3, down3, own_in, mine_out = sync(*ring_step(up2, down2), own_in, mine_out)
    own_out = lax.all_to_all(mine_out, "y", 0, 0)
    grad_blocks = lax.all_gather(after(grads_pair, up2), "z")
    up4, other_in = sync(shift(up3, "z", 1), shift(own_in, "c", 1))
    ring = [(a0, 0), (up1, -1), (down1, 1), (up2, -2), (down2, 2), (up3, -3), (down3, 3), (up4, -4)]
    acts_part = rotate_ring(at, ring, own_in, other_in)
    acts_in = lax.all_to_all(acts_part.reshape(16, 32, TOK), ("xl", "c", "y"), 0, 0)

    own_out = after(own_out, acts_part)
    beside_out = shift(own_out, "xl", 1)
    others = shift(own_out, "c", 1), shift(beside_out, "c", 1)
    grads_part = rotate(at, grad_blocks, (own_out, beside_out, *others))
    acts_in, grads_part = sync(acts_in, grads_part)
    grads_in = lax.all_to_all(grads_part, "y", 0, 0)

    acts = jnp.sum(acts_in.reshape(4, 4, 32, TOK), axis=1).astype(BF16)[None]
    rot_acts = lax.all_gather(pair(acts), "z")

    grads = jnp.sum(grads_in, axis=0).astype(BF16)
    copies = jnp.broadcast_to(grads, (8, COLS, TOK))
    rot_own = lax.all_to_all(copies, ("xl", "y"), 0, 0).reshape(2, 4, COLS, TOK)
    rot_other = shift(rot_own, "c", 1)

    part = products(at, rot_acts, rot_own, rot_other, 1.0 / (TOK * 4))
    return weave(lax.all_to_all(part, "y", 0, 0))


def solution(mesh):
    fine = Mesh(mesh.devices.reshape(SIZES), AXES)
    return jax.shard_map(
        body,
        mesh=fine,
        in_specs=(P(DP, None, TILE), P(DP, None, TILE), P(None, TILE), P(None, TILE)),
        out_specs=P(TILE, DP),
        check_vma=False,
    )
```

```python
import functools

import jax
import jax.numpy as jnp
from jax import lax
from jax.experimental import pallas as pl
from jax.experimental.pallas import tpu as pltpu
from jax.sharding import Mesh, PartitionSpec as P

AXES = ("xl", "c", "y", "xh", "z")
SIZES = (2, 2, 4, 2, 8)
DP = ("xl", "c")
TILE = ("y", "xh", "z")
TOK = 512
COLS = 128
F32 = jnp.float32
BF16 = jnp.bfloat16
ALL_VMEM = pltpu.CompilerParams(vmem_limit_bytes=58 * 1024 * 1024)
PARAMS = pltpu.CompilerParams(vmem_limit_bytes=48 * 1024 * 1024)


def shift(x, axis, by):
    n = lax.axis_size(axis)
    return lax.ppermute(x, axis, [(i, (i + by) % n) for i in range(n)])


def after(x, *others):
    return lax.optimization_barrier((x, *others))[0]


def whole(shape):
    return pl.BlockSpec(shape, lambda *_: (0,) * len(shape))


def split_kernel(half_ref, in_ref, out_ref):
    exact = in_ref[...]
    high = exact.astype(BF16)
    out_ref[0, :, :COLS] = high
    out_ref[0, :, COLS:] = (exact - high.astype(F32)).astype(BF16)


def split_basis(half, basis):
    rows = 1024
    return pl.pallas_call(
        split_kernel,
        grid_spec=pltpu.PrefetchScalarGridSpec(
            num_scalar_prefetch=1,
            grid=(4,),
            in_specs=[pl.BlockSpec((rows, COLS), lambda g, half: (g * 2 + half[0], 0))],
            out_specs=pl.BlockSpec((1, rows, 256), lambda g, half: (g, 0, 0)),
        ),
        out_shape=jax.ShapeDtypeStruct((4, rows, 256), BF16),
        compiler_params=ALL_VMEM,
        cost_estimate=pl.CostEstimate(
            flops=1 << 20, bytes_accessed=4 << 20, transcendentals=0
        ),
    )(half, basis)


def rotate_ring_kernel(offsets, at_ref, *refs):
    blocks, (own_ref, other_ref, out_ref, lhs, sems) = refs[: len(offsets)], refs[len(offsets) :]

    @pl.when(pl.program_id(0) == 0)
    def _():
        turned = lax.rem(at_ref[1] + at_ref[4], 2)
        copies = []
        for i, (block, offset) in enumerate(zip(blocks, offsets)):
            for side in range(2):
                half = turned if side == 0 else 1 - turned
                at = (half * 8 + lax.rem(at_ref[0] + 8 + offset, 8)) * COLS
                lanes = pl.ds(pl.multiple_of(at, COLS), COLS)
                copies.append(
                    pltpu.make_async_copy(block.at[side], lhs.at[:, lanes], sems.at[i * 2 + side])
                )
        for copy in copies:
            copy.start()
        for copy in copies:
            copy.wait()

    both = jnp.dot(lhs[:, :1024], own_ref[0], preferred_element_type=F32)
    both += jnp.dot(lhs[:, 1024:], other_ref[0], preferred_element_type=F32)
    out_ref[0] = (both[:, :COLS] + both[:, COLS:]).T


def rotate_ring(at, ring, own, other):
    slab = pl.BlockSpec((1, 1024, 256), lambda g: (g, 0, 0))
    return pl.pallas_call(
        functools.partial(rotate_ring_kernel, [offset for _, offset in ring]),
        grid=(4,),
        out_shape=jax.ShapeDtypeStruct((4, COLS, TOK), F32),
        in_specs=[pl.BlockSpec(memory_space=pltpu.SMEM)]
        + [pl.BlockSpec(memory_space=pltpu.HBM)] * len(ring)
        + [slab, slab],
        out_specs=pl.BlockSpec((1, COLS, TOK), lambda g: (g, 0, 0)),
        scratch_shapes=[pltpu.VMEM((TOK, 2048), BF16), pltpu.SemaphoreType.DMA((16,))],
        compiler_params=ALL_VMEM,
        cost_estimate=pl.CostEstimate(
            flops=4 * TOK * 2048 * 512, bytes_accessed=7 << 20, transcendentals=0
        ),
    )(at, *[block for block, _ in ring], own, other)


def rotate_kernel(at_ref, block_ref, own_ref, other_ref, out_ref, lhs, sems):
    turned = lax.rem(at_ref[1] + at_ref[4], 2)

    @pl.when(pl.program_id(0) == 0)
    def _():
        copies = []
        for z in range(8):
            for side in range(2):
                at = ((turned if side == 0 else 1 - turned) * 8 + z) * COLS
                lanes = pl.ds(pl.multiple_of(at, COLS), COLS)
                copies.append(
                    pltpu.make_async_copy(block_ref.at[z, side], lhs.at[:, lanes], sems.at[z * 2 + side])
                )
        for copy in copies:
            copy.start()
        for copy in copies:
            copy.wait()

    both = jnp.dot(lhs[:, :1024], own_ref[0], preferred_element_type=F32)
    both += jnp.dot(lhs[:, 1024:], other_ref[0], preferred_element_type=F32)
    out_ref[0] = (both[:, :COLS] + both[:, COLS:]).T


def rotate(at, blocks, own, other):
    slab = pl.BlockSpec((1, 1024, 256), lambda g: (g, 0, 0))
    return pl.pallas_call(
        rotate_kernel,
        grid=(4,),
        out_shape=jax.ShapeDtypeStruct((4, COLS, TOK), F32),
        in_specs=[pl.BlockSpec(memory_space=pltpu.SMEM), pl.BlockSpec(memory_space=pltpu.HBM)]
        + [slab] * 2,
        out_specs=pl.BlockSpec((1, COLS, TOK), lambda g: (g, 0, 0)),
        scratch_shapes=[pltpu.VMEM((TOK, 2048), BF16), pltpu.SemaphoreType.DMA((16,))],
        compiler_params=ALL_VMEM,
        cost_estimate=pl.CostEstimate(
            flops=4 * TOK * 2048 * 512, bytes_accessed=7 << 20, transcendentals=0
        ),
    )(at, blocks, own, other)


def product_kernel(scale, at_ref, acts_ref, own_ref, other_ref, out_ref, right):
    xh, c = at_ref[1], at_ref[4]
    for z in range(8):
        for side in range(2):
            place = (xh if side == 0 else 1 - xh) * 8 + z
            for s in range(4):
                right[s, pl.ds(pl.multiple_of(place * 32, 32), 32), :] = acts_ref[z, side, s]
    for row in range(4):
        total = None
        for grads_ref, core in ((own_ref, c), (other_ref, 1 - c)):
            for side in range(2):
                part = lax.dot_general(
                    grads_ref[side, row],
                    right[side * 2 + core],
                    (((1,), (1,)), ((), ())),
                    preferred_element_type=F32,
                )
                total = part * part if total is None else total + part * part
        out_ref[row] = total * scale


def products(at, acts, own, other, scale):
    return pl.pallas_call(
        functools.partial(product_kernel, scale),
        out_shape=jax.ShapeDtypeStruct((4, COLS, 512), F32),
        in_specs=[pl.BlockSpec(memory_space=pltpu.SMEM)]
        + [pl.BlockSpec(memory_space=pltpu.VMEM)] * 3,
        out_specs=pl.BlockSpec(memory_space=pltpu.VMEM),
        scratch_shapes=[pltpu.VMEM((4, 512, TOK), BF16)],
        compiler_params=PARAMS,
        cost_estimate=pl.CostEstimate(
            flops=2 * 4 * 512 * 512 * TOK, bytes_accessed=5 << 20, transcendentals=0
        ),
    )(at, acts, own, other)


def weave_kernel(in_ref, out_ref):
    for tile in range(4):
        lanes = slice(tile * 32, tile * 32 + 32)
        out_ref[:, tile * COLS : (tile + 1) * COLS] = jnp.concatenate(
            [in_ref[q, :, lanes] for q in range(4)], axis=1
        )


def weave(parts):
    return pl.pallas_call(
        weave_kernel,
        grid=(4,),
        out_shape=jax.ShapeDtypeStruct((COLS, 2048), F32),
        in_specs=[pl.BlockSpec((4, COLS, 128), lambda g: (0, 0, g))],
        out_specs=pl.BlockSpec((COLS, 512), lambda g: (0, g)),
        compiler_params=PARAMS,
    )(parts)


def sync(*arrays):
    return lax.optimization_barrier(arrays)


def pair(x):
    return jnp.concatenate([x, shift(x, "xh", 1)])


def ring_step(up, down):
    return shift(up, "z", 1), shift(down, "z", -1)


def body(activations, gradients, basis_in, basis_out):
    z, xh, y, xl, c = (lax.axis_index(a) for a in ("z", "xh", "y", "xl", "c"))
    at = jnp.stack([z, xh, y, xl, c]).astype(jnp.int32)
    half = c.astype(jnp.int32).reshape(1)

    a0, grads_pair, mine_in, basis_out = sync(
        pair(activations), pair(gradients), split_basis(half, basis_in), basis_out
    )
    own_in = lax.all_to_all(mine_in, "y", 0, 0)
    up1, down1, mine_out = sync(*ring_step(a0, a0), split_basis(half, basis_out))
    up2, down2, mine_out = sync(*ring_step(up1, down1), mine_out)
    up3, down3, own_in, mine_out = sync(*ring_step(up2, down2), own_in, mine_out)
    own_out = lax.all_to_all(mine_out, "y", 0, 0)
    grad_blocks = lax.all_gather(after(grads_pair, up2), "z")
    up4, other_in = sync(shift(up3, "z", 1), shift(own_in, "c", 1))
    ring = [(a0, 0), (up1, -1), (down1, 1), (up2, -2), (down2, 2), (up3, -3), (down3, 3), (up4, -4)]
    acts_part = rotate_ring(at, ring, own_in, other_in)
    acts_in = lax.all_to_all(acts_part.reshape(16, 32, TOK), ("xl", "c", "y"), 0, 0)

    other_out = shift(after(own_out, acts_part), "c", 1)
    grads_part = rotate(at, grad_blocks, own_out, other_out)
    acts_in, grads_part = sync(acts_in, grads_part)
    grads_in = lax.all_to_all(grads_part, "y", 0, 0)

    acts = jnp.sum(acts_in.reshape(4, 4, 32, TOK), axis=1).astype(BF16)[None]
    rot_acts = lax.all_gather(pair(acts), "z")

    grads = jnp.sum(grads_in, axis=0).astype(BF16)
    copies = jnp.broadcast_to(grads, (8, COLS, TOK))
    rot_own = lax.all_to_all(copies, ("xl", "y"), 0, 0).reshape(2, 4, COLS, TOK)
    rot_other = shift(rot_own, "c", 1)

    part = products(at, rot_acts, rot_own, rot_other, 1.0 / (TOK * 4))
    return weave(lax.all_to_all(part, "y", 0, 0))


def solution(mesh):
    fine = Mesh(mesh.devices.reshape(SIZES), AXES)
    return jax.shard_map(
        body,
        mesh=fine,
        in_specs=(P(DP, None, TILE), P(DP, None, TILE), P(None, TILE), P(None, TILE)),
        out_specs=P(TILE, DP),
        check_vma=False,
    )
```

```python
import functools

import jax
import jax.numpy as jnp
from jax import lax
from jax.experimental import pallas as pl
from jax.experimental.pallas import tpu as pltpu
from jax.sharding import Mesh, PartitionSpec as P

AXES = ("xl", "c", "y", "xh", "z")
SIZES = (2, 2, 4, 2, 8)
DP = ("xl", "c")
TILE = ("y", "xh", "z")
TOK = 512
COLS = 128
F32 = jnp.float32
BF16 = jnp.bfloat16
ALL_VMEM = pltpu.CompilerParams(vmem_limit_bytes=58 * 1024 * 1024)
PARAMS = pltpu.CompilerParams(vmem_limit_bytes=48 * 1024 * 1024)


def shift(x, axis, by):
    n = lax.axis_size(axis)
    return lax.ppermute(x, axis, [(i, (i + by) % n) for i in range(n)])


def after(x, *others):
    return lax.optimization_barrier((x, *others))[0]


def whole(shape):
    return pl.BlockSpec(shape, lambda *_: (0,) * len(shape))


def split_kernel(half_ref, in_ref, out_ref):
    exact = in_ref[...]
    high = exact.astype(BF16)
    out_ref[0, :, :COLS] = high
    out_ref[0, :, COLS:] = (exact - high.astype(F32)).astype(BF16)


def split_basis(half, basis):
    rows = 1024
    return pl.pallas_call(
        split_kernel,
        grid_spec=pltpu.PrefetchScalarGridSpec(
            num_scalar_prefetch=1,
            grid=(4,),
            in_specs=[pl.BlockSpec((rows, COLS), lambda g, half: (g * 2 + half[0], 0))],
            out_specs=pl.BlockSpec((1, rows, 256), lambda g, half: (g, 0, 0)),
        ),
        out_shape=jax.ShapeDtypeStruct((4, rows, 256), BF16),
        compiler_params=ALL_VMEM,
        cost_estimate=pl.CostEstimate(
            flops=1 << 20, bytes_accessed=4 << 20, transcendentals=0
        ),
    )(half, basis)


def rotate_ring_kernel(offsets, at_ref, *refs):
    blocks, (own_ref, other_ref, out_ref, lhs, sems) = refs[: len(offsets)], refs[len(offsets) :]

    @pl.when(pl.program_id(0) == 0)
    def _():
        turned = lax.rem(at_ref[1] + at_ref[4], 2)
        copies = []
        for i, (block, offset) in enumerate(zip(blocks, offsets)):
            for side in range(2):
                half = turned if side == 0 else 1 - turned
                at = (half * 8 + lax.rem(at_ref[0] + 8 + offset, 8)) * COLS
                lanes = pl.ds(pl.multiple_of(at, COLS), COLS)
                copies.append(
                    pltpu.make_async_copy(block.at[side], lhs.at[:, lanes], sems.at[i * 2 + side])
                )
        for copy in copies:
            copy.start()
        for copy in copies:
            copy.wait()

    both = jnp.dot(lhs[:, :1024], own_ref[0], preferred_element_type=F32)
    both += jnp.dot(lhs[:, 1024:], other_ref[0], preferred_element_type=F32)
    out_ref[0] = (both[:, :COLS] + both[:, COLS:]).T


def rotate_ring(at, ring, own, other):
    slab = pl.BlockSpec((1, 1024, 256), lambda g: (g, 0, 0))
    return pl.pallas_call(
        functools.partial(rotate_ring_kernel, [offset for _, offset in ring]),
        grid=(4,),
        out_shape=jax.ShapeDtypeStruct((4, COLS, TOK), F32),
        in_specs=[pl.BlockSpec(memory_space=pltpu.SMEM)]
        + [pl.BlockSpec(memory_space=pltpu.HBM)] * len(ring)
        + [slab, slab],
        out_specs=pl.BlockSpec((1, COLS, TOK), lambda g: (g, 0, 0)),
        scratch_shapes=[pltpu.VMEM((TOK, 2048), BF16), pltpu.SemaphoreType.DMA((16,))],
        compiler_params=ALL_VMEM,
        cost_estimate=pl.CostEstimate(
            flops=4 * TOK * 2048 * 512, bytes_accessed=7 << 20, transcendentals=0
        ),
    )(at, *[block for block, _ in ring], own, other)


def reach_kernel(rows_ref, in_ref, own_ref, near_ref, far_ref):
    def put(out_ref):
        exact = in_ref[...]
        high = exact.astype(BF16)
        out_ref[:, :COLS] = high
        out_ref[:, COLS:] = (exact - high.astype(F32)).astype(BF16)

    step = pl.program_id(0)
    pl.when(step < 2)(lambda: put(own_ref))
    pl.when((step >= 2) & (step < 4))(lambda: put(near_ref))
    pl.when(step == 4)(lambda: put(far_ref))


def reach_basis(rows, basis):
    return pl.pallas_call(
        reach_kernel,
        grid_spec=pltpu.PrefetchScalarGridSpec(
            num_scalar_prefetch=1,
            grid=(5,),
            in_specs=[pl.BlockSpec((1024, COLS), lambda g, rows: (rows[g], 0))],
            out_specs=[
                pl.BlockSpec((1024, 256), lambda g, rows: (jnp.minimum(g, 1), 0)),
                pl.BlockSpec((1024, 256), lambda g, rows: (jnp.clip(g - 2, 0, 1), 0)),
                pl.BlockSpec((1024, 256), lambda g, rows: (0, 0)),
            ],
        ),
        out_shape=[jax.ShapeDtypeStruct((n, 256), BF16) for n in (2048, 2048, 1024)],
        compiler_params=ALL_VMEM,
        cost_estimate=pl.CostEstimate(
            flops=1 << 20, bytes_accessed=5 << 20, transcendentals=0
        ),
    )(rows, basis)


def rotate_kernel(at_ref, block_ref, *refs):
    own_ref, near_ref, near_swapped, far_ref, far_swapped, out_ref, lhs, sems = refs
    xh, y, c = at_ref[1], at_ref[2], at_ref[4]
    copies = []
    for z in range(8):
        for side in range(2):
            at = ((xh if side == 0 else 1 - xh) * 8 + z) * COLS
            lanes = pl.ds(pl.multiple_of(at, COLS), COLS)
            copies.append(
                pltpu.make_async_copy(block_ref.at[z, side], lhs.at[:, lanes], sems.at[z * 2 + side])
            )
    for copy in copies:
        copy.start()
    for copy in copies:
        copy.wait()

    def put(place, both):
        out_ref[lax.rem(place, 4)] = (both[:, :COLS] + both[:, COLS:]).T

    for offset, ref in ((4, own_ref), (3 + 2 * c, near_ref), (5 - 2 * c, near_swapped)):
        put(y + offset, jnp.dot(lhs[...], ref[...], preferred_element_type=F32))
    mine = lhs[:, pl.ds(pl.multiple_of(c * 1024, 1024), 1024)]
    rest = lhs[:, pl.ds(pl.multiple_of((1 - c) * 1024, 1024), 1024)]
    both = jnp.dot(mine, far_ref[...], preferred_element_type=F32)
    put(y + 2, both + jnp.dot(rest, far_swapped[...], preferred_element_type=F32))


def rotate(at, blocks, slabs):
    return pl.pallas_call(
        rotate_kernel,
        out_shape=jax.ShapeDtypeStruct((4, COLS, TOK), F32),
        in_specs=[pl.BlockSpec(memory_space=pltpu.SMEM), pl.BlockSpec(memory_space=pltpu.HBM)]
        + [pl.BlockSpec(memory_space=pltpu.VMEM)] * 5,
        out_specs=pl.BlockSpec(memory_space=pltpu.VMEM),
        scratch_shapes=[pltpu.VMEM((TOK, 2048), BF16), pltpu.SemaphoreType.DMA((16,))],
        compiler_params=PARAMS,
        cost_estimate=pl.CostEstimate(
            flops=4 * TOK * 2048 * 512, bytes_accessed=7 << 20, transcendentals=0
        ),
    )(at, blocks, *slabs)


def product_kernel(scale, at_ref, acts_ref, own_ref, other_ref, out_ref, right):
    xh, c = at_ref[1], at_ref[4]
    for z in range(8):
        for side in range(2):
            place = (xh if side == 0 else 1 - xh) * 8 + z
            for s in range(4):
                right[s, pl.ds(pl.multiple_of(place * 32, 32), 32), :] = acts_ref[z, side, s]
    for row in range(4):
        total = None
        for grads_ref, core in ((own_ref, c), (other_ref, 1 - c)):
            for side in range(2):
                part = lax.dot_general(
                    grads_ref[side, row],
                    right[side * 2 + core],
                    (((1,), (1,)), ((), ())),
                    preferred_element_type=F32,
                )
                total = part * part if total is None else total + part * part
        out_ref[row] = total * scale


def products(at, acts, own, other, scale):
    return pl.pallas_call(
        functools.partial(product_kernel, scale),
        out_shape=jax.ShapeDtypeStruct((4, COLS, 512), F32),
        in_specs=[pl.BlockSpec(memory_space=pltpu.SMEM)]
        + [pl.BlockSpec(memory_space=pltpu.VMEM)] * 3,
        out_specs=pl.BlockSpec(memory_space=pltpu.VMEM),
        scratch_shapes=[pltpu.VMEM((4, 512, TOK), BF16)],
        compiler_params=PARAMS,
        cost_estimate=pl.CostEstimate(
            flops=2 * 4 * 512 * 512 * TOK, bytes_accessed=5 << 20, transcendentals=0
        ),
    )(at, acts, own, other)


def weave_kernel(in_ref, out_ref):
    for tile in range(4):
        lanes = slice(tile * 32, tile * 32 + 32)
        out_ref[:, tile * COLS : (tile + 1) * COLS] = jnp.concatenate(
            [in_ref[q, :, lanes] for q in range(4)], axis=1
        )


def weave(parts):
    return pl.pallas_call(
        weave_kernel,
        grid=(4,),
        out_shape=jax.ShapeDtypeStruct((COLS, 2048), F32),
        in_specs=[pl.BlockSpec((4, COLS, 128), lambda g: (0, 0, g))],
        out_specs=pl.BlockSpec((COLS, 512), lambda g: (0, g)),
        compiler_params=PARAMS,
    )(parts)


def sync(*arrays):
    return lax.optimization_barrier(arrays)


def pair(x):
    return jnp.concatenate([x, shift(x, "xh", 1)])


def ring_step(up, down):
    return shift(up, "z", 1), shift(down, "z", -1)


def shift_near(x):
    pairs = [(i, (i + 1) % 4) for i in range(4)] + [(4 + i, 4 + (i + 3) % 4) for i in range(4)]
    return lax.ppermute(x, ("c", "y"), pairs)


def body(activations, gradients, basis_in, basis_out):
    z, xh, y, xl, c = (lax.axis_index(a) for a in ("z", "xh", "y", "xl", "c"))
    at = jnp.stack([z, xh, y, xl, c]).astype(jnp.int32)
    half = c.astype(jnp.int32).reshape(1)
    near_y, far_y = (y + 1 + 2 * c) % 4, (y + 2) % 4
    rows = jnp.stack(
        [y * 2, y * 2 + 1, near_y * 2, near_y * 2 + 1, far_y * 2 + c]
    ).astype(jnp.int32)

    a0, grads_pair, mine_in, basis_out = sync(
        pair(activations), pair(gradients), split_basis(half, basis_in), basis_out
    )
    own_in = lax.all_to_all(mine_in, "y", 0, 0)
    own_out, near_out, far_out = reach_basis(rows, basis_out)
    up1, down1, near_out, far_out = sync(*ring_step(a0, a0), near_out, far_out)
    up2, down2, near_out, far_out = sync(*ring_step(up1, down1), near_out, far_out)
    near_out = shift_near(near_out)
    up3, down3, own_in, far_out = sync(*ring_step(up2, down2), own_in, far_out)
    grad_blocks = lax.all_gather(after(grads_pair, up2), "z")
    far_out = shift(far_out, "y", 2)
    up4, other_in = sync(shift(up3, "z", 1), shift(own_in, "c", 1))
    ring = [(a0, 0), (up1, -1), (down1, 1), (up2, -2), (down2, 2), (up3, -3), (down3, 3), (up4, -4)]
    acts_part = rotate_ring(at, ring, own_in, other_in)
    near_out, far_out, acts_part = sync(near_out, far_out, acts_part)
    acts_in = lax.all_to_all(acts_part.reshape(16, 32, TOK), ("xl", "c", "y"), 0, 0)
    near_out2, far_out2 = shift(near_out, "c", 1), shift(far_out, "c", 1)

    acts = jnp.sum(acts_in.reshape(4, 4, 32, TOK), axis=1).astype(BF16)[None]
    rot_pair = pair(acts)
    rot_acts = lax.all_gather(rot_pair, "z")

    grad_blocks, rot_pair = sync(grad_blocks, rot_pair)
    grads_part = rotate(at, grad_blocks, (own_out, near_out, near_out2, far_out, far_out2))
    grads_in = lax.all_to_all(grads_part, "y", 0, 0)
    grads = jnp.sum(grads_in, axis=0).astype(BF16)
    copies = jnp.broadcast_to(grads, (8, COLS, TOK))
    rot_own = lax.all_to_all(copies, ("xl", "y"), 0, 0).reshape(2, 4, COLS, TOK)
    rot_other = shift(rot_own, "c", 1)

    part = products(at, rot_acts, rot_own, rot_other, 1.0 / (TOK * 4))
    return weave(lax.all_to_all(part, "y", 0, 0))


def solution(mesh):
    fine = Mesh(mesh.devices.reshape(SIZES), AXES)
    return jax.shard_map(
        body,
        mesh=fine,
        in_specs=(P(DP, None, TILE), P(DP, None, TILE), P(None, TILE), P(None, TILE)),
        out_specs=P(TILE, DP),
        check_vma=False,
    )
```

```python
import functools

import jax
import jax.numpy as jnp
from jax import lax
from jax.experimental import pallas as pl
from jax.experimental.pallas import tpu as pltpu
from jax.sharding import Mesh, PartitionSpec as P

AXES = ("xl", "c", "y", "xh", "z")
SIZES = (2, 2, 4, 2, 8)
DP = ("xl", "c")
TILE = ("y", "xh", "z")
TOK = 512
COLS = 128
F32 = jnp.float32
BF16 = jnp.bfloat16
ALL_VMEM = pltpu.CompilerParams(vmem_limit_bytes=58 * 1024 * 1024)
PARAMS = pltpu.CompilerParams(vmem_limit_bytes=48 * 1024 * 1024)


def shift(x, axis, by):
    n = lax.axis_size(axis)
    return lax.ppermute(x, axis, [(i, (i + by) % n) for i in range(n)])


def after(x, *others):
    return lax.optimization_barrier((x, *others))[0]


def whole(shape):
    return pl.BlockSpec(shape, lambda *_: (0,) * len(shape))


def split_kernel(half_ref, in_ref, out_ref):
    exact = in_ref[...]
    high = exact.astype(BF16)
    out_ref[0, :, :COLS] = high
    out_ref[0, :, COLS:] = (exact - high.astype(F32)).astype(BF16)


def split_basis(half, basis):
    rows = 1024
    return pl.pallas_call(
        split_kernel,
        grid_spec=pltpu.PrefetchScalarGridSpec(
            num_scalar_prefetch=1,
            grid=(4,),
            in_specs=[pl.BlockSpec((rows, COLS), lambda g, half: (g * 2 + half[0], 0))],
            out_specs=pl.BlockSpec((1, rows, 256), lambda g, half: (g, 0, 0)),
        ),
        out_shape=jax.ShapeDtypeStruct((4, rows, 256), BF16),
        compiler_params=ALL_VMEM,
        cost_estimate=pl.CostEstimate(
            flops=1 << 20, bytes_accessed=4 << 20, transcendentals=0
        ),
    )(half, basis)


def rotate_ring_kernel(offsets, at_ref, *refs):
    blocks, (own_ref, other_ref, out_ref, lhs, sems) = refs[: len(offsets)], refs[len(offsets) :]

    @pl.when(pl.program_id(0) == 0)
    def _():
        turned = lax.rem(at_ref[1] + at_ref[4], 2)
        copies = []
        for i, (block, offset) in enumerate(zip(blocks, offsets)):
            for side in range(2):
                half = turned if side == 0 else 1 - turned
                at = (half * 8 + lax.rem(at_ref[0] + 8 + offset, 8)) * COLS
                lanes = pl.ds(pl.multiple_of(at, COLS), COLS)
                copies.append(
                    pltpu.make_async_copy(block.at[side], lhs.at[:, lanes], sems.at[i * 2 + side])
                )
        for copy in copies:
            copy.start()
        for copy in copies:
            copy.wait()

    both = jnp.dot(lhs[:, :1024], own_ref[0], preferred_element_type=F32)
    both += jnp.dot(lhs[:, 1024:], other_ref[0], preferred_element_type=F32)
    out_ref[0] = (both[:, :COLS] + both[:, COLS:]).T


def rotate_ring(at, ring, own, other):
    slab = pl.BlockSpec((1, 1024, 256), lambda g: (g, 0, 0))
    return pl.pallas_call(
        functools.partial(rotate_ring_kernel, [offset for _, offset in ring]),
        grid=(4,),
        out_shape=jax.ShapeDtypeStruct((4, COLS, TOK), F32),
        in_specs=[pl.BlockSpec(memory_space=pltpu.SMEM)]
        + [pl.BlockSpec(memory_space=pltpu.HBM)] * len(ring)
        + [slab, slab],
        out_specs=pl.BlockSpec((1, COLS, TOK), lambda g: (g, 0, 0)),
        scratch_shapes=[pltpu.VMEM((TOK, 2048), BF16), pltpu.SemaphoreType.DMA((16,))],
        compiler_params=ALL_VMEM,
        cost_estimate=pl.CostEstimate(
            flops=4 * TOK * 2048 * 512, bytes_accessed=7 << 20, transcendentals=0
        ),
    )(at, *[block for block, _ in ring], own, other)


def reach_kernel(rows_ref, in_ref, own_ref, near_ref, far_ref):
    def put(out_ref):
        exact = in_ref[...]
        high = exact.astype(BF16)
        out_ref[:, :COLS] = high
        out_ref[:, COLS:] = (exact - high.astype(F32)).astype(BF16)

    step = pl.program_id(0)
    pl.when(step < 2)(lambda: put(own_ref))
    pl.when((step >= 2) & (step < 4))(lambda: put(near_ref))
    pl.when(step == 4)(lambda: put(far_ref))


def reach_basis(rows, basis):
    return pl.pallas_call(
        reach_kernel,
        grid_spec=pltpu.PrefetchScalarGridSpec(
            num_scalar_prefetch=1,
            grid=(5,),
            in_specs=[pl.BlockSpec((1024, COLS), lambda g, rows: (rows[g], 0))],
            out_specs=[
                pl.BlockSpec((1024, 256), lambda g, rows: (jnp.minimum(g, 1), 0)),
                pl.BlockSpec((1024, 256), lambda g, rows: (jnp.clip(g - 2, 0, 1), 0)),
                pl.BlockSpec((1024, 256), lambda g, rows: (0, 0)),
            ],
        ),
        out_shape=[jax.ShapeDtypeStruct((n, 256), BF16) for n in (2048, 2048, 1024)],
        compiler_params=ALL_VMEM,
        cost_estimate=pl.CostEstimate(
            flops=1 << 20, bytes_accessed=5 << 20, transcendentals=0
        ),
    )(rows, basis)


def rotate_kernel(at_ref, block_ref, *refs):
    own_ref, near_ref, near_swapped, far_ref, far_swapped, out_ref, lhs, sems = refs
    xh, y, c = at_ref[1], at_ref[2], at_ref[4]
    copies = []
    for z in range(8):
        for side in range(2):
            at = ((xh if side == 0 else 1 - xh) * 8 + z) * COLS
            lanes = pl.ds(pl.multiple_of(at, COLS), COLS)
            copies.append(
                pltpu.make_async_copy(block_ref.at[z, side], lhs.at[:, lanes], sems.at[z * 2 + side])
            )
    for copy in copies:
        copy.start()
    for copy in copies:
        copy.wait()

    def put(place, both):
        out_ref[lax.rem(place, 4)] = (both[:, :COLS] + both[:, COLS:]).T

    for offset, ref in ((4, own_ref), (3 + 2 * c, near_ref), (5 - 2 * c, near_swapped)):
        put(y + offset, jnp.dot(lhs[...], ref[...], preferred_element_type=F32))
    mine = lhs[:, pl.ds(pl.multiple_of(c * 1024, 1024), 1024)]
    rest = lhs[:, pl.ds(pl.multiple_of((1 - c) * 1024, 1024), 1024)]
    both = jnp.dot(mine, far_ref[...], preferred_element_type=F32)
    put(y + 2, both + jnp.dot(rest, far_swapped[...], preferred_element_type=F32))


def rotate(at, blocks, slabs):
    return pl.pallas_call(
        rotate_kernel,
        out_shape=jax.ShapeDtypeStruct((4, COLS, TOK), F32),
        in_specs=[pl.BlockSpec(memory_space=pltpu.SMEM), pl.BlockSpec(memory_space=pltpu.HBM)]
        + [pl.BlockSpec(memory_space=pltpu.VMEM)] * 5,
        out_specs=pl.BlockSpec(memory_space=pltpu.VMEM),
        scratch_shapes=[pltpu.VMEM((TOK, 2048), BF16), pltpu.SemaphoreType.DMA((16,))],
        compiler_params=PARAMS,
        cost_estimate=pl.CostEstimate(
            flops=4 * TOK * 2048 * 512, bytes_accessed=7 << 20, transcendentals=0
        ),
    )(at, blocks, *slabs)


def product_kernel(scale, at_ref, acts_ref, own_ref, other_ref, out_ref, right):
    xh, c = at_ref[1], at_ref[4]
    for z in range(8):
        for side in range(2):
            place = (xh if side == 0 else 1 - xh) * 8 + z
            for s in range(4):
                right[s, pl.ds(pl.multiple_of(place * 32, 32), 32), :] = acts_ref[z, side, s]
    for row in range(4):
        total = None
        for grads_ref, core in ((own_ref, c), (other_ref, 1 - c)):
            for side in range(2):
                part = lax.dot_general(
                    grads_ref[side, row],
                    right[side * 2 + core],
                    (((1,), (1,)), ((), ())),
                    preferred_element_type=F32,
                )
                total = part * part if total is None else total + part * part
        out_ref[row] = (total * scale).astype(BF16)


def products(at, acts, own, other, scale):
    return pl.pallas_call(
        functools.partial(product_kernel, scale),
        out_shape=jax.ShapeDtypeStruct((4, COLS, 512), BF16),
        in_specs=[pl.BlockSpec(memory_space=pltpu.SMEM)]
        + [pl.BlockSpec(memory_space=pltpu.VMEM)] * 3,
        out_specs=pl.BlockSpec(memory_space=pltpu.VMEM),
        scratch_shapes=[pltpu.VMEM((4, 512, TOK), BF16)],
        compiler_params=PARAMS,
        cost_estimate=pl.CostEstimate(
            flops=2 * 4 * 512 * 512 * TOK, bytes_accessed=5 << 20, transcendentals=0
        ),
    )(at, acts, own, other)


def weave_kernel(in_ref, out_ref):
    for tile in range(4):
        lanes = slice(tile * 32, tile * 32 + 32)
        out_ref[:, tile * COLS : (tile + 1) * COLS] = jnp.concatenate(
            [in_ref[q].astype(F32)[:, lanes] for q in range(4)], axis=1
        )


def weave(parts):
    return pl.pallas_call(
        weave_kernel,
        grid=(4,),
        out_shape=jax.ShapeDtypeStruct((COLS, 2048), F32),
        in_specs=[pl.BlockSpec((4, COLS, 128), lambda g: (0, 0, g))],
        out_specs=pl.BlockSpec((COLS, 512), lambda g: (0, g)),
        compiler_params=PARAMS,
    )(parts)


def sync(*arrays):
    return lax.optimization_barrier(arrays)


def pair(x):
    return jnp.concatenate([x, shift(x, "xh", 1)])


def ring_step(up, down):
    return shift(up, "z", 1), shift(down, "z", -1)


def shift_near(x):
    pairs = [(i, (i + 1) % 4) for i in range(4)] + [(4 + i, 4 + (i + 3) % 4) for i in range(4)]
    return lax.ppermute(x, ("c", "y"), pairs)


def body(activations, gradients, basis_in, basis_out):
    z, xh, y, xl, c = (lax.axis_index(a) for a in ("z", "xh", "y", "xl", "c"))
    at = jnp.stack([z, xh, y, xl, c]).astype(jnp.int32)
    half = c.astype(jnp.int32).reshape(1)
    near_y, far_y = (y + 1 + 2 * c) % 4, (y + 2) % 4
    rows = jnp.stack(
        [y * 2, y * 2 + 1, near_y * 2, near_y * 2 + 1, far_y * 2 + c]
    ).astype(jnp.int32)

    a0, grads_pair, mine_in, basis_out = sync(
        pair(activations), pair(gradients), split_basis(half, basis_in), basis_out
    )
    own_in = lax.all_to_all(mine_in, "y", 0, 0)
    own_out, near_out, far_out = reach_basis(rows, basis_out)
    up1, down1, near_out, far_out = sync(*ring_step(a0, a0), near_out, far_out)
    up2, down2, near_out, far_out = sync(*ring_step(up1, down1), near_out, far_out)
    near_out = shift_near(near_out)
    up3, down3, own_in, far_out = sync(*ring_step(up2, down2), own_in, far_out)
    grad_blocks = lax.all_gather(after(grads_pair, up2), "z")
    far_out = shift(far_out, "y", 2)
    up4, other_in = sync(shift(up3, "z", 1), shift(own_in, "c", 1))
    ring = [(a0, 0), (up1, -1), (down1, 1), (up2, -2), (down2, 2), (up3, -3), (down3, 3), (up4, -4)]
    acts_part = rotate_ring(at, ring, own_in, other_in)
    near_out, far_out, acts_part = sync(near_out, far_out, acts_part)
    acts_in = lax.all_to_all(acts_part.reshape(16, 32, TOK), ("xl", "c", "y"), 0, 0)
    near_out2, far_out2 = shift(near_out, "c", 1), shift(far_out, "c", 1)

    acts = jnp.sum(acts_in.reshape(4, 4, 32, TOK), axis=1).astype(BF16)[None]
    rot_pair = pair(acts)
    rot_acts = lax.all_gather(rot_pair, "z")

    grad_blocks, rot_pair = sync(grad_blocks, rot_pair)
    grads_part = rotate(at, grad_blocks, (own_out, near_out, near_out2, far_out, far_out2))
    grads_in = lax.all_to_all(grads_part, "y", 0, 0)
    grads = jnp.sum(grads_in, axis=0).astype(BF16)
    copies = jnp.broadcast_to(grads, (8, COLS, TOK))
    rot_own = lax.all_to_all(copies, ("xl", "y"), 0, 0).reshape(2, 4, COLS, TOK)
    rot_other = shift(rot_own, "c", 1)

    part = products(at, rot_acts, rot_own, rot_other, 1.0 / (TOK * 4))
    return weave(lax.all_to_all(part, "y", 0, 0))


def solution(mesh):
    fine = Mesh(mesh.devices.reshape(SIZES), AXES)
    return jax.shard_map(
        body,
        mesh=fine,
        in_specs=(P(DP, None, TILE), P(DP, None, TILE), P(None, TILE), P(None, TILE)),
        out_specs=P(TILE, DP),
        check_vma=False,
    )
```

```python
import functools

import jax
import jax.numpy as jnp
from jax import lax
from jax.experimental import pallas as pl
from jax.experimental.pallas import tpu as pltpu
from jax.sharding import Mesh, PartitionSpec as P

AXES = ("xl", "c", "y", "xh", "z")
SIZES = (2, 2, 4, 2, 8)
DP = ("xl", "c")
TILE = ("y", "xh", "z")
TOK = 512
COLS = 128
F32 = jnp.float32
BF16 = jnp.bfloat16
ALL_VMEM = pltpu.CompilerParams(vmem_limit_bytes=58 * 1024 * 1024)
PARAMS = pltpu.CompilerParams(vmem_limit_bytes=48 * 1024 * 1024)


def shift(x, axis, by):
    n = lax.axis_size(axis)
    return lax.ppermute(x, axis, [(i, (i + by) % n) for i in range(n)])


def after(x, *others):
    return lax.optimization_barrier((x, *others))[0]


def whole(shape):
    return pl.BlockSpec(shape, lambda *_: (0,) * len(shape))


def split_kernel(half_ref, in_ref, out_ref):
    exact = in_ref[...]
    high = exact.astype(BF16)
    out_ref[0, :, :COLS] = high
    out_ref[0, :, COLS:] = (exact - high.astype(F32)).astype(BF16)


def split_basis(half, basis):
    rows = 1024
    return pl.pallas_call(
        split_kernel,
        grid_spec=pltpu.PrefetchScalarGridSpec(
            num_scalar_prefetch=1,
            grid=(4,),
            in_specs=[pl.BlockSpec((rows, COLS), lambda g, half: (g * 2 + half[0], 0))],
            out_specs=pl.BlockSpec((1, rows, 256), lambda g, half: (g, 0, 0)),
        ),
        out_shape=jax.ShapeDtypeStruct((4, rows, 256), BF16),
        compiler_params=ALL_VMEM,
        cost_estimate=pl.CostEstimate(
            flops=1 << 20, bytes_accessed=4 << 20, transcendentals=0
        ),
    )(half, basis)


def rotate_ring_kernel(offsets, at_ref, *refs):
    blocks, (own_ref, other_ref, out_ref, lhs, sems) = refs[: len(offsets)], refs[len(offsets) :]

    @pl.when(pl.program_id(0) == 0)
    def _():
        turned = lax.rem(at_ref[1] + at_ref[4], 2)
        copies = []
        for i, (block, offset) in enumerate(zip(blocks, offsets)):
            for side in range(2):
                half = turned if side == 0 else 1 - turned
                at = (half * 8 + lax.rem(at_ref[0] + 8 + offset, 8)) * COLS
                lanes = pl.ds(pl.multiple_of(at, COLS), COLS)
                copies.append(
                    pltpu.make_async_copy(block.at[side], lhs.at[:, lanes], sems.at[i * 2 + side])
                )
        for copy in copies:
            copy.start()
        for copy in copies:
            copy.wait()

    both = jnp.dot(lhs[:, :1024], own_ref[0], preferred_element_type=F32)
    both += jnp.dot(lhs[:, 1024:], other_ref[0], preferred_element_type=F32)
    out_ref[0] = (both[:, :COLS] + both[:, COLS:]).T


def rotate_ring(at, ring, own, other):
    slab = pl.BlockSpec((1, 1024, 256), lambda g: (g, 0, 0))
    return pl.pallas_call(
        functools.partial(rotate_ring_kernel, [offset for _, offset in ring]),
        grid=(4,),
        out_shape=jax.ShapeDtypeStruct((4, COLS, TOK), F32),
        in_specs=[pl.BlockSpec(memory_space=pltpu.SMEM)]
        + [pl.BlockSpec(memory_space=pltpu.HBM)] * len(ring)
        + [slab, slab],
        out_specs=pl.BlockSpec((1, COLS, TOK), lambda g: (g, 0, 0)),
        scratch_shapes=[pltpu.VMEM((TOK, 2048), BF16), pltpu.SemaphoreType.DMA((16,))],
        compiler_params=ALL_VMEM,
        cost_estimate=pl.CostEstimate(
            flops=4 * TOK * 2048 * 512, bytes_accessed=7 << 20, transcendentals=0
        ),
    )(at, *[block for block, _ in ring], own, other)


def reach_kernel(rows_ref, in_ref, own_ref, near_ref, far_ref):
    def put(out_ref):
        exact = in_ref[...]
        high = exact.astype(BF16)
        out_ref[:, :COLS] = high
        out_ref[:, COLS:] = (exact - high.astype(F32)).astype(BF16)

    step = pl.program_id(0)
    pl.when(step < 2)(lambda: put(own_ref))
    pl.when((step >= 2) & (step < 4))(lambda: put(near_ref))
    pl.when(step == 4)(lambda: put(far_ref))


def reach_basis(rows, basis):
    return pl.pallas_call(
        reach_kernel,
        grid_spec=pltpu.PrefetchScalarGridSpec(
            num_scalar_prefetch=1,
            grid=(5,),
            in_specs=[pl.BlockSpec((1024, COLS), lambda g, rows: (rows[g], 0))],
            out_specs=[
                pl.BlockSpec((1024, 256), lambda g, rows: (jnp.minimum(g, 1), 0)),
                pl.BlockSpec((1024, 256), lambda g, rows: (jnp.clip(g - 2, 0, 1), 0)),
                pl.BlockSpec((1024, 256), lambda g, rows: (0, 0)),
            ],
        ),
        out_shape=[jax.ShapeDtypeStruct((n, 256), BF16) for n in (2048, 2048, 1024)],
        compiler_params=ALL_VMEM,
        cost_estimate=pl.CostEstimate(
            flops=1 << 20, bytes_accessed=5 << 20, transcendentals=0
        ),
    )(rows, basis)


def rotate_kernel(at_ref, block_ref, *refs):
    own_ref, near_ref, near_swapped, far_ref, far_swapped, out_ref, lhs, sems = refs
    xh, y, c = at_ref[1], at_ref[2], at_ref[4]
    copies = []
    for z in range(8):
        for side in range(2):
            at = ((xh if side == 0 else 1 - xh) * 8 + z) * COLS
            lanes = pl.ds(pl.multiple_of(at, COLS), COLS)
            copies.append(
                pltpu.make_async_copy(block_ref.at[z, side], lhs.at[:, lanes], sems.at[z * 2 + side])
            )
    for copy in copies:
        copy.start()
    for copy in copies:
        copy.wait()

    def put(place, both):
        out_ref[lax.rem(place, 4)] = (both[:, :COLS] + both[:, COLS:]).T

    for offset, ref in ((4, own_ref), (3 + 2 * c, near_ref), (5 - 2 * c, near_swapped)):
        put(y + offset, jnp.dot(lhs[...], ref[...], preferred_element_type=F32))
    mine = lhs[:, pl.ds(pl.multiple_of(c * 1024, 1024), 1024)]
    rest = lhs[:, pl.ds(pl.multiple_of((1 - c) * 1024, 1024), 1024)]
    both = jnp.dot(mine, far_ref[...], preferred_element_type=F32)
    put(y + 2, both + jnp.dot(rest, far_swapped[...], preferred_element_type=F32))


def rotate(at, blocks, slabs):
    return pl.pallas_call(
        rotate_kernel,
        out_shape=jax.ShapeDtypeStruct((4, COLS, TOK), F32),
        in_specs=[pl.BlockSpec(memory_space=pltpu.SMEM), pl.BlockSpec(memory_space=pltpu.HBM)]
        + [pl.BlockSpec(memory_space=pltpu.VMEM)] * 5,
        out_specs=pl.BlockSpec(memory_space=pltpu.VMEM),
        scratch_shapes=[pltpu.VMEM((TOK, 2048), BF16), pltpu.SemaphoreType.DMA((16,))],
        compiler_params=PARAMS,
        cost_estimate=pl.CostEstimate(
            flops=4 * TOK * 2048 * 512, bytes_accessed=7 << 20, transcendentals=0
        ),
    )(at, blocks, *slabs)


def product_kernel(scale, at_ref, acts_ref, own_ref, other_ref, out_ref, right):
    xh, c = at_ref[1], at_ref[4]
    for z in range(8):
        for side in range(2):
            place = (xh if side == 0 else 1 - xh) * 8 + z
            for s in range(4):
                right[s, pl.ds(pl.multiple_of(place * 32, 32), 32), :] = acts_ref[z, side, s]
    for row in range(4):
        total = None
        for grads_ref, core in ((own_ref, c), (other_ref, 1 - c)):
            for side in range(2):
                part = lax.dot_general(
                    grads_ref[side, row],
                    right[side * 2 + core],
                    (((1,), (1,)), ((), ())),
                    preferred_element_type=F32,
                )
                total = part * part if total is None else total + part * part
        out_ref[row] = (total * scale).astype(BF16)


def products(at, acts, own, other, scale):
    return pl.pallas_call(
        functools.partial(product_kernel, scale),
        out_shape=jax.ShapeDtypeStruct((4, COLS, 512), BF16),
        in_specs=[pl.BlockSpec(memory_space=pltpu.SMEM)]
        + [pl.BlockSpec(memory_space=pltpu.VMEM)] * 3,
        out_specs=pl.BlockSpec(memory_space=pltpu.VMEM),
        scratch_shapes=[pltpu.VMEM((4, 512, TOK), BF16)],
        compiler_params=PARAMS,
        cost_estimate=pl.CostEstimate(
            flops=2 * 4 * 512 * 512 * TOK, bytes_accessed=5 << 20, transcendentals=0
        ),
    )(at, acts, own, other)


def weave_kernel(in_ref, out_ref):
    for tile in range(4):
        lanes = slice(tile * 32, tile * 32 + 32)
        out_ref[:, tile * COLS : (tile + 1) * COLS] = jnp.concatenate(
            [in_ref[q].astype(F32)[:, lanes] for q in range(4)], axis=1
        )


def weave(parts):
    return pl.pallas_call(
        weave_kernel,
        grid=(4,),
        out_shape=jax.ShapeDtypeStruct((COLS, 2048), F32),
        in_specs=[pl.BlockSpec((4, COLS, 128), lambda g: (0, 0, g))],
        out_specs=pl.BlockSpec((COLS, 512), lambda g: (0, g)),
        compiler_params=PARAMS,
    )(parts)


def sync(*arrays):
    return lax.optimization_barrier(arrays)


def pair(x):
    return jnp.concatenate([x, shift(x, "xh", 1)])


def ring_step(up, down):
    return shift(up, "z", 1), shift(down, "z", -1)


def shift_near(x):
    pairs = [(i, (i + 1) % 4) for i in range(4)] + [(4 + i, 4 + (i + 3) % 4) for i in range(4)]
    return lax.ppermute(x, ("c", "y"), pairs)


def body(activations, gradients, basis_in, basis_out):
    z, xh, y, xl, c = (lax.axis_index(a) for a in ("z", "xh", "y", "xl", "c"))
    at = jnp.stack([z, xh, y, xl, c]).astype(jnp.int32)
    half = c.astype(jnp.int32).reshape(1)
    near_y, far_y = (y + 1 + 2 * c) % 4, (y + 2) % 4
    rows = jnp.stack(
        [y * 2, y * 2 + 1, near_y * 2, near_y * 2 + 1, far_y * 2 + c]
    ).astype(jnp.int32)

    a0, grads_pair, mine_in, basis_out = sync(
        pair(activations), pair(gradients), split_basis(half, basis_in), basis_out
    )
    own_in = lax.all_to_all(mine_in, "y", 0, 0)
    own_out, near_out, far_out = reach_basis(rows, basis_out)
    up1, down1, near_out, far_out = sync(*ring_step(a0, a0), near_out, far_out)
    up2, down2, near_out, far_out = sync(*ring_step(up1, down1), near_out, far_out)
    near_out = shift_near(near_out)
    up3, down3, own_in, far_out = sync(*ring_step(up2, down2), own_in, far_out)
    grad_blocks = lax.all_gather(after(grads_pair, up2), "z")
    far_out = shift(far_out, "y", 2)
    up4, other_in = sync(shift(up3, "z", 1), shift(own_in, "c", 1))
    ring = [(a0, 0), (up1, -1), (down1, 1), (up2, -2), (down2, 2), (up3, -3), (down3, 3), (up4, -4)]
    acts_part = rotate_ring(at, ring, own_in, other_in)
    near_out, far_out, acts_part = sync(near_out, far_out, acts_part)
    acts_in = lax.all_to_all(acts_part.reshape(16, 32, TOK), ("xl", "c", "y"), 0, 0)
    near_out2, far_out2 = shift(near_out, "c", 1), shift(far_out, "c", 1)
    grads_part = rotate(at, grad_blocks, (own_out, near_out, near_out2, far_out, far_out2))
    acts_in, grads_part = sync(acts_in, grads_part)

    acts = jnp.sum(acts_in.reshape(4, 4, 32, TOK), axis=1).astype(BF16)[None]
    rot_acts = lax.all_gather(pair(acts), "z")

    grads_in = lax.all_to_all(grads_part, "y", 0, 0)
    grads = jnp.sum(grads_in, axis=0).astype(BF16)
    copies = jnp.broadcast_to(grads, (8, COLS, TOK))
    rot_own = lax.all_to_all(copies, ("xl", "y"), 0, 0).reshape(2, 4, COLS, TOK)
    rot_other = shift(rot_own, "c", 1)

    part = products(at, rot_acts, rot_own, rot_other, 1.0 / (TOK * 4))
    return weave(lax.all_to_all(part, "y", 0, 0))


def solution(mesh):
    fine = Mesh(mesh.devices.reshape(SIZES), AXES)
    return jax.shard_map(
        body,
        mesh=fine,
        in_specs=(P(DP, None, TILE), P(DP, None, TILE), P(None, TILE), P(None, TILE)),
        out_specs=P(TILE, DP),
        check_vma=False,
    )
```

```python
import functools

import jax
import jax.numpy as jnp
from jax import lax
from jax.experimental import pallas as pl
from jax.experimental.pallas import tpu as pltpu
from jax.sharding import Mesh, PartitionSpec as P

AXES = ("xl", "c", "y", "xh", "z")
SIZES = (2, 2, 4, 2, 8)
DP = ("xl", "c")
TILE = ("y", "xh", "z")
TOK = 512
COLS = 128
F32 = jnp.float32
BF16 = jnp.bfloat16
ALL_VMEM = pltpu.CompilerParams(vmem_limit_bytes=58 * 1024 * 1024)
PARAMS = pltpu.CompilerParams(vmem_limit_bytes=48 * 1024 * 1024)


def shift(x, axis, by):
    n = lax.axis_size(axis)
    return lax.ppermute(x, axis, [(i, (i + by) % n) for i in range(n)])


def after(x, *others):
    return lax.optimization_barrier((x, *others))[0]


def whole(shape):
    return pl.BlockSpec(shape, lambda *_: (0,) * len(shape))


def split_kernel(half_ref, in_ref, out_ref):
    exact = in_ref[...]
    high = exact.astype(BF16)
    out_ref[0, :, :COLS] = high
    out_ref[0, :, COLS:] = (exact - high.astype(F32)).astype(BF16)


def split_basis(half, basis):
    rows = 1024
    return pl.pallas_call(
        split_kernel,
        grid_spec=pltpu.PrefetchScalarGridSpec(
            num_scalar_prefetch=1,
            grid=(4,),
            in_specs=[pl.BlockSpec((rows, COLS), lambda g, half: (g * 2 + half[0], 0))],
            out_specs=pl.BlockSpec((1, rows, 256), lambda g, half: (g, 0, 0)),
        ),
        out_shape=jax.ShapeDtypeStruct((4, rows, 256), BF16),
        compiler_params=ALL_VMEM,
        cost_estimate=pl.CostEstimate(
            flops=1 << 20, bytes_accessed=4 << 20, transcendentals=0
        ),
    )(half, basis)


def rotate_ring_kernel(offsets, at_ref, *refs):
    blocks, (own_ref, other_ref, out_ref, lhs, sems) = refs[: len(offsets)], refs[len(offsets) :]

    @pl.when(pl.program_id(0) == 0)
    def _():
        turned = lax.rem(at_ref[1] + at_ref[4], 2)
        copies = []
        for i, (block, offset) in enumerate(zip(blocks, offsets)):
            for side in range(2):
                half = turned if side == 0 else 1 - turned
                at = (half * 8 + lax.rem(at_ref[0] + 8 + offset, 8)) * COLS
                lanes = pl.ds(pl.multiple_of(at, COLS), COLS)
                copies.append(
                    pltpu.make_async_copy(block.at[side], lhs.at[:, lanes], sems.at[i * 2 + side])
                )
        for copy in copies:
            copy.start()
        for copy in copies:
            copy.wait()

    both = jnp.dot(lhs[:, :1024], own_ref[0], preferred_element_type=F32)
    both += jnp.dot(lhs[:, 1024:], other_ref[0], preferred_element_type=F32)
    out_ref[0] = (both[:, :COLS] + both[:, COLS:]).T


def rotate_ring(at, ring, own, other):
    slab = pl.BlockSpec((1, 1024, 256), lambda g: (g, 0, 0))
    return pl.pallas_call(
        functools.partial(rotate_ring_kernel, [offset for _, offset in ring]),
        grid=(4,),
        out_shape=jax.ShapeDtypeStruct((4, COLS, TOK), F32),
        in_specs=[pl.BlockSpec(memory_space=pltpu.SMEM)]
        + [pl.BlockSpec(memory_space=pltpu.HBM)] * len(ring)
        + [slab, slab],
        out_specs=pl.BlockSpec((1, COLS, TOK), lambda g: (g, 0, 0)),
        scratch_shapes=[pltpu.VMEM((TOK, 2048), BF16), pltpu.SemaphoreType.DMA((16,))],
        compiler_params=ALL_VMEM,
        cost_estimate=pl.CostEstimate(
            flops=4 * TOK * 2048 * 512, bytes_accessed=7 << 20, transcendentals=0
        ),
    )(at, *[block for block, _ in ring], own, other)


def reach_kernel(rows_ref, in_ref, own_ref, near_ref, far_ref):
    def put(out_ref):
        exact = in_ref[...]
        high = exact.astype(BF16)
        out_ref[:, :COLS] = high
        out_ref[:, COLS:] = (exact - high.astype(F32)).astype(BF16)

    step = pl.program_id(0)
    pl.when(step < 2)(lambda: put(own_ref))
    pl.when((step >= 2) & (step < 4))(lambda: put(near_ref))
    pl.when(step == 4)(lambda: put(far_ref))


def reach_basis(rows, basis):
    return pl.pallas_call(
        reach_kernel,
        grid_spec=pltpu.PrefetchScalarGridSpec(
            num_scalar_prefetch=1,
            grid=(5,),
            in_specs=[pl.BlockSpec((1024, COLS), lambda g, rows: (rows[g], 0))],
            out_specs=[
                pl.BlockSpec((1024, 256), lambda g, rows: (jnp.minimum(g, 1), 0)),
                pl.BlockSpec((1024, 256), lambda g, rows: (jnp.clip(g - 2, 0, 1), 0)),
                pl.BlockSpec((1024, 256), lambda g, rows: (0, 0)),
            ],
        ),
        out_shape=[jax.ShapeDtypeStruct((n, 256), BF16) for n in (2048, 2048, 1024)],
        compiler_params=ALL_VMEM,
        cost_estimate=pl.CostEstimate(
            flops=1 << 20, bytes_accessed=5 << 20, transcendentals=0
        ),
    )(rows, basis)


def rotate_kernel(at_ref, block_ref, *refs):
    own_ref, near_ref, near_swapped, far_ref, far_swapped, out_ref, lhs, sems = refs
    xh, y, c = at_ref[1], at_ref[2], at_ref[4]
    copies = []
    for z in range(8):
        for side in range(2):
            at = ((xh if side == 0 else 1 - xh) * 8 + z) * COLS
            lanes = pl.ds(pl.multiple_of(at, COLS), COLS)
            copies.append(
                pltpu.make_async_copy(block_ref.at[z, side], lhs.at[:, lanes], sems.at[z * 2 + side])
            )
    for copy in copies:
        copy.start()
    for copy in copies:
        copy.wait()

    def put(place, both):
        out_ref[lax.rem(place, 4)] = (both[:, :COLS] + both[:, COLS:]).T

    for offset, ref in ((4, own_ref), (3 + 2 * c, near_ref), (5 - 2 * c, near_swapped)):
        put(y + offset, jnp.dot(lhs[...], ref[...], preferred_element_type=F32))
    mine = lhs[:, pl.ds(pl.multiple_of(c * 1024, 1024), 1024)]
    rest = lhs[:, pl.ds(pl.multiple_of((1 - c) * 1024, 1024), 1024)]
    both = jnp.dot(mine, far_ref[...], preferred_element_type=F32)
    put(y + 2, both + jnp.dot(rest, far_swapped[...], preferred_element_type=F32))


def rotate(at, blocks, slabs):
    return pl.pallas_call(
        rotate_kernel,
        out_shape=jax.ShapeDtypeStruct((4, COLS, TOK), F32),
        in_specs=[pl.BlockSpec(memory_space=pltpu.SMEM), pl.BlockSpec(memory_space=pltpu.HBM)]
        + [pl.BlockSpec(memory_space=pltpu.VMEM)] * 5,
        out_specs=pl.BlockSpec(memory_space=pltpu.VMEM),
        scratch_shapes=[pltpu.VMEM((TOK, 2048), BF16), pltpu.SemaphoreType.DMA((16,))],
        compiler_params=PARAMS,
        cost_estimate=pl.CostEstimate(
            flops=4 * TOK * 2048 * 512, bytes_accessed=7 << 20, transcendentals=0
        ),
    )(at, blocks, *slabs)


def product_kernel(scale, at_ref, acts_ref, own_ref, other_ref, out_ref, right):
    xh, c = at_ref[1], at_ref[4]
    for z in range(8):
        for side in range(2):
            place = (xh if side == 0 else 1 - xh) * 8 + z
            for s in range(4):
                right[s, pl.ds(pl.multiple_of(place * 32, 32), 32), :] = acts_ref[z, side, s]
    for row in range(4):
        total = None
        for grads_ref, core in ((own_ref, c), (other_ref, 1 - c)):
            for side in range(2):
                part = lax.dot_general(
                    grads_ref[side, row],
                    right[side * 2 + core],
                    (((1,), (1,)), ((), ())),
                    preferred_element_type=F32,
                )
                total = part * part if total is None else total + part * part
        out_ref[row] = (total * scale).astype(BF16)


def products(at, acts, own, other, scale):
    return pl.pallas_call(
        functools.partial(product_kernel, scale),
        out_shape=jax.ShapeDtypeStruct((4, COLS, 512), BF16),
        in_specs=[pl.BlockSpec(memory_space=pltpu.SMEM)]
        + [pl.BlockSpec(memory_space=pltpu.VMEM)] * 3,
        out_specs=pl.BlockSpec(memory_space=pltpu.VMEM),
        scratch_shapes=[pltpu.VMEM((4, 512, TOK), BF16)],
        compiler_params=PARAMS,
        cost_estimate=pl.CostEstimate(
            flops=2 * 4 * 512 * 512 * TOK, bytes_accessed=5 << 20, transcendentals=0
        ),
    )(at, acts, own, other)


def weave_kernel(in_ref, out_ref):
    for tile in range(4):
        lanes = slice(tile * 32, tile * 32 + 32)
        out_ref[:, tile * COLS : (tile + 1) * COLS] = jnp.concatenate(
            [in_ref[q].astype(F32)[:, lanes] for q in range(4)], axis=1
        )


def weave(parts):
    return pl.pallas_call(
        weave_kernel,
        grid=(4,),
        out_shape=jax.ShapeDtypeStruct((COLS, 2048), F32),
        in_specs=[pl.BlockSpec((4, COLS, 128), lambda g: (0, 0, g))],
        out_specs=pl.BlockSpec((COLS, 512), lambda g: (0, g)),
        compiler_params=PARAMS,
    )(parts)


def sync(*arrays):
    return lax.optimization_barrier(arrays)


def pair(x):
    return jnp.concatenate([x, shift(x, "xh", 1)])


def ring_step(up, down):
    return shift(up, "z", 1), shift(down, "z", -1)


def shift_near(x):
    pairs = [(i, (i + 1) % 4) for i in range(4)] + [(4 + i, 4 + (i + 3) % 4) for i in range(4)]
    return lax.ppermute(x, ("c", "y"), pairs)


def body(activations, gradients, basis_in, basis_out):
    z, xh, y, xl, c = (lax.axis_index(a) for a in ("z", "xh", "y", "xl", "c"))
    at = jnp.stack([z, xh, y, xl, c]).astype(jnp.int32)
    half = c.astype(jnp.int32).reshape(1)
    near_y, far_y = (y + 1 + 2 * c) % 4, (y + 2) % 4
    rows = jnp.stack(
        [y * 2, y * 2 + 1, near_y * 2, near_y * 2 + 1, far_y * 2 + c]
    ).astype(jnp.int32)

    own_in = lax.all_to_all(split_basis(half, basis_in), "y", 0, 0)
    a0, grads_pair, basis_out = sync(pair(activations), pair(gradients), basis_out)
    own_out, near_out, far_out = reach_basis(rows, basis_out)
    up1, down1, near_out, far_out = sync(*ring_step(a0, a0), near_out, far_out)
    up2, down2, near_out, far_out = sync(*ring_step(up1, down1), near_out, far_out)
    up3, down3, own_in, near_out, far_out = sync(
        *ring_step(up2, down2), own_in, shift_near(near_out), far_out
    )
    grad_blocks = lax.all_gather(after(grads_pair, up2), "z")
    far_out = shift(far_out, "y", 2)
    up4, other_in = sync(shift(up3, "z", 1), shift(own_in, "c", 1))
    ring = [(a0, 0), (up1, -1), (down1, 1), (up2, -2), (down2, 2), (up3, -3), (down3, 3), (up4, -4)]
    acts_part = rotate_ring(at, ring, own_in, other_in)
    near_out, far_out, acts_part = sync(near_out, far_out, acts_part)
    acts_in = lax.all_to_all(acts_part.reshape(16, 32, TOK), ("xl", "c", "y"), 0, 0)
    near_out2, far_out2 = shift(near_out, "c", 1), shift(far_out, "c", 1)
    grads_part = rotate(at, grad_blocks, (own_out, near_out, near_out2, far_out, far_out2))
    acts_in, grads_part = sync(acts_in, grads_part)

    acts = jnp.sum(acts_in.reshape(4, 4, 32, TOK), axis=1).astype(BF16)[None]
    rot_acts = lax.all_gather(pair(acts), "z")

    grads_in = lax.all_to_all(grads_part, "y", 0, 0)
    grads = jnp.sum(grads_in, axis=0).astype(BF16)
    copies = jnp.broadcast_to(grads, (8, COLS, TOK))
    rot_own = lax.all_to_all(copies, ("xl", "y"), 0, 0).reshape(2, 4, COLS, TOK)
    rot_other = shift(rot_own, "c", 1)

    part = products(at, rot_acts, rot_own, rot_other, 1.0 / (TOK * 4))
    return weave(lax.all_to_all(part, "y", 0, 0))


def solution(mesh):
    fine = Mesh(mesh.devices.reshape(SIZES), AXES)
    return jax.shard_map(
        body,
        mesh=fine,
        in_specs=(P(DP, None, TILE), P(DP, None, TILE), P(None, TILE), P(None, TILE)),
        out_specs=P(TILE, DP),
        check_vma=False,
    )
```

```python
import functools

import jax
import jax.numpy as jnp
from jax import lax
from jax.experimental import pallas as pl
from jax.experimental.pallas import tpu as pltpu
from jax.sharding import Mesh, PartitionSpec as P

AXES = ("xl", "c", "y", "xh", "z")
SIZES = (2, 2, 4, 2, 8)
DP = ("xl", "c")
TILE = ("y", "xh", "z")
TOK = 512
COLS = 128
F32 = jnp.float32
BF16 = jnp.bfloat16
ALL_VMEM = pltpu.CompilerParams(vmem_limit_bytes=58 * 1024 * 1024)
PARAMS = pltpu.CompilerParams(vmem_limit_bytes=48 * 1024 * 1024)


def shift(x, axis, by):
    n = lax.axis_size(axis)
    return lax.ppermute(x, axis, [(i, (i + by) % n) for i in range(n)])


def after(x, *others):
    return lax.optimization_barrier((x, *others))[0]


def whole(shape):
    return pl.BlockSpec(shape, lambda *_: (0,) * len(shape))


def split_kernel(half_ref, in_ref, out_ref):
    exact = in_ref[...]
    high = exact.astype(BF16)
    out_ref[0, :, :COLS] = high
    out_ref[0, :, COLS:] = (exact - high.astype(F32)).astype(BF16)


def split_basis(half, basis):
    rows = 1024
    return pl.pallas_call(
        split_kernel,
        grid_spec=pltpu.PrefetchScalarGridSpec(
            num_scalar_prefetch=1,
            grid=(4,),
            in_specs=[pl.BlockSpec((rows, COLS), lambda g, half: (g * 2 + half[0], 0))],
            out_specs=pl.BlockSpec((1, rows, 256), lambda g, half: (g, 0, 0)),
        ),
        out_shape=jax.ShapeDtypeStruct((4, rows, 256), BF16),
        compiler_params=ALL_VMEM,
        cost_estimate=pl.CostEstimate(
            flops=1 << 20, bytes_accessed=4 << 20, transcendentals=0
        ),
    )(half, basis)


def rotate_ring_kernel(offsets, at_ref, *refs):
    blocks, (own_ref, other_ref, out_ref, lhs, sems) = refs[: len(offsets)], refs[len(offsets) :]

    @pl.when(pl.program_id(0) == 0)
    def _():
        turned = lax.rem(at_ref[1] + at_ref[4], 2)
        copies = []
        for i, (block, offset) in enumerate(zip(blocks, offsets)):
            for side in range(2):
                half = turned if side == 0 else 1 - turned
                at = (half * 8 + lax.rem(at_ref[0] + 8 + offset, 8)) * COLS
                lanes = pl.ds(pl.multiple_of(at, COLS), COLS)
                copies.append(
                    pltpu.make_async_copy(block.at[side], lhs.at[:, lanes], sems.at[i * 2 + side])
                )
        for copy in copies:
            copy.start()
        for copy in copies:
            copy.wait()

    both = jnp.dot(lhs[:, :1024], own_ref[0], preferred_element_type=F32)
    both += jnp.dot(lhs[:, 1024:], other_ref[0], preferred_element_type=F32)
    out_ref[0] = (both[:, :COLS] + both[:, COLS:]).T


def rotate_ring(at, ring, own, other):
    slab = pl.BlockSpec((1, 1024, 256), lambda g: (g, 0, 0))
    return pl.pallas_call(
        functools.partial(rotate_ring_kernel, [offset for _, offset in ring]),
        grid=(4,),
        out_shape=jax.ShapeDtypeStruct((4, COLS, TOK), F32),
        in_specs=[pl.BlockSpec(memory_space=pltpu.SMEM)]
        + [pl.BlockSpec(memory_space=pltpu.HBM)] * len(ring)
        + [slab, slab],
        out_specs=pl.BlockSpec((1, COLS, TOK), lambda g: (g, 0, 0)),
        scratch_shapes=[pltpu.VMEM((TOK, 2048), BF16), pltpu.SemaphoreType.DMA((16,))],
        compiler_params=ALL_VMEM,
        cost_estimate=pl.CostEstimate(
            flops=4 * TOK * 2048 * 512, bytes_accessed=7 << 20, transcendentals=0
        ),
    )(at, *[block for block, _ in ring], own, other)


def reach_kernel(rows_ref, in_ref, own_ref, near_ref, far_ref):
    def put(out_ref):
        exact = in_ref[...]
        high = exact.astype(BF16)
        out_ref[:, :COLS] = high
        out_ref[:, COLS:] = (exact - high.astype(F32)).astype(BF16)

    step = pl.program_id(0)
    pl.when(step < 2)(lambda: put(own_ref))
    pl.when((step >= 2) & (step < 4))(lambda: put(near_ref))
    pl.when(step == 4)(lambda: put(far_ref))


def reach_basis(rows, basis):
    return pl.pallas_call(
        reach_kernel,
        grid_spec=pltpu.PrefetchScalarGridSpec(
            num_scalar_prefetch=1,
            grid=(5,),
            in_specs=[pl.BlockSpec((1024, COLS), lambda g, rows: (rows[g], 0))],
            out_specs=[
                pl.BlockSpec((1024, 256), lambda g, rows: (jnp.minimum(g, 1), 0)),
                pl.BlockSpec((1024, 256), lambda g, rows: (jnp.clip(g - 2, 0, 1), 0)),
                pl.BlockSpec((1024, 256), lambda g, rows: (0, 0)),
            ],
        ),
        out_shape=[jax.ShapeDtypeStruct((n, 256), BF16) for n in (2048, 2048, 1024)],
        compiler_params=ALL_VMEM,
        cost_estimate=pl.CostEstimate(
            flops=1 << 20, bytes_accessed=5 << 20, transcendentals=0
        ),
    )(rows, basis)


def rotate_kernel(at_ref, block_ref, *refs):
    own_ref, near_ref, near_swapped, far_ref, far_swapped, out_ref, lhs, sems = refs
    xh, y, c = at_ref[1], at_ref[2], at_ref[4]
    copies = []
    for z in range(8):
        for side in range(2):
            at = ((xh if side == 0 else 1 - xh) * 8 + z) * COLS
            lanes = pl.ds(pl.multiple_of(at, COLS), COLS)
            copies.append(
                pltpu.make_async_copy(block_ref.at[z, side], lhs.at[:, lanes], sems.at[z * 2 + side])
            )
    for copy in copies:
        copy.start()
    for copy in copies:
        copy.wait()

    def put(place, both):
        out_ref[lax.rem(place, 4)] = (both[:, :COLS] + both[:, COLS:]).T

    for offset, ref in ((4, own_ref), (3 + 2 * c, near_ref), (5 - 2 * c, near_swapped)):
        put(y + offset, jnp.dot(lhs[...], ref[...], preferred_element_type=F32))
    mine = lhs[:, pl.ds(pl.multiple_of(c * 1024, 1024), 1024)]
    rest = lhs[:, pl.ds(pl.multiple_of((1 - c) * 1024, 1024), 1024)]
    both = jnp.dot(mine, far_ref[...], preferred_element_type=F32)
    put(y + 2, both + jnp.dot(rest, far_swapped[...], preferred_element_type=F32))


def rotate(at, blocks, slabs):
    return pl.pallas_call(
        rotate_kernel,
        out_shape=jax.ShapeDtypeStruct((4, COLS, TOK), F32),
        in_specs=[pl.BlockSpec(memory_space=pltpu.SMEM), pl.BlockSpec(memory_space=pltpu.HBM)]
        + [pl.BlockSpec(memory_space=pltpu.VMEM)] * 5,
        out_specs=pl.BlockSpec(memory_space=pltpu.VMEM),
        scratch_shapes=[pltpu.VMEM((TOK, 2048), BF16), pltpu.SemaphoreType.DMA((16,))],
        compiler_params=PARAMS,
        cost_estimate=pl.CostEstimate(
            flops=4 * TOK * 2048 * 512, bytes_accessed=7 << 20, transcendentals=0
        ),
    )(at, blocks, *slabs)


def product_kernel(scale, at_ref, acts_ref, own_ref, other_ref, out_ref, right):
    xh, c = at_ref[1], at_ref[4]
    for z in range(8):
        for side in range(2):
            place = (xh if side == 0 else 1 - xh) * 8 + z
            for s in range(4):
                right[s, pl.ds(pl.multiple_of(place * 32, 32), 32), :] = acts_ref[z, side, s]
    for row in range(4):
        total = None
        for grads_ref, core in ((own_ref, c), (other_ref, 1 - c)):
            for side in range(2):
                part = lax.dot_general(
                    grads_ref[side, row],
                    right[side * 2 + core],
                    (((1,), (1,)), ((), ())),
                    preferred_element_type=F32,
                )
                total = part * part if total is None else total + part * part
        out_ref[row] = (total * scale).astype(BF16)


def products(at, acts, own, other, scale):
    return pl.pallas_call(
        functools.partial(product_kernel, scale),
        out_shape=jax.ShapeDtypeStruct((4, COLS, 512), BF16),
        in_specs=[pl.BlockSpec(memory_space=pltpu.SMEM)]
        + [pl.BlockSpec(memory_space=pltpu.VMEM)] * 3,
        out_specs=pl.BlockSpec(memory_space=pltpu.VMEM),
        scratch_shapes=[pltpu.VMEM((4, 512, TOK), BF16)],
        compiler_params=PARAMS,
        cost_estimate=pl.CostEstimate(
            flops=2 * 4 * 512 * 512 * TOK, bytes_accessed=5 << 20, transcendentals=0
        ),
    )(at, acts, own, other)


def weave_kernel(in_ref, out_ref):
    for tile in range(4):
        lanes = slice(tile * 32, tile * 32 + 32)
        out_ref[:, tile * COLS : (tile + 1) * COLS] = jnp.concatenate(
            [in_ref[q].astype(F32)[:, lanes] for q in range(4)], axis=1
        )


def weave(parts):
    return pl.pallas_call(
        weave_kernel,
        grid=(4,),
        out_shape=jax.ShapeDtypeStruct((COLS, 2048), F32),
        in_specs=[pl.BlockSpec((4, COLS, 128), lambda g: (0, 0, g))],
        out_specs=pl.BlockSpec((COLS, 512), lambda g: (0, g)),
        compiler_params=PARAMS,
    )(parts)


def sync(*arrays):
    return lax.optimization_barrier(arrays)


def pair(x):
    return jnp.concatenate([x, shift(x, "xh", 1)])


def ring_step(up, down):
    return shift(up, "z", 1), shift(down, "z", -1)


def shift_near(x):
    pairs = [(i, (i + 1) % 4) for i in range(4)] + [(4 + i, 4 + (i + 3) % 4) for i in range(4)]
    return lax.ppermute(x, ("c", "y"), pairs)


def body(activations, gradients, basis_in, basis_out):
    z, xh, y, xl, c = (lax.axis_index(a) for a in ("z", "xh", "y", "xl", "c"))
    at = jnp.stack([z, xh, y, xl, c]).astype(jnp.int32)
    half = c.astype(jnp.int32).reshape(1)
    near_y, far_y = (y + 1 + 2 * c) % 4, (y + 2) % 4
    rows = jnp.stack(
        [y * 2, y * 2 + 1, near_y * 2, near_y * 2 + 1, far_y * 2 + c]
    ).astype(jnp.int32)

    a0, grads_pair, mine_in, basis_out = sync(
        pair(activations), pair(gradients), split_basis(half, basis_in), basis_out
    )
    own_in = lax.all_to_all(mine_in, "y", 0, 0)
    own_out, near_out, far_out = reach_basis(rows, basis_out)
    up1, down1, near_out, far_out = sync(*ring_step(a0, a0), near_out, far_out)
    up2, down2, own_in, near_out, far_out = sync(
        *ring_step(up1, down1), own_in, near_out, far_out
    )
    near_out = shift_near(near_out)
    up3, down3, other_in = sync(*ring_step(up2, down2), shift(own_in, "c", 1))
    grad_blocks = lax.all_gather(after(grads_pair, up2), "z")
    far_out = shift(far_out, "y", 2)
    up4 = shift(up3, "z", 1)
    ring = [(a0, 0), (up1, -1), (down1, 1), (up2, -2), (down2, 2), (up3, -3), (down3, 3), (up4, -4)]
    acts_part = rotate_ring(at, ring, own_in, other_in)
    near_out, far_out, acts_part = sync(near_out, far_out, acts_part)
    acts_in = lax.all_to_all(acts_part.reshape(16, 32, TOK), ("xl", "c", "y"), 0, 0)
    near_out2, far_out2 = shift(near_out, "c", 1), shift(far_out, "c", 1)
    grads_part = rotate(at, grad_blocks, (own_out, near_out, near_out2, far_out, far_out2))
    acts_in, grads_part = sync(acts_in, grads_part)

    acts = jnp.sum(acts_in.reshape(4, 4, 32, TOK), axis=1).astype(BF16)[None]
    rot_acts = lax.all_gather(pair(acts), "z")

    grads_in = lax.all_to_all(grads_part, "y", 0, 0)
    grads = jnp.sum(grads_in, axis=0).astype(BF16)
    copies = jnp.broadcast_to(grads, (8, COLS, TOK))
    rot_own = lax.all_to_all(copies, ("xl", "y"), 0, 0).reshape(2, 4, COLS, TOK)
    rot_other = shift(rot_own, "c", 1)

    part = products(at, rot_acts, rot_own, rot_other, 1.0 / (TOK * 4))
    return weave(lax.all_to_all(part, "y", 0, 0))


def solution(mesh):
    fine = Mesh(mesh.devices.reshape(SIZES), AXES)
    return jax.shard_map(
        body,
        mesh=fine,
        in_specs=(P(DP, None, TILE), P(DP, None, TILE), P(None, TILE), P(None, TILE)),
        out_specs=P(TILE, DP),
        check_vma=False,
    )
```

```python
import functools

import jax
import jax.numpy as jnp
from jax import lax
from jax.experimental import pallas as pl
from jax.experimental.pallas import tpu as pltpu
from jax.sharding import Mesh, PartitionSpec as P

AXES = ("xl", "c", "y", "xh", "z")
SIZES = (2, 2, 4, 2, 8)
DP = ("xl", "c")
TILE = ("y", "xh", "z")
TOK = 512
COLS = 128
F32 = jnp.float32
BF16 = jnp.bfloat16
ALL_VMEM = pltpu.CompilerParams(vmem_limit_bytes=58 * 1024 * 1024)
PARAMS = pltpu.CompilerParams(vmem_limit_bytes=48 * 1024 * 1024)


def shift(x, axis, by):
    n = lax.axis_size(axis)
    return lax.ppermute(x, axis, [(i, (i + by) % n) for i in range(n)])


def after(x, *others):
    return lax.optimization_barrier((x, *others))[0]


def whole(shape):
    return pl.BlockSpec(shape, lambda *_: (0,) * len(shape))


def split_kernel(half_ref, in_ref, out_ref):
    exact = in_ref[...]
    high = exact.astype(BF16)
    out_ref[0, :, :COLS] = high
    out_ref[0, :, COLS:] = (exact - high.astype(F32)).astype(BF16)


def split_basis(half, basis):
    rows = 1024
    return pl.pallas_call(
        split_kernel,
        grid_spec=pltpu.PrefetchScalarGridSpec(
            num_scalar_prefetch=1,
            grid=(4,),
            in_specs=[pl.BlockSpec((rows, COLS), lambda g, half: (g * 2 + half[0], 0))],
            out_specs=pl.BlockSpec((1, rows, 256), lambda g, half: (g, 0, 0)),
        ),
        out_shape=jax.ShapeDtypeStruct((4, rows, 256), BF16),
        compiler_params=ALL_VMEM,
        cost_estimate=pl.CostEstimate(
            flops=1 << 20, bytes_accessed=4 << 20, transcendentals=0
        ),
    )(half, basis)


def rotate_ring_kernel(offsets, at_ref, *refs):
    blocks, (own_ref, other_ref, out_ref, lhs, sems) = refs[: len(offsets)], refs[len(offsets) :]

    @pl.when(pl.program_id(0) == 0)
    def _():
        turned = lax.rem(at_ref[1] + at_ref[4], 2)
        copies = []
        for i, (block, offset) in enumerate(zip(blocks, offsets)):
            for side in range(2):
                half = turned if side == 0 else 1 - turned
                at = (half * 8 + lax.rem(at_ref[0] + 8 + offset, 8)) * COLS
                lanes = pl.ds(pl.multiple_of(at, COLS), COLS)
                copies.append(
                    pltpu.make_async_copy(block.at[side], lhs.at[:, lanes], sems.at[i * 2 + side])
                )
        for copy in copies:
            copy.start()
        for copy in copies:
            copy.wait()

    both = jnp.dot(lhs[:, :1024], own_ref[0], preferred_element_type=F32)
    both += jnp.dot(lhs[:, 1024:], other_ref[0], preferred_element_type=F32)
    out_ref[0] = (both[:, :COLS] + both[:, COLS:]).T


def rotate_ring(at, ring, own, other):
    slab = pl.BlockSpec((1, 1024, 256), lambda g: (g, 0, 0))
    return pl.pallas_call(
        functools.partial(rotate_ring_kernel, [offset for _, offset in ring]),
        grid=(4,),
        out_shape=jax.ShapeDtypeStruct((4, COLS, TOK), F32),
        in_specs=[pl.BlockSpec(memory_space=pltpu.SMEM)]
        + [pl.BlockSpec(memory_space=pltpu.HBM)] * len(ring)
        + [slab, slab],
        out_specs=pl.BlockSpec((1, COLS, TOK), lambda g: (g, 0, 0)),
        scratch_shapes=[pltpu.VMEM((TOK, 2048), BF16), pltpu.SemaphoreType.DMA((16,))],
        compiler_params=ALL_VMEM,
        cost_estimate=pl.CostEstimate(
            flops=4 * TOK * 2048 * 512, bytes_accessed=7 << 20, transcendentals=0
        ),
    )(at, *[block for block, _ in ring], own, other)


def reach_kernel(rows_ref, in_ref, own_ref, near_ref, far_ref):
    def put(out_ref):
        exact = in_ref[...]
        high = exact.astype(BF16)
        out_ref[:, :COLS] = high
        out_ref[:, COLS:] = (exact - high.astype(F32)).astype(BF16)

    step = pl.program_id(0)
    pl.when(step < 2)(lambda: put(own_ref))
    pl.when((step >= 2) & (step < 4))(lambda: put(near_ref))
    pl.when(step == 4)(lambda: put(far_ref))


def reach_basis(rows, basis):
    return pl.pallas_call(
        reach_kernel,
        grid_spec=pltpu.PrefetchScalarGridSpec(
            num_scalar_prefetch=1,
            grid=(5,),
            in_specs=[pl.BlockSpec((1024, COLS), lambda g, rows: (rows[g], 0))],
            out_specs=[
                pl.BlockSpec((1024, 256), lambda g, rows: (jnp.minimum(g, 1), 0)),
                pl.BlockSpec((1024, 256), lambda g, rows: (jnp.clip(g - 2, 0, 1), 0)),
                pl.BlockSpec((1024, 256), lambda g, rows: (0, 0)),
            ],
        ),
        out_shape=[jax.ShapeDtypeStruct((n, 256), BF16) for n in (2048, 2048, 1024)],
        compiler_params=ALL_VMEM,
        cost_estimate=pl.CostEstimate(
            flops=1 << 20, bytes_accessed=5 << 20, transcendentals=0
        ),
    )(rows, basis)


def rotate_kernel(at_ref, block_ref, *refs):
    own_ref, near_ref, near_swapped, far_ref, far_swapped, out_ref, lhs, sems = refs
    xh, y, c = at_ref[1], at_ref[2], at_ref[4]
    copies = []
    for z in range(8):
        for side in range(2):
            at = ((xh if side == 0 else 1 - xh) * 8 + z) * COLS
            lanes = pl.ds(pl.multiple_of(at, COLS), COLS)
            copies.append(
                pltpu.make_async_copy(block_ref.at[z, side], lhs.at[:, lanes], sems.at[z * 2 + side])
            )
    for copy in copies:
        copy.start()
    for copy in copies:
        copy.wait()

    def put(place, both):
        out_ref[lax.rem(place, 4)] = (both[:, :COLS] + both[:, COLS:]).T

    for offset, ref in ((4, own_ref), (3 + 2 * c, near_ref), (5 - 2 * c, near_swapped)):
        put(y + offset, jnp.dot(lhs[...], ref[...], preferred_element_type=F32))
    mine = lhs[:, pl.ds(pl.multiple_of(c * 1024, 1024), 1024)]
    rest = lhs[:, pl.ds(pl.multiple_of((1 - c) * 1024, 1024), 1024)]
    both = jnp.dot(mine, far_ref[...], preferred_element_type=F32)
    put(y + 2, both + jnp.dot(rest, far_swapped[...], preferred_element_type=F32))


def rotate(at, blocks, slabs):
    return pl.pallas_call(
        rotate_kernel,
        out_shape=jax.ShapeDtypeStruct((4, COLS, TOK), F32),
        in_specs=[pl.BlockSpec(memory_space=pltpu.SMEM), pl.BlockSpec(memory_space=pltpu.HBM)]
        + [pl.BlockSpec(memory_space=pltpu.VMEM)] * 5,
        out_specs=pl.BlockSpec(memory_space=pltpu.VMEM),
        scratch_shapes=[pltpu.VMEM((TOK, 2048), BF16), pltpu.SemaphoreType.DMA((16,))],
        compiler_params=PARAMS,
        cost_estimate=pl.CostEstimate(
            flops=4 * TOK * 2048 * 512, bytes_accessed=7 << 20, transcendentals=0
        ),
    )(at, blocks, *slabs)


def product_kernel(scale, at_ref, acts_ref, own_ref, other_ref, out_ref, right):
    xh, c = at_ref[1], at_ref[4]
    for z in range(8):
        for side in range(2):
            place = (xh if side == 0 else 1 - xh) * 8 + z
            for s in range(4):
                right[s, pl.ds(pl.multiple_of(place * 32, 32), 32), :] = acts_ref[z, side, s]
    for row in range(4):
        total = None
        for grads_ref, core in ((own_ref, c), (other_ref, 1 - c)):
            for side in range(2):
                part = lax.dot_general(
                    grads_ref[side, row],
                    right[side * 2 + core],
                    (((1,), (1,)), ((), ())),
                    preferred_element_type=F32,
                )
                total = part * part if total is None else total + part * part
        out_ref[row] = (total * scale).astype(BF16)


def products(at, acts, own, other, scale):
    return pl.pallas_call(
        functools.partial(product_kernel, scale),
        out_shape=jax.ShapeDtypeStruct((4, COLS, 512), BF16),
        in_specs=[pl.BlockSpec(memory_space=pltpu.SMEM)]
        + [pl.BlockSpec(memory_space=pltpu.VMEM)] * 3,
        out_specs=pl.BlockSpec(memory_space=pltpu.VMEM),
        scratch_shapes=[pltpu.VMEM((4, 512, TOK), BF16)],
        compiler_params=PARAMS,
        cost_estimate=pl.CostEstimate(
            flops=2 * 4 * 512 * 512 * TOK, bytes_accessed=5 << 20, transcendentals=0
        ),
    )(at, acts, own, other)


def weave_kernel(in_ref, out_ref):
    for tile in range(4):
        lanes = slice(tile * 32, tile * 32 + 32)
        out_ref[:, tile * COLS : (tile + 1) * COLS] = jnp.concatenate(
            [in_ref[q].astype(F32)[:, lanes] for q in range(4)], axis=1
        )


def weave(parts):
    return pl.pallas_call(
        weave_kernel,
        grid=(4,),
        out_shape=jax.ShapeDtypeStruct((COLS, 2048), F32),
        in_specs=[pl.BlockSpec((4, COLS, 128), lambda g: (0, 0, g))],
        out_specs=pl.BlockSpec((COLS, 512), lambda g: (0, g)),
        compiler_params=PARAMS,
    )(parts)


def sync(*arrays):
    return lax.optimization_barrier(arrays)


def pair(x):
    return jnp.concatenate([x, shift(x, "xh", 1)])


def ring_step(up, down):
    return shift(up, "z", 1), shift(down, "z", -1)


def shift_near(x):
    pairs = [(i, (i + 1) % 4) for i in range(4)] + [(4 + i, 4 + (i + 3) % 4) for i in range(4)]
    return lax.ppermute(x, ("c", "y"), pairs)


def body(activations, gradients, basis_in, basis_out):
    z, xh, y, xl, c = (lax.axis_index(a) for a in ("z", "xh", "y", "xl", "c"))
    at = jnp.stack([z, xh, y, xl, c]).astype(jnp.int32)
    half = c.astype(jnp.int32).reshape(1)
    near_y, far_y = (y + 1 + 2 * c) % 4, (y + 2) % 4
    rows = jnp.stack(
        [y * 2, y * 2 + 1, near_y * 2, near_y * 2 + 1, far_y * 2 + c]
    ).astype(jnp.int32)

    a0, gradients, mine_in, basis_out = sync(
        pair(activations), gradients, split_basis(half, basis_in), basis_out
    )
    own_in = lax.all_to_all(mine_in, "y", 0, 0)
    own_out, near_out, far_out = reach_basis(rows, basis_out)
    up1, down1, grads_pair, near_out, far_out = sync(
        *ring_step(a0, a0), pair(gradients), near_out, far_out
    )
    up2, down2, near_out, far_out = sync(*ring_step(up1, down1), near_out, far_out)
    near_out = shift_near(near_out)
    up3, down3, own_in, far_out = sync(*ring_step(up2, down2), own_in, far_out)
    grad_blocks = lax.all_gather(after(grads_pair, up2), "z")
    far_out = shift(far_out, "y", 2)
    up4, other_in = sync(shift(up3, "z", 1), shift(own_in, "c", 1))
    ring = [(a0, 0), (up1, -1), (down1, 1), (up2, -2), (down2, 2), (up3, -3), (down3, 3), (up4, -4)]
    acts_part = rotate_ring(at, ring, own_in, other_in)
    near_out, far_out, acts_part = sync(near_out, far_out, acts_part)
    acts_in = lax.all_to_all(acts_part.reshape(16, 32, TOK), ("xl", "c", "y"), 0, 0)
    near_out2, far_out2 = shift(near_out, "c", 1), shift(far_out, "c", 1)
    grads_part = rotate(at, grad_blocks, (own_out, near_out, near_out2, far_out, far_out2))
    acts_in, grads_part = sync(acts_in, grads_part)

    acts = jnp.sum(acts_in.reshape(4, 4, 32, TOK), axis=1).astype(BF16)[None]
    rot_acts = lax.all_gather(pair(acts), "z")

    grads_in = lax.all_to_all(grads_part, "y", 0, 0)
    grads = jnp.sum(grads_in, axis=0).astype(BF16)
    copies = jnp.broadcast_to(grads, (8, COLS, TOK))
    rot_own = lax.all_to_all(copies, ("xl", "y"), 0, 0).reshape(2, 4, COLS, TOK)
    rot_other = shift(rot_own, "c", 1)

    part = products(at, rot_acts, rot_own, rot_other, 1.0 / (TOK * 4))
    return weave(lax.all_to_all(part, "y", 0, 0))


def solution(mesh):
    fine = Mesh(mesh.devices.reshape(SIZES), AXES)
    return jax.shard_map(
        body,
        mesh=fine,
        in_specs=(P(DP, None, TILE), P(DP, None, TILE), P(None, TILE), P(None, TILE)),
        out_specs=P(TILE, DP),
        check_vma=False,
    )
```

```python
import functools

import jax
import jax.numpy as jnp
from jax import lax
from jax.experimental import pallas as pl
from jax.experimental.pallas import tpu as pltpu
from jax.sharding import Mesh, PartitionSpec as P

AXES = ("xl", "c", "y", "xh", "z")
SIZES = (2, 2, 4, 2, 8)
DP = ("xl", "c")
TILE = ("y", "xh", "z")
TOK = 512
COLS = 128
F32 = jnp.float32
BF16 = jnp.bfloat16
ALL_VMEM = pltpu.CompilerParams(vmem_limit_bytes=58 * 1024 * 1024)
PARAMS = pltpu.CompilerParams(vmem_limit_bytes=48 * 1024 * 1024)


def shift(x, axis, by):
    n = lax.axis_size(axis)
    return lax.ppermute(x, axis, [(i, (i + by) % n) for i in range(n)])


def after(x, *others):
    return lax.optimization_barrier((x, *others))[0]


def whole(shape):
    return pl.BlockSpec(shape, lambda *_: (0,) * len(shape))


def split_kernel(half_ref, in_ref, out_ref):
    exact = in_ref[...]
    high = exact.astype(BF16)
    out_ref[0, :, :COLS] = high
    out_ref[0, :, COLS:] = (exact - high.astype(F32)).astype(BF16)


def split_basis(half, basis):
    rows = 1024
    return pl.pallas_call(
        split_kernel,
        grid_spec=pltpu.PrefetchScalarGridSpec(
            num_scalar_prefetch=1,
            grid=(4,),
            in_specs=[pl.BlockSpec((rows, COLS), lambda g, half: (g * 2 + half[0], 0))],
            out_specs=pl.BlockSpec((1, rows, 256), lambda g, half: (g, 0, 0)),
        ),
        out_shape=jax.ShapeDtypeStruct((4, rows, 256), BF16),
        compiler_params=ALL_VMEM,
        cost_estimate=pl.CostEstimate(
            flops=1 << 20, bytes_accessed=4 << 20, transcendentals=0
        ),
    )(half, basis)


def rotate_ring_kernel(offsets, at_ref, *refs):
    blocks, (own_ref, other_ref, out_ref, lhs, sems) = refs[: len(offsets)], refs[len(offsets) :]

    @pl.when(pl.program_id(0) == 0)
    def _():
        turned = lax.rem(at_ref[1] + at_ref[4], 2)
        copies = []
        for i, (block, offset) in enumerate(zip(blocks, offsets)):
            for side in range(2):
                half = turned if side == 0 else 1 - turned
                at = (half * 8 + lax.rem(at_ref[0] + 8 + offset, 8)) * COLS
                lanes = pl.ds(pl.multiple_of(at, COLS), COLS)
                copies.append(
                    pltpu.make_async_copy(block.at[side], lhs.at[:, lanes], sems.at[i * 2 + side])
                )
        for copy in copies:
            copy.start()
        for copy in copies:
            copy.wait()

    both = jnp.dot(lhs[:, :1024], own_ref[0], preferred_element_type=F32)
    both += jnp.dot(lhs[:, 1024:], other_ref[0], preferred_element_type=F32)
    out_ref[0] = (both[:, :COLS] + both[:, COLS:]).T


def rotate_ring(at, ring, own, other):
    slab = pl.BlockSpec((1, 1024, 256), lambda g: (g, 0, 0))
    return pl.pallas_call(
        functools.partial(rotate_ring_kernel, [offset for _, offset in ring]),
        grid=(4,),
        out_shape=jax.ShapeDtypeStruct((4, COLS, TOK), F32),
        in_specs=[pl.BlockSpec(memory_space=pltpu.SMEM)]
        + [pl.BlockSpec(memory_space=pltpu.HBM)] * len(ring)
        + [slab, slab],
        out_specs=pl.BlockSpec((1, COLS, TOK), lambda g: (g, 0, 0)),
        scratch_shapes=[pltpu.VMEM((TOK, 2048), BF16), pltpu.SemaphoreType.DMA((16,))],
        compiler_params=ALL_VMEM,
        cost_estimate=pl.CostEstimate(
            flops=4 * TOK * 2048 * 512, bytes_accessed=7 << 20, transcendentals=0
        ),
    )(at, *[block for block, _ in ring], own, other)


def split_rows_kernel(rows_ref, in_ref, out_ref):
    exact = in_ref[...]
    high = exact.astype(BF16)
    out_ref[:, :COLS] = high
    out_ref[:, COLS:] = (exact - high.astype(F32)).astype(BF16)


def split_rows(rows, basis):
    count = len(rows)
    return pl.pallas_call(
        split_rows_kernel,
        grid_spec=pltpu.PrefetchScalarGridSpec(
            num_scalar_prefetch=1,
            grid=(count,),
            in_specs=[pl.BlockSpec((1024, COLS), lambda g, rows: (rows[g], 0))],
            out_specs=pl.BlockSpec((1024, 256), lambda g, rows: (g, 0)),
        ),
        out_shape=jax.ShapeDtypeStruct((count * 1024, 256), BF16),
        compiler_params=ALL_VMEM,
        cost_estimate=pl.CostEstimate(
            flops=count << 18, bytes_accessed=count << 20, transcendentals=0
        ),
    )(jnp.stack(rows).astype(jnp.int32), basis)


def rotate_kernel(at_ref, block_ref, *refs):
    own_ref, near_ref, near_swapped, far_ref, far_swapped, out_ref, lhs, sems = refs
    xh, y, c = at_ref[1], at_ref[2], at_ref[4]
    copies = []
    for z in range(8):
        for side in range(2):
            at = ((xh if side == 0 else 1 - xh) * 8 + z) * COLS
            lanes = pl.ds(pl.multiple_of(at, COLS), COLS)
            copies.append(
                pltpu.make_async_copy(block_ref.at[z, side], lhs.at[:, lanes], sems.at[z * 2 + side])
            )
    for copy in copies:
        copy.start()
    for copy in copies:
        copy.wait()

    def put(place, both):
        out_ref[lax.rem(place, 4)] = (both[:, :COLS] + both[:, COLS:]).T

    for offset, ref in ((4, own_ref), (3 + 2 * c, near_ref), (5 - 2 * c, near_swapped)):
        put(y + offset, jnp.dot(lhs[...], ref[...], preferred_element_type=F32))
    mine = lhs[:, pl.ds(pl.multiple_of(c * 1024, 1024), 1024)]
    rest = lhs[:, pl.ds(pl.multiple_of((1 - c) * 1024, 1024), 1024)]
    both = jnp.dot(mine, far_ref[...], preferred_element_type=F32)
    put(y + 2, both + jnp.dot(rest, far_swapped[...], preferred_element_type=F32))


def rotate(at, blocks, slabs):
    return pl.pallas_call(
        rotate_kernel,
        out_shape=jax.ShapeDtypeStruct((4, COLS, TOK), F32),
        in_specs=[pl.BlockSpec(memory_space=pltpu.SMEM), pl.BlockSpec(memory_space=pltpu.HBM)]
        + [pl.BlockSpec(memory_space=pltpu.VMEM)] * 5,
        out_specs=pl.BlockSpec(memory_space=pltpu.VMEM),
        scratch_shapes=[pltpu.VMEM((TOK, 2048), BF16), pltpu.SemaphoreType.DMA((16,))],
        compiler_params=PARAMS,
        cost_estimate=pl.CostEstimate(
            flops=4 * TOK * 2048 * 512, bytes_accessed=7 << 20, transcendentals=0
        ),
    )(at, blocks, *slabs)


def product_kernel(scale, at_ref, acts_ref, own_ref, other_ref, out_ref, right):
    xh, c = at_ref[1], at_ref[4]
    for z in range(8):
        for side in range(2):
            place = (xh if side == 0 else 1 - xh) * 8 + z
            for s in range(4):
                right[s, pl.ds(pl.multiple_of(place * 32, 32), 32), :] = acts_ref[z, side, s]
    for row in range(4):
        total = None
        for grads_ref, core in ((own_ref, c), (other_ref, 1 - c)):
            for side in range(2):
                part = lax.dot_general(
                    grads_ref[side, row],
                    right[side * 2 + core],
                    (((1,), (1,)), ((), ())),
                    preferred_element_type=F32,
                )
                total = part * part if total is None else total + part * part
        out_ref[row] = (total * scale).astype(BF16)


def products(at, acts, own, other, scale):
    return pl.pallas_call(
        functools.partial(product_kernel, scale),
        out_shape=jax.ShapeDtypeStruct((4, COLS, 512), BF16),
        in_specs=[pl.BlockSpec(memory_space=pltpu.SMEM)]
        + [pl.BlockSpec(memory_space=pltpu.VMEM)] * 3,
        out_specs=pl.BlockSpec(memory_space=pltpu.VMEM),
        scratch_shapes=[pltpu.VMEM((4, 512, TOK), BF16)],
        compiler_params=PARAMS,
        cost_estimate=pl.CostEstimate(
            flops=2 * 4 * 512 * 512 * TOK, bytes_accessed=5 << 20, transcendentals=0
        ),
    )(at, acts, own, other)


def weave_kernel(in_ref, out_ref):
    for tile in range(4):
        lanes = slice(tile * 32, tile * 32 + 32)
        out_ref[:, tile * COLS : (tile + 1) * COLS] = jnp.concatenate(
            [in_ref[q].astype(F32)[:, lanes] for q in range(4)], axis=1
        )


def weave(parts):
    return pl.pallas_call(
        weave_kernel,
        grid=(4,),
        out_shape=jax.ShapeDtypeStruct((COLS, 2048), F32),
        in_specs=[pl.BlockSpec((4, COLS, 128), lambda g: (0, 0, g))],
        out_specs=pl.BlockSpec((COLS, 512), lambda g: (0, g)),
        compiler_params=PARAMS,
    )(parts)


def sync(*arrays):
    return lax.optimization_barrier(arrays)


def pair(x):
    return jnp.concatenate([x, shift(x, "xh", 1)])


def ring_step(up, down):
    return shift(up, "z", 1), shift(down, "z", -1)


def shift_near(x):
    pairs = [(i, (i + 1) % 4) for i in range(4)] + [(4 + i, 4 + (i + 3) % 4) for i in range(4)]
    return lax.ppermute(x, ("c", "y"), pairs)


def body(activations, gradients, basis_in, basis_out):
    z, xh, y, xl, c = (lax.axis_index(a) for a in ("z", "xh", "y", "xl", "c"))
    at = jnp.stack([z, xh, y, xl, c]).astype(jnp.int32)
    half = c.astype(jnp.int32).reshape(1)
    near_y, far_y = (y + 1 + 2 * c) % 4, (y + 2) % 4

    a0, gradients, mine_in, basis_out = sync(
        pair(activations), gradients, split_basis(half, basis_in), basis_out
    )
    own_in = lax.all_to_all(mine_in, "y", 0, 0)
    near_out = split_rows([near_y * 2, near_y * 2 + 1], basis_out)
    up1, down1, grads_pair, near_out, basis_out = sync(
        *ring_step(a0, a0), pair(gradients), near_out, basis_out
    )
    own_out = split_rows([y * 2, y * 2 + 1], basis_out)
    far_out = split_rows([far_y * 2 + c], basis_out)
    up2, down2, own_out, near_out, far_out = sync(
        *ring_step(up1, down1), own_out, near_out, far_out
    )
    near_out = shift_near(near_out)
    up3, down3, own_in, far_out = sync(*ring_step(up2, down2), own_in, far_out)
    grad_blocks = lax.all_gather(after(grads_pair, up2), "z")
    far_out = shift(far_out, "y", 2)
    up4, other_in = sync(shift(up3, "z", 1), shift(own_in, "c", 1))
    ring = [(a0, 0), (up1, -1), (down1, 1), (up2, -2), (down2, 2), (up3, -3), (down3, 3), (up4, -4)]
    acts_part = rotate_ring(at, ring, own_in, other_in)
    near_out, far_out, acts_part = sync(near_out, far_out, acts_part)
    acts_in = lax.all_to_all(acts_part.reshape(16, 32, TOK), ("xl", "c", "y"), 0, 0)
    near_out2, far_out2 = shift(near_out, "c", 1), shift(far_out, "c", 1)
    grads_part = rotate(at, grad_blocks, (own_out, near_out, near_out2, far_out, far_out2))
    acts_in, grads_part = sync(acts_in, grads_part)

    acts = jnp.sum(acts_in.reshape(4, 4, 32, TOK), axis=1).astype(BF16)[None]
    rot_acts = lax.all_gather(pair(acts), "z")

    grads_in = lax.all_to_all(grads_part, "y", 0, 0)
    grads = jnp.sum(grads_in, axis=0).astype(BF16)
    copies = jnp.broadcast_to(grads, (8, COLS, TOK))
    rot_own = lax.all_to_all(copies, ("xl", "y"), 0, 0).reshape(2, 4, COLS, TOK)
    rot_other = shift(rot_own, "c", 1)

    part = products(at, rot_acts, rot_own, rot_other, 1.0 / (TOK * 4))
    return weave(lax.all_to_all(part, "y", 0, 0))


def solution(mesh):
    fine = Mesh(mesh.devices.reshape(SIZES), AXES)
    return jax.shard_map(
        body,
        mesh=fine,
        in_specs=(P(DP, None, TILE), P(DP, None, TILE), P(None, TILE), P(None, TILE)),
        out_specs=P(TILE, DP),
        check_vma=False,
    )
```

```python
import functools

import jax
import jax.numpy as jnp
from jax import lax
from jax.experimental import pallas as pl
from jax.experimental.pallas import tpu as pltpu
from jax.sharding import Mesh, PartitionSpec as P

AXES = ("xl", "c", "y", "xh", "z")
SIZES = (2, 2, 4, 2, 8)
DP = ("xl", "c")
TILE = ("y", "xh", "z")
TOK = 512
COLS = 128
F32 = jnp.float32
BF16 = jnp.bfloat16
ALL_VMEM = pltpu.CompilerParams(vmem_limit_bytes=58 * 1024 * 1024)
PARAMS = pltpu.CompilerParams(vmem_limit_bytes=48 * 1024 * 1024)


def shift(x, axis, by):
    n = lax.axis_size(axis)
    return lax.ppermute(x, axis, [(i, (i + by) % n) for i in range(n)])


def after(x, *others):
    return lax.optimization_barrier((x, *others))[0]


def whole(shape):
    return pl.BlockSpec(shape, lambda *_: (0,) * len(shape))


def split_kernel(half_ref, in_ref, out_ref):
    exact = in_ref[...]
    high = exact.astype(BF16)
    out_ref[0, :, :COLS] = high
    out_ref[0, :, COLS:] = (exact - high.astype(F32)).astype(BF16)


def split_basis(half, basis):
    rows = 1024
    return pl.pallas_call(
        split_kernel,
        grid_spec=pltpu.PrefetchScalarGridSpec(
            num_scalar_prefetch=1,
            grid=(4,),
            in_specs=[pl.BlockSpec((rows, COLS), lambda g, half: (g * 2 + half[0], 0))],
            out_specs=pl.BlockSpec((1, rows, 256), lambda g, half: (g, 0, 0)),
        ),
        out_shape=jax.ShapeDtypeStruct((4, rows, 256), BF16),
        compiler_params=ALL_VMEM,
        cost_estimate=pl.CostEstimate(
            flops=1 << 20, bytes_accessed=4 << 20, transcendentals=0
        ),
    )(half, basis)


def rotate_ring_kernel(offsets, at_ref, *refs):
    blocks, (own_ref, other_ref, out_ref, lhs, sems) = refs[: len(offsets)], refs[len(offsets) :]

    @pl.when(pl.program_id(0) == 0)
    def _():
        turned = lax.rem(at_ref[1] + at_ref[4], 2)
        copies = []
        for i, (block, offset) in enumerate(zip(blocks, offsets)):
            for side in range(2):
                half = turned if side == 0 else 1 - turned
                at = (half * 8 + lax.rem(at_ref[0] + 8 + offset, 8)) * COLS
                lanes = pl.ds(pl.multiple_of(at, COLS), COLS)
                copies.append(
                    pltpu.make_async_copy(block.at[side], lhs.at[:, lanes], sems.at[i * 2 + side])
                )
        for copy in copies:
            copy.start()
        for copy in copies:
            copy.wait()

    for i in range(2):
        both = jnp.dot(lhs[:, :1024], own_ref[i], preferred_element_type=F32)
        both += jnp.dot(lhs[:, 1024:], other_ref[i], preferred_element_type=F32)
        out_ref[i] = (both[:, :COLS] + both[:, COLS:]).T


def rotate_ring(at, ring, own, other):
    slab = pl.BlockSpec((2, 1024, 256), lambda g: (g, 0, 0))
    return pl.pallas_call(
        functools.partial(rotate_ring_kernel, [offset for _, offset in ring]),
        grid=(2,),
        out_shape=jax.ShapeDtypeStruct((4, COLS, TOK), F32),
        in_specs=[pl.BlockSpec(memory_space=pltpu.SMEM)]
        + [pl.BlockSpec(memory_space=pltpu.HBM)] * len(ring)
        + [slab, slab],
        out_specs=pl.BlockSpec((2, COLS, TOK), lambda g: (g, 0, 0)),
        scratch_shapes=[pltpu.VMEM((TOK, 2048), BF16), pltpu.SemaphoreType.DMA((16,))],
        compiler_params=ALL_VMEM,
        cost_estimate=pl.CostEstimate(
            flops=4 * TOK * 2048 * 512, bytes_accessed=7 << 20, transcendentals=0
        ),
    )(at, *[block for block, _ in ring], own, other)


def split_rows_kernel(rows_ref, in_ref, out_ref):
    exact = in_ref[...]
    high = exact.astype(BF16)
    out_ref[:, :COLS] = high
    out_ref[:, COLS:] = (exact - high.astype(F32)).astype(BF16)


def split_rows(rows, basis):
    count = len(rows)
    return pl.pallas_call(
        split_rows_kernel,
        grid_spec=pltpu.PrefetchScalarGridSpec(
            num_scalar_prefetch=1,
            grid=(count,),
            in_specs=[pl.BlockSpec((1024, COLS), lambda g, rows: (rows[g], 0))],
            out_specs=pl.BlockSpec((1024, 256), lambda g, rows: (g, 0)),
        ),
        out_shape=jax.ShapeDtypeStruct((count * 1024, 256), BF16),
        compiler_params=ALL_VMEM,
        cost_estimate=pl.CostEstimate(
            flops=count << 18, bytes_accessed=count << 20, transcendentals=0
        ),
    )(jnp.stack(rows).astype(jnp.int32), basis)


def rotate_kernel(at_ref, block_ref, *refs):
    own_ref, near_ref, near_swapped, far_ref, far_swapped, out_ref, lhs, sems = refs
    xh, y, c = at_ref[1], at_ref[2], at_ref[4]
    copies = []
    for z in range(8):
        for side in range(2):
            at = ((xh if side == 0 else 1 - xh) * 8 + z) * COLS
            lanes = pl.ds(pl.multiple_of(at, COLS), COLS)
            copies.append(
                pltpu.make_async_copy(block_ref.at[z, side], lhs.at[:, lanes], sems.at[z * 2 + side])
            )
    for copy in copies:
        copy.start()
    for copy in copies:
        copy.wait()

    def put(place, both):
        out_ref[lax.rem(place, 4)] = (both[:, :COLS] + both[:, COLS:]).T

    for offset, ref in ((4, own_ref), (3 + 2 * c, near_ref), (5 - 2 * c, near_swapped)):
        put(y + offset, jnp.dot(lhs[...], ref[...], preferred_element_type=F32))
    mine = lhs[:, pl.ds(pl.multiple_of(c * 1024, 1024), 1024)]
    rest = lhs[:, pl.ds(pl.multiple_of((1 - c) * 1024, 1024), 1024)]
    both = jnp.dot(mine, far_ref[...], preferred_element_type=F32)
    put(y + 2, both + jnp.dot(rest, far_swapped[...], preferred_element_type=F32))


def rotate(at, blocks, slabs):
    return pl.pallas_call(
        rotate_kernel,
        out_shape=jax.ShapeDtypeStruct((4, COLS, TOK), F32),
        in_specs=[pl.BlockSpec(memory_space=pltpu.SMEM), pl.BlockSpec(memory_space=pltpu.HBM)]
        + [pl.BlockSpec(memory_space=pltpu.VMEM)] * 5,
        out_specs=pl.BlockSpec(memory_space=pltpu.VMEM),
        scratch_shapes=[pltpu.VMEM((TOK, 2048), BF16), pltpu.SemaphoreType.DMA((16,))],
        compiler_params=PARAMS,
        cost_estimate=pl.CostEstimate(
            flops=4 * TOK * 2048 * 512, bytes_accessed=7 << 20, transcendentals=0
        ),
    )(at, blocks, *slabs)


def product_kernel(scale, at_ref, acts_ref, own_ref, other_ref, out_ref, right):
    xh, c = at_ref[1], at_ref[4]
    for z in range(8):
        for side in range(2):
            place = (xh if side == 0 else 1 - xh) * 8 + z
            for s in range(4):
                right[s, pl.ds(pl.multiple_of(place * 32, 32), 32), :] = acts_ref[z, side, s]
    for row in range(4):
        total = None
        for grads_ref, core in ((own_ref, c), (other_ref, 1 - c)):
            for side in range(2):
                part = lax.dot_general(
                    grads_ref[side, row],
                    right[side * 2 + core],
                    (((1,), (1,)), ((), ())),
                    preferred_element_type=F32,
                )
                total = part * part if total is None else total + part * part
        out_ref[row] = (total * scale).astype(BF16)


def products(at, acts, own, other, scale):
    return pl.pallas_call(
        functools.partial(product_kernel, scale),
        out_shape=jax.ShapeDtypeStruct((4, COLS, 512), BF16),
        in_specs=[pl.BlockSpec(memory_space=pltpu.SMEM)]
        + [pl.BlockSpec(memory_space=pltpu.VMEM)] * 3,
        out_specs=pl.BlockSpec(memory_space=pltpu.VMEM),
        scratch_shapes=[pltpu.VMEM((4, 512, TOK), BF16)],
        compiler_params=PARAMS,
        cost_estimate=pl.CostEstimate(
            flops=2 * 4 * 512 * 512 * TOK, bytes_accessed=5 << 20, transcendentals=0
        ),
    )(at, acts, own, other)


def weave_kernel(in_ref, out_ref):
    for tile in range(8):
        lanes = slice(tile * 32, tile * 32 + 32)
        out_ref[:, tile * COLS : (tile + 1) * COLS] = jnp.concatenate(
            [in_ref[q].astype(F32)[:, lanes] for q in range(4)], axis=1
        )


def weave(parts):
    return pl.pallas_call(
        weave_kernel,
        grid=(2,),
        out_shape=jax.ShapeDtypeStruct((COLS, 2048), F32),
        in_specs=[pl.BlockSpec((4, COLS, 256), lambda g: (0, 0, g))],
        out_specs=pl.BlockSpec((COLS, 1024), lambda g: (0, g)),
        compiler_params=PARAMS,
    )(parts)


def sync(*arrays):
    return lax.optimization_barrier(arrays)


def pair(x):
    return jnp.concatenate([x, shift(x, "xh", 1)])


def ring_step(up, down):
    return shift(up, "z", 1), shift(down, "z", -1)


def shift_near(x):
    pairs = [(i, (i + 1) % 4) for i in range(4)] + [(4 + i, 4 + (i + 3) % 4) for i in range(4)]
    return lax.ppermute(x, ("c", "y"), pairs)


def body(activations, gradients, basis_in, basis_out):
    z, xh, y, xl, c = (lax.axis_index(a) for a in ("z", "xh", "y", "xl", "c"))
    at = jnp.stack([z, xh, y, xl, c]).astype(jnp.int32)
    half = c.astype(jnp.int32).reshape(1)
    near_y, far_y = (y + 1 + 2 * c) % 4, (y + 2) % 4

    a0, gradients, mine_in, basis_out = sync(
        pair(activations), gradients, split_basis(half, basis_in), basis_out
    )
    own_in = lax.all_to_all(mine_in, "y", 0, 0)
    near_out = split_rows([near_y * 2, near_y * 2 + 1], basis_out)
    up1, down1, grads_pair, near_out, basis_out = sync(
        *ring_step(a0, a0), pair(gradients), near_out, basis_out
    )
    own_out = split_rows([y * 2, y * 2 + 1], basis_out)
    far_out = split_rows([far_y * 2 + c], basis_out)
    up2, down2, own_out, near_out, far_out = sync(
        *ring_step(up1, down1), own_out, near_out, far_out
    )
    near_out = shift_near(near_out)
    up3, down3, own_in, far_out = sync(*ring_step(up2, down2), own_in, far_out)
    grad_blocks = lax.all_gather(after(grads_pair, up2), "z")
    far_out = shift(far_out, "y", 2)
    up4, other_in = sync(shift(up3, "z", 1), shift(own_in, "c", 1))
    ring = [(a0, 0), (up1, -1), (down1, 1), (up2, -2), (down2, 2), (up3, -3), (down3, 3), (up4, -4)]
    acts_part = rotate_ring(at, ring, own_in, other_in)
    near_out, far_out, acts_part = sync(near_out, far_out, acts_part)
    acts_in = lax.all_to_all(acts_part.reshape(16, 32, TOK), ("xl", "c", "y"), 0, 0)
    near_out2, far_out2 = shift(near_out, "c", 1), shift(far_out, "c", 1)
    grads_part = rotate(at, grad_blocks, (own_out, near_out, near_out2, far_out, far_out2))
    acts_in, grads_part = sync(acts_in, grads_part)

    acts = jnp.sum(acts_in.reshape(4, 4, 32, TOK), axis=1).astype(BF16)[None]
    rot_acts = lax.all_gather(pair(acts), "z")

    grads_in = lax.all_to_all(grads_part, "y", 0, 0)
    grads = jnp.sum(grads_in, axis=0).astype(BF16)
    copies = jnp.broadcast_to(grads, (8, COLS, TOK))
    rot_own = lax.all_to_all(copies, ("xl", "y"), 0, 0).reshape(2, 4, COLS, TOK)
    rot_other = shift(rot_own, "c", 1)

    part = products(at, rot_acts, rot_own, rot_other, 1.0 / (TOK * 4))
    return weave(lax.all_to_all(part, "y", 0, 0))


def solution(mesh):
    fine = Mesh(mesh.devices.reshape(SIZES), AXES)
    return jax.shard_map(
        body,
        mesh=fine,
        in_specs=(P(DP, None, TILE), P(DP, None, TILE), P(None, TILE), P(None, TILE)),
        out_specs=P(TILE, DP),
        check_vma=False,
    )
```
